32 devices in a mesh: sec: 4 (over x, core), exp: 4 (over z), tp: 2 (over y).
Axes of the slice: x: 2, y: 2, z: 4, core: 2. Of those that a mesh axis runs over, the one named last changes fastest.
Arguments:
- tokens: bfloat16 [4, 1024, 1024], P('sec', 'exp'), may hold values from -6 to 6
- routes: int32 [4, 1024, 2], P('sec', 'exp'), may hold values from 0 to 3, all different within a row; in each aligned block of 256 rows (0 to 255, 256 to 511, ..., all dimensions but the last counted through in order) at most 192 rows name the same one
- gate_weights: float32 [4, 1024, 2], P('sec', 'exp'), may hold values from 0.1 to 0.9
- moe_gain: float32 [4, 1024], P('sec'), may hold values from 0.25 to 1.75
- attn_gain: float32 [4, 1024], P('sec'), may hold values from 0.25 to 1.75
- expert_in: bfloat16 [4, 4, 1024, 4096], P('sec', 'exp', None, 'tp'), may hold values from -0.1875 to 0.1875
- expert_out: bfloat16 [4, 4, 4096, 1024], P('sec', 'exp', 'tp'), may hold values from -0.09375 to 0.09375
- query_weight: bfloat16 [4, 1024, 1024], P('sec', None, 'tp'), may hold values from -0.1875 to 0.1875
- key_weight: bfloat16 [4, 1024, 1024], P('sec', None, 'tp'), may hold values from -0.1875 to 0.1875
- value_weight: bfloat16 [4, 1024, 1024], P('sec', None, 'tp'), may hold values from -0.1875 to 0.1875
- cotangent: bfloat16 [4, 1024, 1024], P('sec', 'exp', 'tp'), may hold values from -24 to 24
Outputs:
- section_out: bfloat16 [4, 1024, 1024], P('sec', 'exp', 'tp')
- enc_grad: bfloat16 [1024, 1024], P('exp', ('sec', 'tp'))
The draws below stay inside these ranges and needn't reach their ends.
Inputs may be any that keep to these rules, and one draw needn't show every extreme that they name: `routes`: each token names two different experts; among the 256 tokens of one aligned block of a section no expert is named more than 192 times.
All inputs are finite; a program needn't handle non-finite values.
Results may differ from the reference program's by a relative error of at most 0.025.
Values may be sent and summed in bfloat16 or wider, within the bound.
No kernel may reach another device: no remote copies, remote signals or barrier semaphores. Data moves between devices by JAX's collectives and lax.ppermute only.
A program may use at most 64 MiB of HBM per device.

```python
import math
import jax
import jax.numpy as jnp
import numpy as np
from jax import lax

D = 1024
HID = 4096
HEADS = 8
HD = 128
SEQ = 128
TOK_DEV = 256
TOKENS = 1024
EXPERTS = 4
CAP = 192
N_SEC = 4
N_EXP = 4


def level_of(rng, dims, cuts, smallest, high):
    level = 1.0
    for dim, shards_of in cuts:
        draws = jax.random.uniform(jax.random.fold_in(jax.random.fold_in(rng, 6), dim), (shards_of,), jnp.float32, smallest / len(cuts), high / len(cuts))
        level = level * jnp.repeat(jnp.exp(draws), dims[dim] // shards_of).reshape((-1,) + (1,) * (len(dims) - 1 - dim))
    return level


def assign_block(key, own, number, rows, amount, top, reach, slope):
    ranking = jax.random.permutation(key, amount)
    heavy_load, common = load_shares(amount, rows * top, reach, slope, True), load_shares(amount, rows * top, reach, slope, False)
    places = jnp.arange(amount)

    def named(sizes, offset_by):
        used = int((sizes > 0).sum())
        fixed = max(1, used // 4)
        shifted = fixed + (places - fixed + offset_by * (used - fixed)) % max(1, amount - fixed)
        return jnp.zeros((amount,), jnp.int32).at[ranking[jnp.where(places < fixed, places, shifted)]].set(jnp.asarray(sizes, jnp.int32))

    sizes = jnp.where(number % 4 == 0, named(heavy_load, number // 4), named(common, number - number // 4 - 1))
    mixed = jax.random.permutation(jax.random.fold_in(own, 3), amount)
    donor, taker = mixed[0:amount // 2 * 2:2], mixed[1:amount // 2 * 2:2]
    margin = jnp.minimum(sizes[donor] - 1, reach - sizes[taker]) // 2
    margin = jnp.where((donor == ranking[0]) | (taker == ranking[0]) | (sizes[taker] == 0), 0, jnp.maximum(margin, 0))
    shifted = jax.random.randint(jax.random.fold_in(own, 4), (amount // 2,), 0, 1 << 20) % (margin + 1)
    sizes = sizes.at[donor].add(-shifted).at[taker].add(shifted)
    items = jnp.searchsorted(jnp.cumsum(sizes), jnp.arange(rows * top), side="right").astype(jnp.int32)
    listing = items.reshape(top, rows).T
    listing = listing[jax.random.permutation(jax.random.fold_in(own, 1), rows)]
    offset_by = jax.random.randint(jax.random.fold_in(own, 2), (rows, 1), 0, top)
    return jnp.take_along_axis(listing, (jnp.arange(top)[None, :] + offset_by) % top, axis=1)


def load_shares(count, total, reach, slope, full):
    weights = [(1 << 20) // math.isqrt(rank ** slope) + 1 for rank in range(1, count + 1)]
    largest = reach if full else min(reach, max(-(-total // count), total * weights[0] // sum(weights)))
    least = 1 if total - largest >= count - 1 else 0
    given, rest = [largest] + [least] * (count - 1), total - largest - least * (count - 1)
    while rest > 0:
        candidates = [i for i in range(1, count) if given[i] < largest] or [i for i in range(1, count) if given[i] < reach]
        whole, left = sum([weights[i] for i in candidates]), rest
        for i in candidates:
            extra = min(reach - given[i], max(1, left * weights[i] // whole), rest)
            given[i] = given[i] + extra
            rest = rest - extra
    return np.array(given)


def scatter_about(own_key, dims, scale, reach, cuts=(), kind=jnp.bfloat16):
    loudness = level_of(own_key, dims, cuts, -0.22, 0.18) if cuts else 1.0
    entries = jax.random.normal(own_key, dims, jnp.float32) * scale * loudness
    return jnp.minimum(jnp.maximum(entries, -reach), reach).astype(kind)


def setup_inputs(seed: int = 0) -> dict:
    arg_keys = jax.random.split(jax.random.key(seed), 12)
    tokens = scatter_about(arg_keys[0], (N_SEC, TOKENS, D), 1.0, 6.0, ((0, 4), (1, 4)))
    routes_keys = jax.random.split(jax.random.fold_in(arg_keys[1], 1), N_SEC * TOKENS // TOK_DEV)
    routes_turns = jax.random.permutation(jax.random.fold_in(arg_keys[1], 3), N_SEC * TOKENS // TOK_DEV)
    routes = jax.vmap(lambda own, number: assign_block(jax.random.fold_in(arg_keys[1], 2), own, number, TOK_DEV, EXPERTS, 2, CAP, 2))(routes_keys, routes_turns).reshape((N_SEC, TOKENS, 2))
    gate_weights = jnp.clip(0.1 + 0.79999997 * jax.random.uniform(arg_keys[2], (N_SEC, TOKENS, 2), jnp.float32) ** level_of(arg_keys[2], (N_SEC, TOKENS, 2), ((0, 4), (1, 4)), -0.2, 0.2), 0.1, 0.9)
    moe_gain = jnp.clip(1.0 + 0.15 * jax.random.normal(arg_keys[3], (N_SEC, D), jnp.float32), 0.25, 1.75)
    attn_gain = jnp.clip(1.0 + 0.15 * jax.random.normal(arg_keys[4], (N_SEC, D), jnp.float32), 0.25, 1.75)
    expert_in = scatter_about(arg_keys[5], (N_SEC, EXPERTS, D, HID), D ** -0.5, 0.1875, ((0, 4), (1, 4), (3, 2)))
    expert_out = scatter_about(arg_keys[6], (N_SEC, EXPERTS, HID, D), HID ** -0.5, 0.09375, ((0, 4), (1, 4), (2, 2)))
    query_weight = scatter_about(arg_keys[7], (N_SEC, D, HEADS * HD), D ** -0.5, 0.1875, ((0, 4), (2, 2)))
    key_weight = scatter_about(arg_keys[8], (N_SEC, D, HEADS * HD), D ** -0.5, 0.1875, ((0, 4), (2, 2)))
    value_weight = scatter_about(arg_keys[9], (N_SEC, D, HEADS * HD), D ** -0.5, 0.1875, ((0, 4), (2, 2)))
    cotangent = scatter_about(arg_keys[10], (N_SEC, TOKENS, HEADS * HD), 4.0, 24.0, ((0, 4), (1, 4), (2, 2)))
    return dict(tokens=tokens, routes=routes, gate_weights=gate_weights, moe_gain=moe_gain, attn_gain=attn_gain, expert_in=expert_in, expert_out=expert_out, query_weight=query_weight, key_weight=key_weight, value_weight=value_weight, cotangent=cotangent)


EPS = 1e-05

def normalize(values, gain):
    wide = values.astype(jnp.float32)
    average = lax.optimization_barrier(jnp.mean(wide, axis=-1, keepdims=True))
    centred = wide - average
    spread = lax.optimization_barrier(jnp.mean(centred * centred, axis=-1, keepdims=True))
    return centred * lax.rsqrt(spread + EPS) * gain.astype(jnp.float32)

def slot_table(route_block, experts, capacity):
    flat_routes = route_block.reshape(-1).astype(jnp.int32)
    labels = jnp.arange(experts, dtype=jnp.int32)
    onehot = (flat_routes[:, None] == labels[None, :]).astype(jnp.int32)
    before = (jnp.cumsum(onehot, axis=0) - onehot).astype(jnp.int32)
    position = lax.optimization_barrier(jnp.sum(before * onehot, axis=1)).astype(jnp.int32)
    slot_index = (flat_routes * capacity + position).astype(jnp.int32)
    targets = jnp.arange(experts * capacity, dtype=jnp.int32)
    table = (targets[:, None] == slot_index[None, :]).astype(jnp.bfloat16)
    return table.reshape(experts * capacity, route_block.shape[0], 2)

def moe_section(tokens_here, route_here, gate_here, gain, first, second):
    normed = normalize(tokens_here, gain).astype(jnp.bfloat16)
    blocks = route_here.reshape(N_EXP, TOK_DEV, 2)
    tables = jax.vmap(lambda block: slot_table(block, EXPERTS, CAP))(blocks).astype(jnp.float32)
    token_blocks = normed.reshape(N_EXP, TOK_DEV, D).astype(jnp.float32)
    sent = jnp.einsum('bjtk,btd->bjd', tables, token_blocks).astype(jnp.bfloat16)
    arrived = sent.reshape(N_EXP, EXPERTS, CAP, D).transpose(1, 0, 2, 3).reshape(EXPERTS, N_EXP * CAP, D)

    def expert(operands):
        row_block, weight_first, weight_second = operands
        inner = jnp.maximum(jnp.dot(row_block, weight_first, preferred_element_type=jnp.float32), 0.0).astype(jnp.bfloat16)
        return jnp.dot(inner, weight_second, preferred_element_type=jnp.float32).astype(jnp.bfloat16)
    results = lax.map(expert, (arrived, first, second))
    returned = results.reshape(EXPERTS, N_EXP, CAP, D).transpose(1, 0, 2, 3).reshape(N_EXP, EXPERTS * CAP, D)
    picked = jnp.einsum('bjtk,bjd->btkd', tables, returned.astype(jnp.float32))
    weights = gate_here.reshape(N_EXP, TOK_DEV, 2).astype(jnp.float32)
    mixed = tokens_here.reshape(N_EXP, TOK_DEV, D).astype(jnp.float32)
    mixed = mixed + weights[:, :, 0:1] * picked[:, :, 0] + weights[:, :, 1:2] * picked[:, :, 1]
    return mixed.reshape(N_EXP * TOK_DEV, D).astype(jnp.bfloat16)

def attend(queries, key_rows, value_rows, upstream):
    shape = (TOKENS // SEQ, SEQ, HEADS, HD)
    scale = 1.0 / math.sqrt(HD)
    query_heads = queries.astype(jnp.float32).reshape(shape)
    key_heads = key_rows.astype(jnp.float32).reshape(shape)
    value_heads = value_rows.astype(jnp.float32).reshape(shape)
    upstream_heads = upstream.astype(jnp.float32).reshape(shape)
    scores = jnp.einsum('sqhd,skhd->shqk', query_heads, key_heads) * scale
    powers = jnp.exp(scores)
    probs = powers / lax.optimization_barrier(jnp.sum(powers, axis=-1, keepdims=True))
    probs_low = lax.optimization_barrier(probs.astype(jnp.bfloat16)).astype(jnp.float32)
    context = jnp.einsum('shqk,skhd->sqhd', probs_low, value_heads).astype(jnp.bfloat16)
    dprobs = jnp.einsum('sqhd,skhd->shqk', upstream_heads, value_heads)
    rowdot = lax.optimization_barrier(jnp.sum(dprobs * probs, axis=-1, keepdims=True))
    dscores = lax.optimization_barrier((probs * (dprobs - rowdot)).astype(jnp.bfloat16)).astype(jnp.float32)
    dvalues = jnp.einsum('shqk,sqhd->skhd', probs_low, upstream_heads).astype(jnp.bfloat16)
    dkeys = (jnp.einsum('shqk,sqhd->skhd', dscores, query_heads) * scale).astype(jnp.bfloat16)
    return (context.reshape(TOKENS, D), dkeys.reshape(TOKENS, D), dvalues.reshape(TOKENS, D))

def reference(tokens, routes, gate_weights, moe_gain, attn_gain, expert_in, expert_out, query_weight, key_weight, value_weight, cotangent):
    hidden = [moe_section(tokens[section], routes[section], gate_weights[section], moe_gain[section], expert_in[section], expert_out[section]) for section in range(N_SEC)]
    encoder = hidden[0]
    outputs = [encoder]
    gradient = jnp.zeros((TOKENS, D), jnp.float32)
    for section in range(1, N_SEC):
        query_in = normalize(hidden[section], attn_gain[section]).astype(jnp.bfloat16)
        queries = jnp.dot(query_in, query_weight[section], preferred_element_type=jnp.float32).astype(jnp.bfloat16)
        key_rows = jnp.dot(encoder, key_weight[section], preferred_element_type=jnp.float32).astype(jnp.bfloat16)
        value_rows = jnp.dot(encoder, value_weight[section], preferred_element_type=jnp.float32).astype(jnp.bfloat16)
        context, dkeys, dvalues = attend(queries, key_rows, value_rows, cotangent[section])
        outputs.append(context)
        gradient = gradient + jnp.dot(dkeys, key_weight[section].T, preferred_element_type=jnp.float32)
        gradient = gradient + jnp.dot(dvalues, value_weight[section].T, preferred_element_type=jnp.float32)
    return (jnp.stack(outputs), gradient.astype(jnp.bfloat16))
```

```python
import math

import jax
import jax.numpy as jnp
from jax import lax
from jax.sharding import PartitionSpec as P

HD = 128
SEQ = 128


EPS = 1e-05


def swap(block, axis, step):
    size = lax.axis_size(axis)
    return lax.ppermute(block, axis, [(i, i ^ step) for i in range(size)])


def send(block, axis, pairs):
    return lax.ppermute(block, axis, pairs)


def normalize(values, gain):
    wide = values.astype(jnp.float32)
    average = jnp.mean(wide, axis=-1, keepdims=True)
    centred = wide - average
    spread = jnp.mean(centred * centred, axis=-1, keepdims=True)
    return centred * lax.rsqrt(spread + EPS) * gain


def halves(mine, other, tp):
    low = jnp.where(tp == 0, mine, other)
    high = jnp.where(tp == 0, other, mine)
    return jnp.concatenate([low, high], axis=1)


def column_part(block, index, width):
    return lax.dynamic_slice_in_dim(block, index * width, width, 1)


def shards(
    tokens,
    routes,
    gate_weights,
    moe_gain,
    attn_gain,
    expert_in,
    expert_out,
    query_weight,
    key_weight,
    value_weight,
    cotangent,
):
    token_rows = tokens[0]
    route_rows = routes[0]
    gate_rows = gate_weights[0]
    token_count, model_width = token_rows.shape
    experts = lax.axis_size("exp")
    sections = lax.axis_size("sec")
    tp_size = lax.axis_size("tp")
    me = lax.axis_index("exp")
    tp = lax.axis_index("tp")
    sec = lax.axis_index("sec")
    half = model_width // tp_size
    capacity = 3 * token_count // experts
    weight_first = expert_in[0, 0]
    weight_second = expert_out[0, 0]

    normed = normalize(token_rows, moe_gain[0]).astype(jnp.bfloat16)
    normed_half = column_part(normed, tp, half)
    token_half = column_part(token_rows, tp, half)

    labels = jnp.arange(experts, dtype=jnp.int32) ^ me
    named = [(route_rows[:, k : k + 1] == labels[None, :]) for k in range(2)]
    either = named[0] | named[1]
    earlier = jnp.arange(token_count)
    earlier = (earlier[:, None] > earlier[None, :]).astype(jnp.bfloat16)
    before = jnp.dot(
        earlier, either.astype(jnp.bfloat16), preferred_element_type=jnp.float32
    ).astype(jnp.int32)
    place = jnp.where(either, before, -1)
    slots = jnp.arange(capacity, dtype=jnp.int32)
    tables = [
        (place[:, e][:, None] == slots[None, :]).astype(jnp.bfloat16) for e in range(experts)
    ]
    gates = jnp.where(named[0], gate_rows[:, 0:1], 0.0) + jnp.where(
        named[1], gate_rows[:, 1:2], 0.0
    )

    def pick(table, rows):
        return lax.dot_general(
            table, rows, (((0,), (0,)), ((), ())), preferred_element_type=jnp.float32
        ).astype(jnp.bfloat16)

    def expert(rows):
        inner = jnp.maximum(
            jnp.dot(rows, weight_first, preferred_element_type=jnp.float32), 0.0
        ).astype(jnp.bfloat16)
        return jnp.dot(inner, weight_second, preferred_element_type=jnp.float32)

    far = {}
    for k in range(experts - 1, 1, -1):
        far[k] = swap(pick(tables[k], normed_half), "exp", k)
    near = swap(pick(tables[1], normed), "exp", 1)
    rows_in = {0: pick(tables[0], normed), 1: near}
    for k in range(experts - 1, 1, -1):
        rows_in[k] = halves(far[k], swap(far[k], "tp", 1), tp)

    returned = {}
    for k in [0, 1] + list(range(experts - 1, 1, -1)):
        partial = expert(rows_in[k])
        away = column_part(partial, 1 - tp, half).astype(jnp.bfloat16)
        kept = column_part(partial, tp, half)
        total = (kept + swap(away, "tp", 1).astype(jnp.float32)).astype(jnp.bfloat16)
        returned[k] = total if k == 0 else swap(total, "exp", k)

    mixed = token_half.astype(jnp.float32)
    for k in range(experts):
        picked = jnp.dot(tables[k], returned[k], preferred_element_type=jnp.float32)
        mixed = mixed + gates[:, k : k + 1] * picked
    hidden_half = mixed.astype(jnp.bfloat16)

    spread = hidden_half
    step = sections // 2
    while step >= 1:
        moved = send(spread, "sec", [(i, i + step) for i in range(0, sections, 2 * step)])
        spread = jnp.where((sec % (2 * step)) == step, moved, spread)
        step //= 2
    hidden = halves(hidden_half, swap(hidden_half, "tp", 1), tp)
    encoder = halves(spread, swap(spread, "tp", 1), tp)

    query_w = query_weight[0]
    key_w = key_weight[0]
    value_w = value_weight[0]
    local_width = query_w.shape[1]
    local_heads = local_width // HD
    sequences = token_count // SEQ
    shape = (sequences, SEQ, local_heads, HD)
    scale = 1.0 / math.sqrt(HD)
    query_in = normalize(hidden, attn_gain[0]).astype(jnp.bfloat16)
    queries = (
        jnp.dot(query_in, query_w, preferred_element_type=jnp.float32)
        .astype(jnp.bfloat16)
        .reshape(shape)
    )
    key_rows = (
        jnp.dot(encoder, key_w, preferred_element_type=jnp.float32)
        .astype(jnp.bfloat16)
        .reshape(shape)
    )
    value_rows = (
        jnp.dot(encoder, value_w, preferred_element_type=jnp.float32)
        .astype(jnp.bfloat16)
        .reshape(shape)
    )
    scores = (
        jnp.einsum("sqhd,skhd->shqk", queries, key_rows, preferred_element_type=jnp.float32) * scale
    )
    powers = jnp.exp(scores)
    probs = powers / jnp.sum(powers, axis=-1, keepdims=True)
    probs_low = probs.astype(jnp.bfloat16)
    context = jnp.einsum(
        "shqk,skhd->sqhd", probs_low, value_rows, preferred_element_type=jnp.float32
    )
    context = context.astype(jnp.bfloat16).reshape(token_count, local_width)
    upstream = cotangent[0].reshape(shape)
    dprobs = jnp.einsum("sqhd,skhd->shqk", upstream, value_rows, preferred_element_type=jnp.float32)
    rowdot = jnp.sum(dprobs * probs, axis=-1, keepdims=True)
    dscores = (probs * (dprobs - rowdot)).astype(jnp.bfloat16)
    dvalues = jnp.einsum("shqk,sqhd->skhd", probs_low, upstream, preferred_element_type=jnp.float32)
    dvalues = dvalues.astype(jnp.bfloat16).reshape(token_count, local_width)
    dkeys = (
        jnp.einsum("shqk,sqhd->skhd", dscores, queries, preferred_element_type=jnp.float32) * scale
    )
    dkeys = dkeys.astype(jnp.bfloat16).reshape(token_count, local_width)
    contract = (((1,), (1,)), ((), ()))
    term = lax.dot_general(dkeys, key_w, contract, preferred_element_type=jnp.float32)
    term = term + lax.dot_general(dvalues, value_w, contract, preferred_element_type=jnp.float32)
    is_encoder = sec == 0
    term = jnp.where(is_encoder, jnp.zeros_like(term), term)

    own = model_width // (sections * tp_size)
    parts = term.reshape(token_count, sections // 2, 2, tp_size * own)
    side = sec % 2
    mine = lax.dynamic_index_in_dim(parts, side, 2, keepdims=False)
    other = lax.dynamic_index_in_dim(parts, 1 - side, 2, keepdims=False)
    mine = mine + swap(other.astype(jnp.bfloat16), "sec", 1).astype(jnp.float32)
    mine = mine.reshape(token_count, model_width // 2)
    here = (sec // 2) * tp_size + tp
    total = column_part(mine, here, own)
    count = sections // 2 * tp_size
    both = sections * tp_size
    for k in range(1, count):
        pairs = []
        for i in range(both):
            place_of, tp_of = i // tp_size, i % tp_size
            target = ((place_of // 2) * tp_size + tp_of) ^ k
            pairs.append((i, (target // tp_size * 2 + place_of % 2) * tp_size + target % tp_size))
        block = column_part(mine, here ^ k, own).astype(jnp.bfloat16)
        total = total + lax.ppermute(block, ("sec", "tp"), pairs).astype(jnp.float32)
    enc_grad = total.astype(jnp.bfloat16)
    section_out = jnp.where(is_encoder, hidden_half, context)
    return (section_out[None], enc_grad)


def solution(mesh):
    placed = (
        P("sec", "exp", None),
        P("sec", "exp", None),
        P("sec", "exp", None),
        P("sec", None),
        P("sec", None),
        P("sec", "exp", None, "tp"),
        P("sec", "exp", "tp", None),
        P("sec", None, "tp"),
        P("sec", None, "tp"),
        P("sec", None, "tp"),
        P("sec", "exp", "tp"),
    )
    return jax.shard_map(
        shards,
        mesh=mesh,
        in_specs=placed,
        out_specs=(P("sec", "exp", "tp"), P("exp", ("sec", "tp"))),
        check_vma=False,
    )
```

```python
import functools
import math

import jax
import jax.numpy as jnp
from jax import lax
from jax.experimental import pallas as pl
from jax.experimental.pallas import tpu as pltpu
from jax.sharding import PartitionSpec as P

HD = 128
SEQ = 128
EPS = 1e-05

LOW = jnp.bfloat16
WIDE = jnp.float32
VMEM = pl.BlockSpec(memory_space=pltpu.VMEM)
NT = (((1,), (1,)), ((), ()))
TN = (((0,), (0,)), ((), ()))


def matmul(a, b, dims=(((1,), (0,)), ((), ()))):
    return lax.dot_general(a, b, dims, preferred_element_type=WIDE)


def call(body, out_shape, inputs, scratch=(), flops=0, limit=40):
    def size(x):
        return math.prod(x.shape) * jnp.dtype(x.dtype).itemsize

    moved = sum(size(x) for x in inputs) + sum(size(x) for x in out_shape)
    return pl.pallas_call(
        body,
        out_shape=out_shape,
        in_specs=[VMEM] * len(inputs),
        out_specs=[VMEM] * len(out_shape),
        scratch_shapes=list(scratch),
        compiler_params=pltpu.CompilerParams(vmem_limit_bytes=limit * 2**20),
        cost_estimate=pl.CostEstimate(flops=flops, bytes_accessed=moved, transcendentals=0),
    )(*inputs)


def shape_of(dims, kind=LOW):
    return jax.ShapeDtypeStruct(dims, kind)


def part(index, width):
    return pl.ds(pl.multiple_of(index * width, width), width)


def places(routes, me, rows):
    token_count = routes.shape[1]
    labels = lax.broadcasted_iota(jnp.int32, (rows, 1), 0) ^ me
    first = routes[0:1, :] == labels
    second = routes[1:2, :] == labels
    either = first | second
    source = lax.broadcasted_iota(jnp.int32, (token_count, token_count), 0)
    target = lax.broadcasted_iota(jnp.int32, (token_count, token_count), 1)
    earlier = jnp.where(source < target, 1.0, 0.0).astype(LOW)
    before = matmul(jnp.where(either, 1.0, 0.0).astype(LOW), earlier)
    return jnp.where(either, before, -1.0), first, second


def prepare(experts, tokens, routes, gain, *outs):
    far, near, own = outs[:-3], outs[-3], outs[-2]
    normed_ref = outs[-1]
    me = lax.axis_index("exp")
    tp = lax.axis_index("tp")
    token_count, width = tokens.shape
    capacity = own.shape[0]
    half = width // 2
    wide = tokens[...].astype(WIDE)
    average = jnp.mean(wide, axis=-1, keepdims=True)
    centred = wide - average
    spread = jnp.mean(centred * centred, axis=-1, keepdims=True)
    normed_ref[...] = (centred * lax.rsqrt(spread + EPS) * gain[...]).astype(LOW)
    place, _, _ = places(routes[...], me, max(16, experts))
    slots = lax.broadcasted_iota(jnp.int32, (capacity, token_count), 0).astype(WIDE)

    def table(k):
        return jnp.where(place[k : k + 1, :] == slots, 1.0, 0.0).astype(LOW)

    normed_half = normed_ref[:, part(tp, half)]
    for k in range(experts - 1, 1, -1):
        far[k - 2][...] = matmul(table(k), normed_half).astype(LOW)
    normed = normed_ref[...]
    near[...] = matmul(table(1), normed).astype(LOW)
    own[...] = matmul(table(0), normed).astype(LOW)


def mixing(experts, routes, gates, high, low):
    me = lax.axis_index("exp")
    token_count = routes.shape[1]
    capacity = high.shape[2]
    place, first, second = places(routes[...], me, max(16, experts))
    gate = jnp.where(first, gates[0:1, :], 0.0) + jnp.where(second, gates[1:2, :], 0.0)
    place = place.T
    gate = gate.T
    slots = lax.broadcasted_iota(jnp.int32, (token_count, capacity), 1).astype(WIDE)
    for k in range(experts):
        weight = jnp.where(place[:, k : k + 1] == slots, gate[:, k : k + 1], 0.0)
        upper = weight.astype(LOW)
        high[k] = upper
        low[k] = (weight - upper.astype(WIDE)).astype(LOW)


def expert(split, *refs):
    rows, refs = refs[: 1 + split], refs[1 + split :]
    first, second, away, kept, inner = refs
    tp = lax.axis_index("tp")
    width, hidden = first.shape
    half = width // 2
    chunk = min(512, hidden)
    for c in range(hidden // chunk):
        columns = slice(c * chunk, (c + 1) * chunk)
        if split:
            value = matmul(rows[0][...], first[part(tp, half), columns])
            value = value + matmul(rows[1][...], first[part(1 - tp, half), columns])
        else:
            value = matmul(rows[0][...], first[:, columns])
        inner[:, columns] = jnp.maximum(value, 0.0).astype(LOW)
    away[...] = matmul(inner[...], second[:, part(1 - tp, half)]).astype(LOW)
    kept[...] = matmul(inner[...], second[:, part(tp, half)])


def combine(experts, tokens, high, low, *refs):
    returned, out = refs[:-1], refs[-1]
    tp = lax.axis_index("tp")
    half = out.shape[1]
    mixed = tokens[:, part(tp, half)].astype(WIDE)
    for k in range(experts):
        rows = returned[k][...]
        mixed = mixed + (matmul(high[k], rows) + matmul(low[k], rows))
    out[...] = mixed.astype(LOW)


def project(mine, other, gain, weight, out):
    tp = lax.axis_index("tp")
    half = mine.shape[1]
    own = mine[...].astype(WIDE)
    rest = other[...].astype(WIDE)
    average = (
        jnp.sum(own, axis=-1, keepdims=True) + jnp.sum(rest, axis=-1, keepdims=True)
    ) / (2 * half)
    own = own - average
    rest = rest - average
    spread = (
        jnp.sum(own * own, axis=-1, keepdims=True) + jnp.sum(rest * rest, axis=-1, keepdims=True)
    ) / (2 * half)
    factor = lax.rsqrt(spread + EPS)
    own = (own * factor * gain[:, part(tp, half)]).astype(LOW)
    rest = (rest * factor * gain[:, part(1 - tp, half)]).astype(LOW)
    value = matmul(own, weight[part(tp, half), :]) + matmul(rest, weight[part(1 - tp, half), :])
    out[...] = value.astype(LOW)


def attend(
    mine, other, queries, upstream, key_w, value_w, hidden, context, away, kept, keys, values, dkeys, dvalues
):
    tp = lax.axis_index("tp")
    sec = lax.axis_index("sec")
    token_count, half = mine.shape
    width = 2 * half
    scale = 1.0 / math.sqrt(HD)

    @pl.when(sec != 0)
    def _():
        for weight, target in ((key_w, keys), (value_w, values)):
            value = matmul(mine[...], weight[part(tp, half), :])
            value = value + matmul(other[...], weight[part(1 - tp, half), :])
            target[...] = value.astype(LOW)
        for s in range(token_count // SEQ):
            for h in range(queries.shape[1] // HD):
                rows, columns = slice(s * SEQ, (s + 1) * SEQ), slice(h * HD, (h + 1) * HD)
                query, key = queries[rows, columns], keys[rows, columns]
                value, up = values[rows, columns], upstream[rows, columns]
                powers = jnp.exp(matmul(key, query, NT) * scale)
                probs = powers * (1.0 / jnp.sum(powers, axis=0, keepdims=True))
                low = probs.astype(LOW)
                dprobs = matmul(value, up, NT)
                rowdot = jnp.sum(dprobs * probs, axis=0, keepdims=True)
                dscores = (probs * (dprobs - rowdot)).astype(LOW)
                dvalues[rows, columns] = matmul(low, up).astype(LOW)
                dkeys[rows, columns] = (matmul(dscores, query) * scale).astype(LOW)
                context[rows, columns] = matmul(low, value, TN).astype(LOW)
        side = sec % 2
        pairs = lax.axis_size("sec") // 2
        block = width // (2 * pairs)
        for target, parity in ((away, 1 - side), (kept, side)):
            for i in range(pairs):
                rows = part(2 * i + parity, block)
                value = matmul(dkeys[...], key_w[rows, :], NT)
                value = value + matmul(dvalues[...], value_w[rows, :], NT)
                target[:, i * block : (i + 1) * block] = value.astype(target.dtype)

    @pl.when(sec == 0)
    def _():
        context[...] = hidden[...]
        away[...] = jnp.zeros_like(away)
        kept[...] = jnp.zeros_like(kept)


def gather_term(kept, arrived, own, *sent):
    tp = lax.axis_index("tp")
    here = lax.axis_index("sec") // 2 * lax.axis_size("tp") + tp
    width = own.shape[1]
    for k in range(len(sent) + 1):
        columns = part(here ^ k, width)
        value = kept[:, columns] + arrived[:, columns].astype(WIDE)
        if k == 0:
            own[...] = value
        else:
            sent[k - 1][...] = value.astype(LOW)


def swap(block, axis, step):
    size = lax.axis_size(axis)
    return lax.ppermute(block, axis, [(i, i ^ step) for i in range(size)])


def shards(
    tokens,
    routes,
    gate_weights,
    moe_gain,
    attn_gain,
    expert_in,
    expert_out,
    query_weight,
    key_weight,
    value_weight,
    cotangent,
):
    token_rows = tokens[0]
    route_rows = routes[0].T
    gate_rows = gate_weights[0].T
    token_count, model_width = token_rows.shape
    experts = lax.axis_size("exp")
    sections = lax.axis_size("sec")
    tp_size = lax.axis_size("tp")
    sec = lax.axis_index("sec")
    half = model_width // tp_size
    capacity = 3 * token_count // experts
    weight_first = expert_in[0, 0]
    weight_second = expert_out[0, 0]
    units = weight_first.shape[1]

    far_count = experts - 2
    prepared = call(
        functools.partial(prepare, experts),
        [shape_of((capacity, half))] * far_count + [shape_of((capacity, model_width))] * 2,
        [token_rows, route_rows, moe_gain],
        [pltpu.VMEM((token_count, model_width), LOW)],
        flops=2 * 3 * token_count * token_count * model_width,
    )
    far_rows, near_rows, own_rows = prepared[:far_count], prepared[far_count], prepared[-1]
    high, low = call(
        functools.partial(mixing, experts),
        [shape_of((experts, token_count, capacity))] * 2,
        [route_rows, gate_rows],
    )

    def through(rows):
        count = rows[0].shape[0]
        away, kept = call(
            functools.partial(expert, len(rows) - 1),
            [shape_of((count, half)), shape_of((count, half), WIDE)],
            [*rows, weight_first, weight_second],
            [pltpu.VMEM((count, units), LOW)],
            flops=4 * count * model_width * units,
        )
        return (kept + swap(away, "tp", 1).astype(WIDE)).astype(LOW)

    far = {k: swap(far_rows[k - 2], "exp", k) for k in range(experts - 1, 1, -1)}
    near = swap(near_rows, "exp", 1)
    returned = {0: through([own_rows]), 1: swap(through([near]), "exp", 1)}
    middle = max(2, experts // 2 + 1)
    for group in (range(experts - 1, middle - 1, -1), range(middle - 1, 1, -1)):
        group = list(group)
        if not group:
            continue
        if len(group) == 1:
            mine = far[group[0]]
        else:
            mine = jnp.concatenate([far[k] for k in group], axis=0)
        total = through([mine, swap(mine, "tp", 1)])
        for i, k in enumerate(group):
            block = total if len(group) == 1 else total[i * capacity : (i + 1) * capacity]
            returned[k] = swap(block, "exp", k)

    hidden_half = call(
        functools.partial(combine, experts),
        [shape_of((token_count, half))],
        [token_rows, high, low, *(returned[k] for k in range(experts))],
        flops=4 * 3 * token_count * token_count * half,
    )[0]

    hidden_other = swap(hidden_half, "tp", 1)
    mine = hidden_half
    other = hidden_other
    step = sections // 2
    while step >= 2:
        pairs = [(i, i + step) for i in range(0, sections, 2 * step)]
        mine = jnp.where(sec % (2 * step) == step, lax.ppermute(mine, "sec", pairs), mine)
        step //= 2
    if sections > 2:
        pairs = []
        for i in range(2, sections, 2):
            pairs += [(i * tp_size + t, i * tp_size + (t ^ 1)) for t in range(tp_size)]
        other = jnp.where(sec >= 2, lax.ppermute(mine, ("sec", "tp"), pairs), other)
    beside = [(i, i + 1) for i in range(0, sections, 2)]
    mine = jnp.where(sec % 2 == 1, lax.ppermute(mine, "sec", beside), mine)
    other = jnp.where(sec % 2 == 1, lax.ppermute(other, "sec", beside), other)

    local_width = query_weight.shape[2]
    queries = call(
        project,
        [shape_of((token_count, local_width))],
        [hidden_half, hidden_other, attn_gain, query_weight[0]],
        flops=2 * token_count * model_width * local_width,
    )[0]
    context, away, kept = call(
        attend,
        [
            shape_of((token_count, local_width)),
            shape_of((token_count, model_width // 2)),
            shape_of((token_count, model_width // 2), WIDE),
        ],
        [mine, other, queries, cotangent[0], key_weight[0], value_weight[0], hidden_half],
        [pltpu.VMEM((token_count, local_width), LOW)] * 4,
        flops=10 * token_count * model_width * local_width,
    )

    own = model_width // (sections * tp_size)
    count = sections // 2 * tp_size
    both = sections * tp_size
    blocks = call(
        gather_term,
        [shape_of((token_count, own), WIDE)] + [shape_of((token_count, own))] * (count - 1),
        [kept, swap(away, "sec", 1)],
    )
    total = blocks[0]
    for k in range(1, count):
        pairs = []
        for i in range(both):
            section, t = i // tp_size, i % tp_size
            target = (section // 2 * tp_size + t) ^ k
            pairs.append((i, (target // tp_size * 2 + section % 2) * tp_size + target % tp_size))
        total = total + lax.ppermute(blocks[k], ("sec", "tp"), pairs).astype(WIDE)
    return (context[None], total.astype(LOW))


def solution(mesh):
    placed = (
        P("sec", "exp", None),
        P("sec", "exp", None),
        P("sec", "exp", None),
        P("sec", None),
        P("sec", None),
        P("sec", "exp", None, "tp"),
        P("sec", "exp", "tp", None),
        P("sec", None, "tp"),
        P("sec", None, "tp"),
        P("sec", None, "tp"),
        P("sec", "exp", "tp"),
    )
    return jax.shard_map(
        shards,
        mesh=mesh,
        in_specs=placed,
        out_specs=(P("sec", "exp", "tp"), P("exp", ("sec", "tp"))),
        check_vma=False,
    )
```

```python
import functools
import math

import jax
import jax.numpy as jnp
from jax import lax
from jax.experimental import pallas as pl
from jax.experimental.pallas import tpu as pltpu
from jax.sharding import PartitionSpec as P

HD = 128
SEQ = 128
EPS = 1e-05

LOW = jnp.bfloat16
WIDE = jnp.float32
VMEM = pl.BlockSpec(memory_space=pltpu.VMEM)
HBM = pl.BlockSpec(memory_space=pltpu.HBM)
ANY = pl.BlockSpec(memory_space=pl.ANY)
NT = (((1,), (1,)), ((), ()))
TN = (((0,), (0,)), ((), ()))


def matmul(a, b, dims=(((1,), (0,)), ((), ()))):
    return lax.dot_general(a, b, dims, preferred_element_type=WIDE)


def call(body, out_shape, inputs, scratch=(), flops=0, limit=40, remote=(), after=(), held=()):
    def size(x):
        return math.prod(x.shape) * jnp.dtype(x.dtype).itemsize

    count, results = len(inputs), len(out_shape)
    extra = len(after) + len(held)

    def run(*refs):
        outs = refs[count + extra : count + extra + results]
        return body(*refs[:count], *outs, *refs[count + extra + results + len(held) :])

    moved = sum(size(x) for x in inputs) + sum(size(x) for x in out_shape)
    return pl.pallas_call(
        run,
        out_shape=[*out_shape, *(shape_of(x.shape, x.dtype) for x in held)],
        in_specs=[HBM if i in remote else VMEM for i in range(count)] + [ANY] * extra,
        out_specs=[VMEM] * results + [ANY] * len(held),
        scratch_shapes=list(scratch),
        input_output_aliases={count + len(after) + i: results + i for i in range(len(held))},
        compiler_params=pltpu.CompilerParams(vmem_limit_bytes=limit * 2**20),
        cost_estimate=pl.CostEstimate(flops=flops, bytes_accessed=moved, transcendentals=0),
    )(*inputs, *after, *held)


def shape_of(dims, kind=LOW):
    return jax.ShapeDtypeStruct(dims, kind)


def part(index, width):
    return pl.ds(pl.multiple_of(index * width, width), width)


def places(routes, me, rows):
    token_count = routes.shape[1]
    labels = lax.broadcasted_iota(jnp.int32, (rows, 1), 0) ^ me
    first = routes[0:1, :] == labels
    second = routes[1:2, :] == labels
    either = first | second
    source = lax.broadcasted_iota(jnp.int32, (token_count, token_count), 0)
    target = lax.broadcasted_iota(jnp.int32, (token_count, token_count), 1)
    earlier = jnp.where(source < target, 1.0, 0.0).astype(LOW)
    before = matmul(jnp.where(either, 1.0, 0.0).astype(LOW), earlier)
    return jnp.where(either, before, -1.0), first, second


def table(place, k, capacity):
    slots = lax.broadcasted_iota(jnp.int32, (capacity, place.shape[1]), 0).astype(WIDE)
    return jnp.where(place[k : k + 1, :] == slots, 1.0, 0.0).astype(LOW)


def prepare(experts, tokens, routes, gain, *outs):
    far, near, own, normed_ref = outs[:-3], outs[-3], outs[-2], outs[-1]
    me = lax.axis_index("exp")
    tp = lax.axis_index("tp")
    capacity, width = own.shape
    half = width // 2
    wide = tokens[...].astype(WIDE)
    average = jnp.mean(wide, axis=-1, keepdims=True)
    centred = wide - average
    spread = jnp.mean(centred * centred, axis=-1, keepdims=True)
    normed_ref[...] = (centred * lax.rsqrt(spread + EPS) * gain[...]).astype(LOW)
    place, _, _ = places(routes[...], me, max(16, experts))
    normed_half = normed_ref[:, part(tp, half)]
    for k in range(experts - 1, 1, -1):
        far[k - 2][...] = matmul(table(place, k, capacity), normed_half).astype(LOW)
    normed = normed_ref[...]
    near[...] = matmul(table(place, 1, capacity), normed).astype(LOW)
    own[...] = matmul(table(place, 0, capacity), normed).astype(LOW)


def mixing(experts, routes, gates, high, low):
    me = lax.axis_index("exp")
    token_count = routes.shape[1]
    capacity = high.shape[2]
    place, first, second = places(routes[...], me, max(16, experts))
    gate = jnp.where(first, gates[0:1, :], 0.0) + jnp.where(second, gates[1:2, :], 0.0)
    place = place.T
    gate = gate.T
    slots = lax.broadcasted_iota(jnp.int32, (token_count, capacity), 1).astype(WIDE)
    for k in range(experts):
        weight = jnp.where(place[:, k : k + 1] == slots, gate[:, k : k + 1], 0.0)
        upper = weight.astype(LOW)
        high[k] = upper
        low[k] = (weight - upper.astype(WIDE)).astype(LOW)


def expert(split, *refs):
    rows, refs = refs[: 1 + split], refs[1 + split :]
    first, second, away, kept, inner = refs
    tp = lax.axis_index("tp")
    width, hidden = first.shape
    half = width // 2
    chunk = min(512, hidden)
    for c in range(hidden // chunk):
        columns = slice(c * chunk, (c + 1) * chunk)
        if split:
            value = matmul(rows[0][...], first[part(tp, half), columns])
            value = value + matmul(rows[1][...], first[part(1 - tp, half), columns])
        else:
            value = matmul(rows[0][...], first[:, columns])
        inner[:, columns] = jnp.maximum(value, 0.0).astype(LOW)
    away[...] = matmul(inner[...], second[:, part(1 - tp, half)]).astype(LOW)
    kept[...] = matmul(inner[...], second[:, part(tp, half)])


def expert_first(rows, first, second, away, kept, first_here, second_here, inner, arrived):
    tp = lax.axis_index("tp")
    width, hidden = first.shape
    half = width // 2
    chunk = min(512, hidden)
    columns = [slice(c * chunk, (c + 1) * chunk) for c in range(hidden // chunk)]
    loads = [
        pltpu.make_async_copy(first.at[:, c], first_here.at[:, c], arrived.at[i])
        for i, c in enumerate(columns)
    ]
    loads.append(pltpu.make_async_copy(second, second_here, arrived.at[len(columns)]))
    for load in loads:
        load.start()
    for c, load in zip(columns, loads):
        load.wait()
        inner[:, c] = jnp.maximum(matmul(rows[...], first_here[:, c]), 0.0).astype(LOW)
    loads[-1].wait()
    away[...] = matmul(inner[...], second_here[:, part(1 - tp, half)]).astype(LOW)
    kept[...] = matmul(inner[...], second_here[:, part(tp, half)])


def idle():
    pass


def combine(experts, tokens, high, low, *refs):
    returned, out = refs[:-1], refs[-1]
    tp = lax.axis_index("tp")
    half = out.shape[1]
    mixed = tokens[:, part(tp, half)].astype(WIDE)
    for k in range(experts):
        rows = returned[k][...]
        mixed = mixed + (matmul(high[k], rows) + matmul(low[k], rows))
    out[...] = mixed.astype(LOW)


def project(mine, other, gain, weight, out):
    tp = lax.axis_index("tp")
    half = mine.shape[1]
    own = mine[...].astype(WIDE)
    rest = other[...].astype(WIDE)
    average = (
        jnp.sum(own, axis=-1, keepdims=True) + jnp.sum(rest, axis=-1, keepdims=True)
    ) / (2 * half)
    own = own - average
    rest = rest - average
    spread = (
        jnp.sum(own * own, axis=-1, keepdims=True) + jnp.sum(rest * rest, axis=-1, keepdims=True)
    ) / (2 * half)
    factor = lax.rsqrt(spread + EPS)
    own = (own * factor * gain[:, part(tp, half)]).astype(LOW)
    rest = (rest * factor * gain[:, part(1 - tp, half)]).astype(LOW)
    value = matmul(own, weight[part(tp, half), :]) + matmul(rest, weight[part(1 - tp, half), :])
    out[...] = value.astype(LOW)


def attend(
    mine, other, queries, upstream, key_w, value_w, hidden, context, away, kept, keys, values, dkeys, dvalues
):
    tp = lax.axis_index("tp")
    sec = lax.axis_index("sec")
    token_count, half = mine.shape
    width = 2 * half
    scale = 1.0 / math.sqrt(HD)

    @pl.when(sec != 0)
    def _():
        for weight, target in ((key_w, keys), (value_w, values)):
            value = matmul(mine[...], weight[part(tp, half), :])
            value = value + matmul(other[...], weight[part(1 - tp, half), :])
            target[...] = value.astype(LOW)
        for s in range(token_count // SEQ):
            for h in range(queries.shape[1] // HD):
                rows, columns = slice(s * SEQ, (s + 1) * SEQ), slice(h * HD, (h + 1) * HD)
                query, key = queries[rows, columns], keys[rows, columns]
                value, up = values[rows, columns], upstream[rows, columns]
                powers = jnp.exp(matmul(key, query, NT) * scale)
                probs = powers * (1.0 / jnp.sum(powers, axis=0, keepdims=True))
                low = probs.astype(LOW)
                dprobs = matmul(value, up, NT)
                rowdot = jnp.sum(dprobs * probs, axis=0, keepdims=True)
                dscores = (probs * (dprobs - rowdot)).astype(LOW)
                dvalues[rows, columns] = matmul(low, up).astype(LOW)
                dkeys[rows, columns] = (matmul(dscores, query) * scale).astype(LOW)
                context[rows, columns] = matmul(low, value, TN).astype(LOW)
        side = sec % 2
        pairs = lax.axis_size("sec") // 2
        block = width // (2 * pairs)
        for target, parity in ((away, 1 - side), (kept, side)):
            for i in range(pairs):
                rows = part(2 * i + parity, block)
                value = matmul(dkeys[...], key_w[rows, :], NT)
                value = value + matmul(dvalues[...], value_w[rows, :], NT)
                target[:, i * block : (i + 1) * block] = value.astype(target.dtype)

    @pl.when(sec == 0)
    def _():
        context[...] = hidden[...]
        away[...] = jnp.zeros_like(away)
        kept[...] = jnp.zeros_like(kept)


def gather_term(kept, arrived, own, *sent):
    tp = lax.axis_index("tp")
    here = lax.axis_index("sec") // 2 * lax.axis_size("tp") + tp
    width = own.shape[1]
    for k in range(len(sent) + 1):
        columns = part(here ^ k, width)
        value = kept[:, columns] + arrived[:, columns].astype(WIDE)
        if k == 0:
            own[...] = value
        else:
            sent[k - 1][...] = value.astype(LOW)


def swap(block, axis, step):
    size = lax.axis_size(axis)
    return lax.ppermute(block, axis, [(i, i ^ step) for i in range(size)])


def shards(
    tokens,
    routes,
    gate_weights,
    moe_gain,
    attn_gain,
    expert_in,
    expert_out,
    query_weight,
    key_weight,
    value_weight,
    cotangent,
):
    token_rows = tokens[0]
    route_rows = routes[0].T
    gate_rows = gate_weights[0].T
    token_count, model_width = token_rows.shape
    experts = lax.axis_size("exp")
    sections = lax.axis_size("sec")
    tp_size = lax.axis_size("tp")
    sec = lax.axis_index("sec")
    half = model_width // tp_size
    capacity = 3 * token_count // experts
    weight_first = expert_in[0, 0]
    weight_second = expert_out[0, 0]
    units = weight_first.shape[1]

    middle = max(2, experts // 2 + 1)
    groups = [list(range(experts - 1, middle - 1, -1)), list(range(middle - 1, 1, -1))]
    row_half, row_whole = shape_of((capacity, half)), shape_of((capacity, model_width))
    *far_rows, near_rows, own_rows = call(
        functools.partial(prepare, experts),
        [row_half] * (experts - 2) + [row_whole] * 2,
        [token_rows, route_rows, moe_gain],
        [pltpu.VMEM((token_count, model_width), LOW)],
        flops=2 * 3 * token_count * token_count * model_width,
    )
    far = {k: swap(far_rows[k - 2], "exp", k) for k in groups[0]}
    loads = max(1, units // 512) + 1
    own_away, own_kept, weight_first, weight_second = call(
        expert_first,
        [
            row_half,
            shape_of((capacity, half), WIDE),
            shape_of(weight_first.shape),
            shape_of(weight_second.shape),
        ],
        [own_rows, weight_first, weight_second],
        [pltpu.VMEM((capacity, units), LOW), pltpu.SemaphoreType.DMA((loads,))],
        flops=4 * capacity * model_width * units,
        remote=(1, 2),
        limit=44,

    )
    far |= {k: swap(far_rows[k - 2], "exp", k) for k in groups[1]}
    near = swap(near_rows, "exp", 1)
    high, low = call(
        functools.partial(mixing, experts),
        [shape_of((experts, token_count, capacity))] * 2,
        [route_rows, gate_rows],
        after=[own_away],
    )

    def total(away, kept):
        return (kept + swap(away, "tp", 1).astype(WIDE)).astype(LOW)

    def through(rows, after):
        count = rows[0].shape[0]
        away, kept = call(
            functools.partial(expert, len(rows) - 1),
            [shape_of((count, half)), shape_of((count, half), WIDE)],
            [*rows, weight_first, weight_second],
            [pltpu.VMEM((count, units), LOW)],
            flops=4 * count * model_width * units,
            after=after,
        )
        return total(away, kept)

    returned = {0: total(own_away, own_kept), 1: swap(through([near], []), "exp", 1)}
    for group in groups[::-1]:
        if not group:
            continue
        if len(group) == 1:
            mine = far[group[0]]
        else:
            mine = jnp.concatenate([far[k] for k in group], axis=0)
        if group is groups[1]:
            mine = call(idle, [], [], after=[own_away], held=[mine])[0]
        mixed = through([mine, swap(mine, "tp", 1)], [high])
        for i, k in enumerate(group):
            block = mixed if len(group) == 1 else mixed[i * capacity : (i + 1) * capacity]
            returned[k] = swap(block, "exp", k)

    hidden_half = call(
        functools.partial(combine, experts),
        [shape_of((token_count, half))],
        [token_rows, high, low, *(returned[k] for k in range(experts))],
        flops=4 * 3 * token_count * token_count * half,
    )[0]

    first = hidden_half
    for i in range(1, sections // 2):
        moved = lax.ppermute(hidden_half, "sec", [(0, 2 * i)])
        first = jnp.where(sec == 2 * i, moved, first)
    for i in range(sections // 2 - 1, -1, -1):
        pairs = [(t, (2 * i + 1) * tp_size + (t ^ 1)) for t in range(tp_size)]
        moved = lax.ppermute(hidden_half, ("sec", "tp"), pairs)
        first = jnp.where(sec == 2 * i + 1, moved, first)
    hidden_other = swap(hidden_half, "tp", 1)
    beside = swap(first, "sec", 1)
    mine = jnp.where(sec % 2 == 0, first, beside)
    other = jnp.where(sec % 2 == 0, beside, first)

    local_width = query_weight.shape[2]
    queries = call(
        project,
        [shape_of((token_count, local_width))],
        [hidden_half, hidden_other, attn_gain, query_weight[0]],
        flops=2 * token_count * model_width * local_width,
    )[0]
    context, away, kept = call(
        attend,
        [
            shape_of((token_count, local_width)),
            shape_of((token_count, model_width // 2)),
            shape_of((token_count, model_width // 2), WIDE),
        ],
        [mine, other, queries, cotangent[0], key_weight[0], value_weight[0], hidden_half],
        [pltpu.VMEM((token_count, local_width), LOW)] * 4,
        flops=10 * token_count * model_width * local_width,
    )

    own = model_width // (sections * tp_size)
    count = sections // 2 * tp_size
    both = sections * tp_size
    blocks = call(
        gather_term,
        [shape_of((token_count, own), WIDE)] + [shape_of((token_count, own))] * (count - 1),
        [kept, swap(away, "sec", 1)],
    )
    total = blocks[0]
    for k in range(1, count):
        pairs = []
        for i in range(both):
            section, t = i // tp_size, i % tp_size
            target = (section // 2 * tp_size + t) ^ k
            pairs.append((i, (target // tp_size * 2 + section % 2) * tp_size + target % tp_size))
        total = total + lax.ppermute(blocks[k], ("sec", "tp"), pairs).astype(WIDE)
    return (context[None], total.astype(LOW))


def solution(mesh):
    placed = (
        P("sec", "exp", None),
        P("sec", "exp", None),
        P("sec", "exp", None),
        P("sec", None),
        P("sec", None),
        P("sec", "exp", None, "tp"),
        P("sec", "exp", "tp", None),
        P("sec", None, "tp"),
        P("sec", None, "tp"),
        P("sec", None, "tp"),
        P("sec", "exp", "tp"),
    )
    return jax.shard_map(
        shards,
        mesh=mesh,
        in_specs=placed,
        out_specs=(P("sec", "exp", "tp"), P("exp", ("sec", "tp"))),
        check_vma=False,
    )
```

```python
import functools
import math

import jax
import jax.numpy as jnp
from jax import lax
from jax.experimental import pallas as pl
from jax.experimental.pallas import tpu as pltpu
from jax.sharding import PartitionSpec as P

HD = 128
SEQ = 128
EPS = 1e-05

LOW = jnp.bfloat16
WIDE = jnp.float32
VMEM = pl.BlockSpec(memory_space=pltpu.VMEM)
HBM = pl.BlockSpec(memory_space=pltpu.HBM)
ANY = pl.BlockSpec(memory_space=pl.ANY)
NT = (((1,), (1,)), ((), ()))
TN = (((0,), (0,)), ((), ()))


def matmul(a, b, dims=(((1,), (0,)), ((), ()))):
    return lax.dot_general(a, b, dims, preferred_element_type=WIDE)


def call(body, out_shape, inputs, scratch=(), flops=0, limit=40, remote=(), after=(), held=()):
    def size(x):
        return math.prod(x.shape) * jnp.dtype(x.dtype).itemsize

    count, results = len(inputs), len(out_shape)
    extra = len(after) + len(held)

    def run(*refs):
        outs = refs[count + extra : count + extra + results]
        return body(*refs[:count], *outs, *refs[count + extra + results + len(held) :])

    moved = sum(size(x) for x in inputs) + sum(size(x) for x in out_shape)
    return pl.pallas_call(
        run,
        out_shape=[*out_shape, *(shape_of(x.shape, x.dtype) for x in held)],
        in_specs=[HBM if i in remote else VMEM for i in range(count)] + [ANY] * extra,
        out_specs=[VMEM] * results + [ANY] * len(held),
        scratch_shapes=list(scratch),
        input_output_aliases={count + len(after) + i: results + i for i in range(len(held))},
        compiler_params=pltpu.CompilerParams(vmem_limit_bytes=limit * 2**20),
        cost_estimate=pl.CostEstimate(flops=flops, bytes_accessed=moved, transcendentals=0),
    )(*inputs, *after, *held)


def shape_of(dims, kind=LOW):
    return jax.ShapeDtypeStruct(dims, kind)


def part(index, width):
    return pl.ds(pl.multiple_of(index * width, width), width)


def places(routes, me, rows):
    token_count = routes.shape[1]
    labels = lax.broadcasted_iota(jnp.int32, (rows, 1), 0) ^ me
    first = routes[0:1, :] == labels
    second = routes[1:2, :] == labels
    either = first | second
    source = lax.broadcasted_iota(jnp.int32, (token_count, token_count), 0)
    target = lax.broadcasted_iota(jnp.int32, (token_count, token_count), 1)
    earlier = jnp.where(source < target, 1.0, 0.0).astype(LOW)
    before = matmul(jnp.where(either, 1.0, 0.0).astype(LOW), earlier)
    return jnp.where(either, before, -1.0), first, second


def table(place, k, capacity):
    slots = lax.broadcasted_iota(jnp.int32, (capacity, place.shape[1]), 0).astype(WIDE)
    return jnp.where(place[k : k + 1, :] == slots, 1.0, 0.0).astype(LOW)


def prepare(experts, tokens, routes, gain, *outs):
    far, near, own, normed_ref = outs[:-3], outs[-3], outs[-2], outs[-1]
    me = lax.axis_index("exp")
    tp = lax.axis_index("tp")
    capacity, width = own.shape
    half = width // 2
    wide = tokens[...].astype(WIDE)
    average = jnp.mean(wide, axis=-1, keepdims=True)
    centred = wide - average
    spread = jnp.mean(centred * centred, axis=-1, keepdims=True)
    normed_ref[...] = (centred * lax.rsqrt(spread + EPS) * gain[...]).astype(LOW)
    place, _, _ = places(routes[...], me, max(16, experts))
    normed_half = normed_ref[:, part(tp, half)]
    for k in range(experts - 1, 1, -1):
        far[k - 2][...] = matmul(table(place, k, capacity), normed_half).astype(LOW)
    normed = normed_ref[...]
    near[...] = matmul(table(place, 1, capacity), normed).astype(LOW)
    own[...] = matmul(table(place, 0, capacity), normed).astype(LOW)


def mixing(experts, routes, gates, high, low):
    me = lax.axis_index("exp")
    token_count = routes.shape[1]
    capacity = high.shape[2]
    place, first, second = places(routes[...], me, max(16, experts))
    gate = jnp.where(first, gates[0:1, :], 0.0) + jnp.where(second, gates[1:2, :], 0.0)
    place = place.T
    gate = gate.T
    slots = lax.broadcasted_iota(jnp.int32, (token_count, capacity), 1).astype(WIDE)
    for k in range(experts):
        weight = jnp.where(place[:, k : k + 1] == slots, gate[:, k : k + 1], 0.0)
        upper = weight.astype(LOW)
        high[k] = upper
        low[k] = (weight - upper.astype(WIDE)).astype(LOW)


def expert(split, *refs):
    rows, refs = refs[: 1 + split], refs[1 + split :]
    first, second, away, kept, inner = refs
    tp = lax.axis_index("tp")
    width, hidden = first.shape
    half = width // 2
    chunk = min(512, hidden)
    for c in range(hidden // chunk):
        columns = slice(c * chunk, (c + 1) * chunk)
        if split:
            value = matmul(rows[0][...], first[part(tp, half), columns])
            value = value + matmul(rows[1][...], first[part(1 - tp, half), columns])
        else:
            value = matmul(rows[0][...], first[:, columns])
        inner[:, columns] = jnp.maximum(value, 0.0).astype(LOW)
    away[...] = matmul(inner[...], second[:, part(1 - tp, half)]).astype(LOW)
    kept[...] = matmul(inner[...], second[:, part(tp, half)])


def expert_first(rows, first, second, away, kept, first_here, second_here, inner, arrived):
    tp = lax.axis_index("tp")
    width, hidden = first.shape
    half = width // 2
    chunk = min(512, hidden)
    columns = [slice(c * chunk, (c + 1) * chunk) for c in range(hidden // chunk)]
    loads = [
        pltpu.make_async_copy(first.at[:, c], first_here.at[:, c], arrived.at[i])
        for i, c in enumerate(columns)
    ]
    loads.append(pltpu.make_async_copy(second, second_here, arrived.at[len(columns)]))
    for load in loads:
        load.start()
    for c, load in zip(columns, loads):
        load.wait()
        inner[:, c] = jnp.maximum(matmul(rows[...], first_here[:, c]), 0.0).astype(LOW)
    loads[-1].wait()
    away[...] = matmul(inner[...], second_here[:, part(1 - tp, half)]).astype(LOW)
    kept[...] = matmul(inner[...], second_here[:, part(tp, half)])


def idle():
    pass


def combine(experts, tokens, high, low, *refs):
    returned, out = refs[:-1], refs[-1]
    tp = lax.axis_index("tp")
    half = out.shape[1]
    mixed = tokens[:, part(tp, half)].astype(WIDE)
    for k in range(experts):
        rows = returned[k][...]
        mixed = mixed + (matmul(high[k], rows) + matmul(low[k], rows))
    out[...] = mixed.astype(LOW)


def project(mine, other, gain, weight, out):
    tp = lax.axis_index("tp")
    half = mine.shape[1]
    own = mine[...].astype(WIDE)
    rest = other[...].astype(WIDE)
    average = (
        jnp.sum(own, axis=-1, keepdims=True) + jnp.sum(rest, axis=-1, keepdims=True)
    ) / (2 * half)
    own = own - average
    rest = rest - average
    spread = (
        jnp.sum(own * own, axis=-1, keepdims=True) + jnp.sum(rest * rest, axis=-1, keepdims=True)
    ) / (2 * half)
    factor = lax.rsqrt(spread + EPS)
    own = (own * factor * gain[:, part(tp, half)]).astype(LOW)
    rest = (rest * factor * gain[:, part(1 - tp, half)]).astype(LOW)
    value = matmul(own, weight[part(tp, half), :]) + matmul(rest, weight[part(1 - tp, half), :])
    out[...] = value.astype(LOW)


def attend(
    mine, other, queries, upstream, key_w, value_w, hidden, context, away, kept, keys, values, dkeys, dvalues
):
    tp = lax.axis_index("tp")
    sec = lax.axis_index("sec")
    token_count, half = mine.shape
    width = 2 * half
    scale = 1.0 / math.sqrt(HD)

    @pl.when(sec != 0)
    def _():
        for weight, target in ((key_w, keys), (value_w, values)):
            value = matmul(mine[...], weight[part(tp, half), :])
            value = value + matmul(other[...], weight[part(1 - tp, half), :])
            target[...] = value.astype(LOW)
        for s in range(token_count // SEQ):
            for h in range(queries.shape[1] // HD):
                rows, columns = slice(s * SEQ, (s + 1) * SEQ), slice(h * HD, (h + 1) * HD)
                query, key = queries[rows, columns], keys[rows, columns]
                value, up = values[rows, columns], upstream[rows, columns]
                powers = jnp.exp(matmul(key, query, NT) * scale)
                probs = powers * (1.0 / jnp.sum(powers, axis=0, keepdims=True))
                low = probs.astype(LOW)
                dprobs = matmul(value, up, NT)
                rowdot = jnp.sum(dprobs * probs, axis=0, keepdims=True)
                dscores = (probs * (dprobs - rowdot)).astype(LOW)
                dvalues[rows, columns] = matmul(low, up).astype(LOW)
                dkeys[rows, columns] = (matmul(dscores, query) * scale).astype(LOW)
                context[rows, columns] = matmul(low, value, TN).astype(LOW)
        side = sec % 2
        pairs = lax.axis_size("sec") // 2
        block = width // (2 * pairs)
        for target, parity in ((away, 1 - side), (kept, side)):
            for i in range(pairs):
                rows = part(2 * i + parity, block)
                value = matmul(dkeys[...], key_w[rows, :], NT)
                value = value + matmul(dvalues[...], value_w[rows, :], NT)
                target[:, i * block : (i + 1) * block] = value.astype(target.dtype)

    @pl.when(sec == 0)
    def _():
        context[...] = hidden[...]
        away[...] = jnp.zeros_like(away)
        kept[...] = jnp.zeros_like(kept)


def gather_term(kept, arrived, own, *sent):
    tp = lax.axis_index("tp")
    here = lax.axis_index("sec") // 2 * lax.axis_size("tp") + tp
    width = own.shape[1]
    for k in range(len(sent) + 1):
        columns = part(here ^ k, width)
        value = kept[:, columns] + arrived[:, columns].astype(WIDE)
        if k == 0:
            own[...] = value
        else:
            sent[k - 1][...] = value.astype(LOW)


def swap(block, axis, step):
    size = lax.axis_size(axis)
    return lax.ppermute(block, axis, [(i, i ^ step) for i in range(size)])


def shards(
    tokens,
    routes,
    gate_weights,
    moe_gain,
    attn_gain,
    expert_in,
    expert_out,
    query_weight,
    key_weight,
    value_weight,
    cotangent,
):
    token_rows = tokens[0]
    route_rows = routes[0].T
    gate_rows = gate_weights[0].T
    token_count, model_width = token_rows.shape
    experts = lax.axis_size("exp")
    sections = lax.axis_size("sec")
    tp_size = lax.axis_size("tp")
    sec = lax.axis_index("sec")
    half = model_width // tp_size
    capacity = 3 * token_count // experts
    weight_first = expert_in[0, 0]
    weight_second = expert_out[0, 0]
    units = weight_first.shape[1]

    middle = max(2, experts // 2 + 1)
    groups = [list(range(middle - 1, 1, -1)), list(range(experts - 1, middle - 1, -1))]
    row_half, row_whole = shape_of((capacity, half)), shape_of((capacity, model_width))
    *far_rows, near_rows, own_rows = call(
        functools.partial(prepare, experts),
        [row_half] * (experts - 2) + [row_whole] * 2,
        [token_rows, route_rows, moe_gain],
        [pltpu.VMEM((token_count, model_width), LOW)],
        flops=2 * 3 * token_count * token_count * model_width,
    )
    def hold(array, after):
        return call(idle, [], [], after=after, held=[array])[0]

    def joined(group):
        blocks = [swap(far_rows[k - 2], "exp", k) for k in group]
        return blocks[0] if len(blocks) == 1 else jnp.concatenate(blocks, axis=0)

    def total(away, kept):
        return (kept + swap(away, "tp", 1).astype(WIDE)).astype(LOW)

    def through(rows, after):
        count = rows[0].shape[0]
        return call(
            functools.partial(expert, len(rows) - 1),
            [shape_of((count, half)), shape_of((count, half), WIDE)],
            [*rows, weight_first, weight_second],
            [pltpu.VMEM((count, units), LOW)],
            flops=4 * count * model_width * units,
            after=after,
        )

    arriving = [joined(group) for group in groups]
    loads = max(1, units // 512) + 1
    own_away, own_kept, weight_first, weight_second, near_rows = call(
        expert_first,
        [
            row_half,
            shape_of((capacity, half), WIDE),
            shape_of(weight_first.shape),
            shape_of(weight_second.shape),
        ],
        [own_rows, weight_first, weight_second],
        [pltpu.VMEM((capacity, units), LOW), pltpu.SemaphoreType.DMA((loads,))],
        flops=4 * capacity * model_width * units,
        remote=(1, 2),
        limit=44,
        held=[near_rows],
    )
    near = swap(near_rows, "exp", 1)
    returned = {0: total(own_away, own_kept)}
    arriving[0] = hold(arriving[0], [own_away])
    others = [swap(arriving[0], "tp", 1)]
    high, low = call(
        functools.partial(mixing, experts),
        [shape_of((experts, token_count, capacity))] * 2,
        [route_rows, gate_rows],
        after=[arriving[0]],
    )
    arriving[1] = hold(arriving[1], [high])
    others.append(swap(arriving[1], "tp", 1))
    results = [through([arriving[0], others[0]], [returned[0], arriving[1]])]
    near_away, near_kept = through([near], [results[0][0]])
    results.append(through([arriving[1], others[1]], [near_away]))
    for group, (away, kept) in zip(groups, results):
        mixed = total(away, kept)
        for i, k in enumerate(group):
            block = mixed if len(group) == 1 else mixed[i * capacity : (i + 1) * capacity]
            returned[k] = swap(block, "exp", k)
    near_away = hold(near_away, [results[1][0]])
    returned[1] = swap(total(near_away, near_kept), "exp", 1)

    hidden_half = call(
        functools.partial(combine, experts),
        [shape_of((token_count, half))],
        [token_rows, high, low, *(returned[k] for k in range(experts))],
        flops=4 * 3 * token_count * token_count * half,
    )[0]

    first = hidden_half
    for i in range(1, sections // 2):
        moved = lax.ppermute(hidden_half, "sec", [(0, 2 * i)])
        first = jnp.where(sec == 2 * i, moved, first)
    for i in range(sections // 2 - 1, -1, -1):
        pairs = [(t, (2 * i + 1) * tp_size + (t ^ 1)) for t in range(tp_size)]
        moved = lax.ppermute(hidden_half, ("sec", "tp"), pairs)
        first = jnp.where(sec == 2 * i + 1, moved, first)
    hidden_other = swap(hidden_half, "tp", 1)
    beside = swap(first, "sec", 1)
    mine = jnp.where(sec % 2 == 0, first, beside)
    other = jnp.where(sec % 2 == 0, beside, first)

    local_width = query_weight.shape[2]
    queries = call(
        project,
        [shape_of((token_count, local_width))],
        [hidden_half, hidden_other, attn_gain, query_weight[0]],
        flops=2 * token_count * model_width * local_width,
    )[0]
    context, away, kept = call(
        attend,
        [
            shape_of((token_count, local_width)),
            shape_of((token_count, model_width // 2)),
            shape_of((token_count, model_width // 2), WIDE),
        ],
        [mine, other, queries, cotangent[0], key_weight[0], value_weight[0], hidden_half],
        [pltpu.VMEM((token_count, local_width), LOW)] * 4,
        flops=10 * token_count * model_width * local_width,
    )

    own = model_width // (sections * tp_size)
    count = sections // 2 * tp_size
    both = sections * tp_size
    blocks = call(
        gather_term,
        [shape_of((token_count, own), WIDE)] + [shape_of((token_count, own))] * (count - 1),
        [kept, swap(away, "sec", 1)],
    )
    total = blocks[0]
    for k in range(1, count):
        pairs = []
        for i in range(both):
            section, t = i // tp_size, i % tp_size
            target = (section // 2 * tp_size + t) ^ k
            pairs.append((i, (target // tp_size * 2 + section % 2) * tp_size + target % tp_size))
        total = total + lax.ppermute(blocks[k], ("sec", "tp"), pairs).astype(WIDE)
    return (context[None], total.astype(LOW))


def solution(mesh):
    placed = (
        P("sec", "exp", None),
        P("sec", "exp", None),
        P("sec", "exp", None),
        P("sec", None),
        P("sec", None),
        P("sec", "exp", None, "tp"),
        P("sec", "exp", "tp", None),
        P("sec", None, "tp"),
        P("sec", None, "tp"),
        P("sec", None, "tp"),
        P("sec", "exp", "tp"),
    )
    return jax.shard_map(
        shards,
        mesh=mesh,
        in_specs=placed,
        out_specs=(P("sec", "exp", "tp"), P("exp", ("sec", "tp"))),
        check_vma=False,
    )
```

```python
import functools
import math

import jax
import jax.numpy as jnp
from jax import lax
from jax.experimental import pallas as pl
from jax.experimental.pallas import tpu as pltpu
from jax.sharding import PartitionSpec as P

HD = 128
SEQ = 128
EPS = 1e-05

LOW = jnp.bfloat16
WIDE = jnp.float32
VMEM = pl.BlockSpec(memory_space=pltpu.VMEM)
HBM = pl.BlockSpec(memory_space=pltpu.HBM)
ANY = pl.BlockSpec(memory_space=pl.ANY)
NT = (((1,), (1,)), ((), ()))
TN = (((0,), (0,)), ((), ()))


def matmul(a, b, dims=(((1,), (0,)), ((), ()))):
    return lax.dot_general(a, b, dims, preferred_element_type=WIDE)


def call(body, out_shape, inputs, scratch=(), flops=0, limit=16, remote=(), after=(), held=()):
    def size(x):
        return math.prod(x.shape) * jnp.dtype(x.dtype).itemsize

    count, results = len(inputs), len(out_shape)
    extra = len(after) + len(held)

    def run(*refs):
        outs = refs[count + extra : count + extra + results]
        return body(*refs[:count], *outs, *refs[count + extra + results + len(held) :])

    moved = sum(size(x) for x in inputs) + sum(size(x) for x in out_shape)
    return pl.pallas_call(
        run,
        out_shape=[*out_shape, *(shape_of(x.shape, x.dtype) for x in held)],
        in_specs=[HBM if i in remote else VMEM for i in range(count)] + [ANY] * extra,
        out_specs=[VMEM] * results + [ANY] * len(held),
        scratch_shapes=list(scratch),
        input_output_aliases={count + len(after) + i: results + i for i in range(len(held))},
        compiler_params=pltpu.CompilerParams(vmem_limit_bytes=limit * 2**20),
        cost_estimate=pl.CostEstimate(flops=flops, bytes_accessed=moved, transcendentals=0),
    )(*inputs, *after, *held)


def shape_of(dims, kind=LOW):
    return jax.ShapeDtypeStruct(dims, kind)


def part(index, width):
    return pl.ds(pl.multiple_of(index * width, width), width)


def places(routes, me, rows):
    token_count = routes.shape[1]
    labels = lax.broadcasted_iota(jnp.int32, (rows, 1), 0) ^ me
    first = routes[0:1, :] == labels
    second = routes[1:2, :] == labels
    either = first | second
    source = lax.broadcasted_iota(jnp.int32, (token_count, token_count), 0)
    target = lax.broadcasted_iota(jnp.int32, (token_count, token_count), 1)
    earlier = jnp.where(source < target, 1.0, 0.0).astype(LOW)
    before = matmul(jnp.where(either, 1.0, 0.0).astype(LOW), earlier)
    return jnp.where(either, before, -1.0), first, second


def table(place, k, capacity):
    slots = lax.broadcasted_iota(jnp.int32, (capacity, place.shape[1]), 0).astype(WIDE)
    return jnp.where(place[k : k + 1, :] == slots, 1.0, 0.0).astype(LOW)


def prepare(experts, tokens, routes, gain, *outs):
    far, near, own, normed_ref = outs[:-3], outs[-3], outs[-2], outs[-1]
    me = lax.axis_index("exp")
    tp = lax.axis_index("tp")
    capacity, width = own.shape
    half = width // 2
    wide = tokens[...].astype(WIDE)
    average = jnp.mean(wide, axis=-1, keepdims=True)
    centred = wide - average
    spread = jnp.mean(centred * centred, axis=-1, keepdims=True)
    normed_ref[...] = (centred * lax.rsqrt(spread + EPS) * gain[...]).astype(LOW)
    place, _, _ = places(routes[...], me, max(16, experts))
    normed_half = normed_ref[:, part(tp, half)]
    for k in range(experts - 1, 1, -1):
        far[k - 2][...] = matmul(table(place, k, capacity), normed_half).astype(LOW)
    normed = normed_ref[...]
    near[...] = matmul(table(place, 1, capacity), normed).astype(LOW)
    own[...] = matmul(table(place, 0, capacity), normed).astype(LOW)


def mixing(experts, routes, gates, high, low):
    me = lax.axis_index("exp")
    token_count = routes.shape[1]
    capacity = high.shape[2]
    place, first, second = places(routes[...], me, max(16, experts))
    gate = jnp.where(first, gates[0:1, :], 0.0) + jnp.where(second, gates[1:2, :], 0.0)
    place = place.T
    gate = gate.T
    slots = lax.broadcasted_iota(jnp.int32, (token_count, capacity), 1).astype(WIDE)
    for k in range(experts):
        weight = jnp.where(place[:, k : k + 1] == slots, gate[:, k : k + 1], 0.0)
        upper = weight.astype(LOW)
        high[k] = upper
        low[k] = (weight - upper.astype(WIDE)).astype(LOW)


def expert(split, *refs):
    rows, refs = refs[: 1 + split], refs[1 + split :]
    first, second, away, kept, inner = refs
    tp = lax.axis_index("tp")
    width, hidden = first.shape
    half = width // 2
    chunk = min(512, hidden)
    for c in range(hidden // chunk):
        columns = slice(c * chunk, (c + 1) * chunk)
        if split:
            value = matmul(rows[0][...], first[part(tp, half), columns])
            value = value + matmul(rows[1][...], first[part(1 - tp, half), columns])
        else:
            value = matmul(rows[0][...], first[:, columns])
        inner[:, columns] = jnp.maximum(value, 0.0).astype(LOW)
    away[...] = matmul(inner[...], second[:, part(1 - tp, half)]).astype(LOW)
    kept[...] = matmul(inner[...], second[:, part(tp, half)])


def load_and_multiply(rows, first, second, first_here, second_here, inner, arrived, away, kept):
    tp = lax.axis_index("tp")
    width, hidden = first.shape
    half = width // 2
    chunk = min(512, hidden)
    columns = [slice(c * chunk, (c + 1) * chunk) for c in range(hidden // chunk)]
    loads = [
        pltpu.make_async_copy(first.at[:, c], first_here.at[:, c], arrived.at[i])
        for i, c in enumerate(columns)
    ]
    loads.append(pltpu.make_async_copy(second, second_here, arrived.at[len(columns)]))
    for load in loads:
        load.start()
    for c, load in zip(columns, loads):
        load.wait()
        if rows is not None:
            inner[:, c] = jnp.maximum(matmul(rows[...], first_here[:, c]), 0.0).astype(LOW)
    loads[-1].wait()
    if rows is not None:
        away[...] = matmul(inner[...], second_here[:, part(1 - tp, half)]).astype(LOW)
        kept[...] = matmul(inner[...], second_here[:, part(tp, half)])


def expert_early(rows, first, second, away, kept, first_here, second_here, inner, arrived):
    @pl.when(lax.axis_index("sec") % 2 == 1)
    def _():
        load_and_multiply(rows, first, second, first_here, second_here, inner, arrived, away, kept)


def expert_late(
    rows, first, second, away_early, kept_early, away, kept, first_here, second_here, inner, arrived
):
    odd = lax.axis_index("sec") % 2 == 1

    @pl.when(odd)
    def _():
        load_and_multiply(None, first, second, first_here, second_here, inner, arrived, away, kept)
        away[...] = away_early[...]
        kept[...] = kept_early[...]

    @pl.when(jnp.logical_not(odd))
    def _():
        load_and_multiply(rows, first, second, first_here, second_here, inner, arrived, away, kept)


def idle():
    pass


def combine(experts, tokens, high, low, *refs):
    returned, out = refs[:-1], refs[-1]
    tp = lax.axis_index("tp")
    half = out.shape[1]
    mixed = tokens[:, part(tp, half)].astype(WIDE)
    for k in range(experts):
        rows = returned[k][...]
        mixed = mixed + (matmul(high[k], rows) + matmul(low[k], rows))
    out[...] = mixed.astype(LOW)


def project(mine, other, gain, weight, out):
    tp = lax.axis_index("tp")
    half = mine.shape[1]
    own = mine[...].astype(WIDE)
    rest = other[...].astype(WIDE)
    average = (
        jnp.sum(own, axis=-1, keepdims=True) + jnp.sum(rest, axis=-1, keepdims=True)
    ) / (2 * half)
    own = own - average
    rest = rest - average
    spread = (
        jnp.sum(own * own, axis=-1, keepdims=True) + jnp.sum(rest * rest, axis=-1, keepdims=True)
    ) / (2 * half)
    factor = lax.rsqrt(spread + EPS)
    own = (own * factor * gain[:, part(tp, half)]).astype(LOW)
    rest = (rest * factor * gain[:, part(1 - tp, half)]).astype(LOW)
    value = matmul(own, weight[part(tp, half), :]) + matmul(rest, weight[part(1 - tp, half), :])
    out[...] = value.astype(LOW)


def attend(
    mine, other, queries, upstream, key_w, value_w, hidden, context, away, kept, keys, values, dkeys, dvalues
):
    tp = lax.axis_index("tp")
    sec = lax.axis_index("sec")
    token_count, half = mine.shape
    width = 2 * half
    scale = 1.0 / math.sqrt(HD)

    @pl.when(sec != 0)
    def _():
        for weight, target in ((key_w, keys), (value_w, values)):
            value = matmul(mine[...], weight[part(tp, half), :])
            value = value + matmul(other[...], weight[part(1 - tp, half), :])
            target[...] = value.astype(LOW)
        for s in range(token_count // SEQ):
            for h in range(queries.shape[1] // HD):
                rows, columns = slice(s * SEQ, (s + 1) * SEQ), slice(h * HD, (h + 1) * HD)
                query, key = queries[rows, columns], keys[rows, columns]
                value, up = values[rows, columns], upstream[rows, columns]
                powers = jnp.exp(matmul(key, query, NT) * scale)
                probs = powers * (1.0 / jnp.sum(powers, axis=0, keepdims=True))
                low = probs.astype(LOW)
                dprobs = matmul(value, up, NT)
                rowdot = jnp.sum(dprobs * probs, axis=0, keepdims=True)
                dscores = (probs * (dprobs - rowdot)).astype(LOW)
                dvalues[rows, columns] = matmul(low, up).astype(LOW)
                dkeys[rows, columns] = (matmul(dscores, query) * scale).astype(LOW)
                context[rows, columns] = matmul(low, value, TN).astype(LOW)
        side = sec % 2
        pairs = lax.axis_size("sec") // 2
        block = width // (2 * pairs)
        for target, parity in ((away, 1 - side), (kept, side)):
            for i in range(pairs):
                rows = part(2 * i + parity, block)
                value = matmul(dkeys[...], key_w[rows, :], NT)
                value = value + matmul(dvalues[...], value_w[rows, :], NT)
                target[:, i * block : (i + 1) * block] = value.astype(target.dtype)

    @pl.when(sec == 0)
    def _():
        context[...] = hidden[...]
        away[...] = jnp.zeros_like(away)
        kept[...] = jnp.zeros_like(kept)


def gather_term(kept, arrived, own, *sent):
    tp = lax.axis_index("tp")
    here = lax.axis_index("sec") // 2 * lax.axis_size("tp") + tp
    width = own.shape[1]
    for k in range(len(sent) + 1):
        columns = part(here ^ k, width)
        value = kept[:, columns] + arrived[:, columns].astype(WIDE)
        if k == 0:
            own[...] = value
        else:
            sent[k - 1][...] = value.astype(LOW)


def swap(block, axis, step):
    size = lax.axis_size(axis)
    return lax.ppermute(block, axis, [(i, i ^ step) for i in range(size)])


def shards(
    tokens,
    routes,
    gate_weights,
    moe_gain,
    attn_gain,
    expert_in,
    expert_out,
    query_weight,
    key_weight,
    value_weight,
    cotangent,
):
    token_rows = tokens[0]
    route_rows = routes[0].T
    gate_rows = gate_weights[0].T
    token_count, model_width = token_rows.shape
    experts = lax.axis_size("exp")
    sections = lax.axis_size("sec")
    tp_size = lax.axis_size("tp")
    sec = lax.axis_index("sec")
    half = model_width // tp_size
    capacity = 3 * token_count // experts
    weight_first = expert_in[0, 0]
    weight_second = expert_out[0, 0]
    units = weight_first.shape[1]

    middle = max(2, experts // 2 + 1)
    groups = [list(range(middle - 1, 1, -1)), list(range(experts - 1, middle - 1, -1))]
    row_half, row_whole = shape_of((capacity, half)), shape_of((capacity, model_width))
    *far_rows, near_rows, own_rows = call(
        functools.partial(prepare, experts),
        [row_half] * (experts - 2) + [row_whole] * 2,
        [token_rows, route_rows, moe_gain],
        [pltpu.VMEM((token_count, model_width), LOW)],
        flops=2 * 3 * token_count * token_count * model_width,
    )
    def hold(array, after):
        return call(idle, [], [], after=after, held=[array])[0]

    def joined(group):
        blocks = [swap(far_rows[k - 2], "exp", k) for k in group]
        return blocks[0] if len(blocks) == 1 else jnp.concatenate(blocks, axis=0)

    def total(away, kept):
        return (kept + swap(away, "tp", 1).astype(WIDE)).astype(LOW)

    def through(rows, after):
        count = rows[0].shape[0]
        return call(
            functools.partial(expert, len(rows) - 1),
            [shape_of((count, half)), shape_of((count, half), WIDE)],
            [*rows, weight_first, weight_second],
            [pltpu.VMEM((count, units), LOW)],
            flops=4 * count * model_width * units,
            limit=24,
            after=after,
        )

    loads = max(1, units // 512) + 1
    block_shapes = [row_half, shape_of((capacity, half), WIDE)]
    weight_shapes = [weight_first.shape, weight_second.shape]
    weights = [weight_first, weight_second]
    work = [pltpu.VMEM((capacity, units), LOW), pltpu.SemaphoreType.DMA((loads,))]
    early_away, early_kept, *far_rows = call(
        expert_early,
        block_shapes,
        [own_rows, *weights],
        [pltpu.VMEM(dims, LOW) for dims in weight_shapes] + work,
        remote=(1, 2),
        limit=50,
        held=far_rows,
    )
    arriving = [joined(group) for group in groups]
    own_away, own_kept, weight_first, weight_second, near_rows = call(
        expert_late,
        block_shapes + [shape_of(dims) for dims in weight_shapes],
        [own_rows, *weights, early_away, early_kept],
        work,
        flops=4 * capacity * model_width * units,
        remote=(1, 2),
        limit=44,
        held=[near_rows],
    )
    near = swap(near_rows, "exp", 1)
    returned = {0: total(own_away, own_kept)}
    arriving[0] = hold(arriving[0], [own_away])
    others = [swap(arriving[0], "tp", 1)]
    high, low = call(
        functools.partial(mixing, experts),
        [shape_of((experts, token_count, capacity))] * 2,
        [route_rows, gate_rows],
        after=[arriving[0]],
    )
    arriving[1] = hold(arriving[1], [high])
    others.append(swap(arriving[1], "tp", 1))
    results = [through([arriving[0], others[0]], [returned[0], arriving[1]])]
    near_away, near_kept = through([near], [results[0][0]])
    results.append(through([arriving[1], others[1]], [near_away]))
    for group, (away, kept) in zip(groups, results):
        mixed = total(away, kept)
        for i, k in enumerate(group):
            block = mixed if len(group) == 1 else mixed[i * capacity : (i + 1) * capacity]
            returned[k] = swap(block, "exp", k)
    near_away = hold(near_away, [results[1][0]])
    returned[1] = swap(total(near_away, near_kept), "exp", 1)

    hidden_half = call(
        functools.partial(combine, experts),
        [shape_of((token_count, half))],
        [token_rows, high, low, *(returned[k] for k in range(experts))],
        flops=4 * 3 * token_count * token_count * half,
    )[0]

    first = hidden_half
    for i in range(1, sections // 2):
        moved = lax.ppermute(hidden_half, "sec", [(0, 2 * i)])
        first = jnp.where(sec == 2 * i, moved, first)
    for i in range(sections // 2 - 1, -1, -1):
        pairs = [(t, (2 * i + 1) * tp_size + (t ^ 1)) for t in range(tp_size)]
        moved = lax.ppermute(hidden_half, ("sec", "tp"), pairs)
        first = jnp.where(sec == 2 * i + 1, moved, first)
    hidden_other = swap(hidden_half, "tp", 1)
    beside = swap(first, "sec", 1)
    mine = jnp.where(sec % 2 == 0, first, beside)
    other = jnp.where(sec % 2 == 0, beside, first)

    local_width = query_weight.shape[2]
    queries = call(
        project,
        [shape_of((token_count, local_width))],
        [hidden_half, hidden_other, attn_gain, query_weight[0]],
        flops=2 * token_count * model_width * local_width,
    )[0]
    context, away, kept = call(
        attend,
        [
            shape_of((token_count, local_width)),
            shape_of((token_count, model_width // 2)),
            shape_of((token_count, model_width // 2), WIDE),
        ],
        [mine, other, queries, cotangent[0], key_weight[0], value_weight[0], hidden_half],
        [pltpu.VMEM((token_count, local_width), LOW)] * 4,
        flops=10 * token_count * model_width * local_width,
    )

    own = model_width // (sections * tp_size)
    count = sections // 2 * tp_size
    both = sections * tp_size
    blocks = call(
        gather_term,
        [shape_of((token_count, own), WIDE)] + [shape_of((token_count, own))] * (count - 1),
        [kept, swap(away, "sec", 1)],
    )
    total = blocks[0]
    for k in range(1, count):
        pairs = []
        for i in range(both):
            section, t = i // tp_size, i % tp_size
            target = (section // 2 * tp_size + t) ^ k
            pairs.append((i, (target // tp_size * 2 + section % 2) * tp_size + target % tp_size))
        total = total + lax.ppermute(blocks[k], ("sec", "tp"), pairs).astype(WIDE)
    return (context[None], total.astype(LOW))


def solution(mesh):
    placed = (
        P("sec", "exp", None),
        P("sec", "exp", None),
        P("sec", "exp", None),
        P("sec", None),
        P("sec", None),
        P("sec", "exp", None, "tp"),
        P("sec", "exp", "tp", None),
        P("sec", None, "tp"),
        P("sec", None, "tp"),
        P("sec", None, "tp"),
        P("sec", "exp", "tp"),
    )
    return jax.shard_map(
        shards,
        mesh=mesh,
        in_specs=placed,
        out_specs=(P("sec", "exp", "tp"), P("exp", ("sec", "tp"))),
        check_vma=False,
    )
```

```python
import functools
import math

import jax
import jax.numpy as jnp
from jax import lax
from jax.experimental import pallas as pl
from jax.experimental.pallas import tpu as pltpu
from jax.sharding import PartitionSpec as P

HD = 128
SEQ = 128
EPS = 1e-05

LOW = jnp.bfloat16
WIDE = jnp.float32
VMEM = pl.BlockSpec(memory_space=pltpu.VMEM)
HBM = pl.BlockSpec(memory_space=pltpu.HBM)
ANY = pl.BlockSpec(memory_space=pl.ANY)
NT = (((1,), (1,)), ((), ()))
TN = (((0,), (0,)), ((), ()))


def matmul(a, b, dims=(((1,), (0,)), ((), ()))):
    return lax.dot_general(a, b, dims, preferred_element_type=WIDE)


def call(body, out_shape, inputs, scratch=(), flops=0, limit=16, remote=(), after=(), held=()):
    def size(x):
        return math.prod(x.shape) * jnp.dtype(x.dtype).itemsize

    count, results = len(inputs), len(out_shape)
    extra = len(after) + len(held)

    def run(*refs):
        outs = refs[count + extra : count + extra + results]
        return body(*refs[:count], *outs, *refs[count + extra + results + len(held) :])

    moved = sum(size(x) for x in inputs) + sum(size(x) for x in out_shape)
    return pl.pallas_call(
        run,
        out_shape=[*out_shape, *(shape_of(x.shape, x.dtype) for x in held)],
        in_specs=[HBM if i in remote else VMEM for i in range(count)] + [ANY] * extra,
        out_specs=[VMEM] * results + [ANY] * len(held),
        scratch_shapes=list(scratch),
        input_output_aliases={count + len(after) + i: results + i for i in range(len(held))},
        compiler_params=pltpu.CompilerParams(vmem_limit_bytes=limit * 2**20),
        cost_estimate=pl.CostEstimate(flops=flops, bytes_accessed=moved, transcendentals=0),
    )(*inputs, *after, *held)


def shape_of(dims, kind=LOW):
    return jax.ShapeDtypeStruct(dims, kind)


def part(index, width):
    return pl.ds(pl.multiple_of(index * width, width), width)


def triangle(out):
    source = lax.broadcasted_iota(jnp.int32, out.shape, 0)
    target = lax.broadcasted_iota(jnp.int32, out.shape, 1)
    out[...] = jnp.where(source < target, 1.0, 0.0).astype(LOW)


def places(routes, earlier, me, rows):
    labels = lax.broadcasted_iota(jnp.int32, (rows, 1), 0) ^ me
    first = routes[0:1, :] == labels
    second = routes[1:2, :] == labels
    either = first | second
    before = matmul(jnp.where(either, 1.0, 0.0).astype(LOW), earlier)
    return jnp.where(either, before, -1.0), first, second


def table(place, k, capacity):
    slots = lax.broadcasted_iota(jnp.int32, (capacity, place.shape[1]), 0).astype(WIDE)
    return jnp.where(place[k : k + 1, :] == slots, 1.0, 0.0).astype(LOW)


def prepare(experts, tokens, routes, gain, earlier, *outs):
    far, near, own, normed_ref = outs[:-3], outs[-3], outs[-2], outs[-1]
    me = lax.axis_index("exp")
    tp = lax.axis_index("tp")
    capacity, width = own.shape
    half = width // 2
    wide = tokens[...].astype(WIDE)
    average = jnp.mean(wide, axis=-1, keepdims=True)
    centred = wide - average
    spread = jnp.mean(centred * centred, axis=-1, keepdims=True)
    normed_ref[...] = (centred * lax.rsqrt(spread + EPS) * gain[...]).astype(LOW)
    place, _, _ = places(routes[...], earlier[...], me, max(16, experts))
    normed_half = normed_ref[:, part(tp, half)]
    for k in range(experts - 1, 1, -1):
        far[k - 2][...] = matmul(table(place, k, capacity), normed_half).astype(LOW)
    normed = normed_ref[...]
    near[...] = matmul(table(place, 1, capacity), normed).astype(LOW)
    own[...] = matmul(table(place, 0, capacity), normed).astype(LOW)


def mixing(experts, routes, gates, earlier, high, low):
    me = lax.axis_index("exp")
    token_count = routes.shape[1]
    capacity = high.shape[2]
    place, first, second = places(routes[...], earlier[...], me, max(16, experts))
    gate = jnp.where(first, gates[0:1, :], 0.0) + jnp.where(second, gates[1:2, :], 0.0)
    place = place.T
    gate = gate.T
    slots = lax.broadcasted_iota(jnp.int32, (token_count, capacity), 1).astype(WIDE)
    for k in range(experts):
        weight = jnp.where(place[:, k : k + 1] == slots, gate[:, k : k + 1], 0.0)
        upper = weight.astype(LOW)
        high[k] = upper
        low[k] = (weight - upper.astype(WIDE)).astype(LOW)


def expert(split, *refs):
    rows, refs = refs[: 1 + split], refs[1 + split :]
    first, second, away, kept, inner = refs
    tp = lax.axis_index("tp")
    width, hidden = first.shape
    half = width // 2
    chunk = min(512, hidden)
    for c in range(hidden // chunk):
        columns = slice(c * chunk, (c + 1) * chunk)
        if split:
            value = matmul(rows[0][...], first[part(tp, half), columns])
            value = value + matmul(rows[1][...], first[part(1 - tp, half), columns])
        else:
            value = matmul(rows[0][...], first[:, columns])
        inner[:, columns] = jnp.maximum(value, 0.0).astype(LOW)
    away[...] = matmul(inner[...], second[:, part(1 - tp, half)]).astype(LOW)
    kept[...] = matmul(inner[...], second[:, part(tp, half)])


def expert_first(rows, first, second, away, kept, first_here, second_here, inner, arrived):
    tp = lax.axis_index("tp")
    width, hidden = first.shape
    half = width // 2
    chunk = min(512, hidden)
    columns = [slice(c * chunk, (c + 1) * chunk) for c in range(hidden // chunk)]
    loads = [
        pltpu.make_async_copy(first.at[:, c], first_here.at[:, c], arrived.at[i])
        for i, c in enumerate(columns)
    ]
    loads.append(pltpu.make_async_copy(second, second_here, arrived.at[len(columns)]))
    for load in loads:
        load.start()
    for c, load in zip(columns, loads):
        load.wait()
        inner[:, c] = jnp.maximum(matmul(rows[...], first_here[:, c]), 0.0).astype(LOW)
    loads[-1].wait()
    away[...] = matmul(inner[...], second_here[:, part(1 - tp, half)]).astype(LOW)
    kept[...] = matmul(inner[...], second_here[:, part(tp, half)])


def idle():
    pass


def combine(experts, tokens, high, low, *refs):
    returned, out = refs[:-1], refs[-1]
    tp = lax.axis_index("tp")
    half = out.shape[1]
    mixed = tokens[:, part(tp, half)].astype(WIDE)
    for k in range(experts):
        rows = returned[k][...]
        mixed = mixed + (matmul(high[k], rows) + matmul(low[k], rows))
    out[...] = mixed.astype(LOW)


def project(mine, other, gain, weight, out):
    tp = lax.axis_index("tp")
    half = mine.shape[1]
    own = mine[...].astype(WIDE)
    rest = other[...].astype(WIDE)
    average = (
        jnp.sum(own, axis=-1, keepdims=True) + jnp.sum(rest, axis=-1, keepdims=True)
    ) / (2 * half)
    own = own - average
    rest = rest - average
    spread = (
        jnp.sum(own * own, axis=-1, keepdims=True) + jnp.sum(rest * rest, axis=-1, keepdims=True)
    ) / (2 * half)
    factor = lax.rsqrt(spread + EPS)
    own = (own * factor * gain[:, part(tp, half)]).astype(LOW)
    rest = (rest * factor * gain[:, part(1 - tp, half)]).astype(LOW)
    value = matmul(own, weight[part(tp, half), :]) + matmul(rest, weight[part(1 - tp, half), :])
    out[...] = value.astype(LOW)


def attend(
    mine, other, queries, upstream, key_w, value_w, hidden, context, away, kept, keys, values, dkeys, dvalues
):
    tp = lax.axis_index("tp")
    sec = lax.axis_index("sec")
    token_count, half = mine.shape
    width = 2 * half
    scale = 1.0 / math.sqrt(HD)

    @pl.when(sec != 0)
    def _():
        for weight, target in ((key_w, keys), (value_w, values)):
            value = matmul(mine[...], weight[part(tp, half), :])
            value = value + matmul(other[...], weight[part(1 - tp, half), :])
            target[...] = value.astype(LOW)
        for s in range(token_count // SEQ):
            for h in range(queries.shape[1] // HD):
                rows, columns = slice(s * SEQ, (s + 1) * SEQ), slice(h * HD, (h + 1) * HD)
                query, key = queries[rows, columns], keys[rows, columns]
                value, up = values[rows, columns], upstream[rows, columns]
                powers = jnp.exp(matmul(key, query, NT) * scale)
                probs = powers * (1.0 / jnp.sum(powers, axis=0, keepdims=True))
                low = probs.astype(LOW)
                dprobs = matmul(value, up, NT)
                rowdot = jnp.sum(dprobs * probs, axis=0, keepdims=True)
                dscores = (probs * (dprobs - rowdot)).astype(LOW)
                dvalues[rows, columns] = matmul(low, up).astype(LOW)
                dkeys[rows, columns] = (matmul(dscores, query) * scale).astype(LOW)
                context[rows, columns] = matmul(low, value, TN).astype(LOW)
        side = sec % 2
        pairs = lax.axis_size("sec") // 2
        block = width // (2 * pairs)
        for target, parity in ((away, 1 - side), (kept, side)):
            for i in range(pairs):
                rows = part(2 * i + parity, block)
                value = matmul(dkeys[...], key_w[rows, :], NT)
                value = value + matmul(dvalues[...], value_w[rows, :], NT)
                target[:, i * block : (i + 1) * block] = value.astype(target.dtype)

    @pl.when(sec == 0)
    def _():
        context[...] = hidden[...]
        away[...] = jnp.zeros_like(away)
        kept[...] = jnp.zeros_like(kept)


def gather_term(kept, arrived, own, *sent):
    tp = lax.axis_index("tp")
    here = lax.axis_index("sec") // 2 * lax.axis_size("tp") + tp
    width = own.shape[1]
    for k in range(len(sent) + 1):
        columns = part(here ^ k, width)
        value = kept[:, columns] + arrived[:, columns].astype(WIDE)
        if k == 0:
            own[...] = value
        else:
            sent[k - 1][...] = value.astype(LOW)


def swap(block, axis, step):
    size = lax.axis_size(axis)
    return lax.ppermute(block, axis, [(i, i ^ step) for i in range(size)])


def shards(
    tokens,
    routes,
    gate_weights,
    moe_gain,
    attn_gain,
    expert_in,
    expert_out,
    query_weight,
    key_weight,
    value_weight,
    cotangent,
):
    token_rows = tokens[0]
    route_rows = routes[0].T
    gate_rows = gate_weights[0].T
    token_count, model_width = token_rows.shape
    experts = lax.axis_size("exp")
    sections = lax.axis_size("sec")
    tp_size = lax.axis_size("tp")
    sec = lax.axis_index("sec")
    half = model_width // tp_size
    capacity = 3 * token_count // experts
    weight_first = expert_in[0, 0]
    weight_second = expert_out[0, 0]
    units = weight_first.shape[1]

    middle = max(2, experts // 2 + 1)
    groups = [list(range(middle - 1, 1, -1)), list(range(experts - 1, middle - 1, -1))]
    row_half, row_whole = shape_of((capacity, half)), shape_of((capacity, model_width))
    earlier = call(
        triangle,
        [shape_of((token_count, token_count))],
        [],
        flops=20 * token_count * token_count * model_width,
    )[0]
    *far_rows, near_rows, own_rows = call(
        functools.partial(prepare, experts),
        [row_half] * (experts - 2) + [row_whole] * 2,
        [token_rows, route_rows, moe_gain, earlier],
        [pltpu.VMEM((token_count, model_width), LOW)],
        flops=2 * 3 * token_count * token_count * model_width,
    )
    def hold(array, after):
        return call(idle, [], [], after=after, held=[array])[0]

    def joined(group):
        blocks = [swap(far_rows[k - 2], "exp", k) for k in group]
        return blocks[0] if len(blocks) == 1 else jnp.concatenate(blocks, axis=0)

    def total(away, kept):
        return (kept + swap(away, "tp", 1).astype(WIDE)).astype(LOW)

    def through(rows, after):
        count = rows[0].shape[0]
        return call(
            functools.partial(expert, len(rows) - 1),
            [shape_of((count, half)), shape_of((count, half), WIDE)],
            [*rows, weight_first, weight_second],
            [pltpu.VMEM((count, units), LOW)],
            flops=4 * count * model_width * units,
            limit=24,
            after=after,
        )

    arriving = [joined(groups[0])]
    later = [far_rows[k - 2] for k in groups[1]] + [near_rows]
    loads = max(1, units // 512) + 1
    own_away, own_kept, weight_first, weight_second, *later = call(
        expert_first,
        [
            row_half,
            shape_of((capacity, half), WIDE),
            shape_of(weight_first.shape),
            shape_of(weight_second.shape),
        ],
        [own_rows, weight_first, weight_second],
        [pltpu.VMEM((capacity, units), LOW), pltpu.SemaphoreType.DMA((loads,))],
        flops=4 * capacity * model_width * units,
        remote=(1, 2),
        limit=44,
        held=later,
    )
    for k, rows in zip(groups[1], later):
        far_rows[k - 2] = rows
    arriving.append(joined(groups[1]))
    near = swap(later[-1], "exp", 1)
    returned = {0: total(own_away, own_kept)}
    arriving[0] = hold(arriving[0], [own_away])
    others = [swap(arriving[0], "tp", 1)]
    high, low = call(
        functools.partial(mixing, experts),
        [shape_of((experts, token_count, capacity))] * 2,
        [route_rows, gate_rows, earlier],
        after=[arriving[0]],
    )
    others.append(swap(arriving[1], "tp", 1))
    def give_back(group, away, kept):
        mixed = total(away, kept)
        for i, k in enumerate(group):
            block = mixed if len(group) == 1 else mixed[i * capacity : (i + 1) * capacity]
            returned[k] = swap(block, "exp", k)
        return mixed

    away, kept = through([arriving[0], others[0]], [returned[0], high])
    near_away, near_kept = through([near], [away])
    mixed = give_back(groups[0], away, kept)
    returned[1] = swap(total(near_away, near_kept), "exp", 1)
    away, kept = through([arriving[1], others[1]], [near_away, mixed])
    give_back(groups[1], away, kept)
    hidden_half = call(
        functools.partial(combine, experts),
        [shape_of((token_count, half))],
        [token_rows, high, low, *(returned[k] for k in range(experts))],
        flops=4 * 3 * token_count * token_count * half,
    )[0]

    def exchange(block, pairs):
        targets = {i: i for i in range(sections * tp_size)}
        for a, b in pairs:
            targets |= {a: b, b: a}
        return lax.ppermute(block, ("sec", "tp"), list(targets.items()))

    first = hidden_half
    for i in range(sections // 2 - 1, 0, -1):
        odd = [(t, (2 * i + 1) * tp_size + (t ^ 1)) for t in range(tp_size)]
        even = [(t, 2 * i * tp_size + t) for t in range(tp_size)]
        first = jnp.where(sec == 2 * i + 1, exchange(hidden_half, odd), first)
        first = jnp.where(sec == 2 * i, exchange(hidden_half, even), first)
    odd = [(t, tp_size + (t ^ 1)) for t in range(tp_size)]
    first = jnp.where(sec == 1, exchange(hidden_half, odd), first)
    halves = [(s * tp_size, s * tp_size + 1) for s in range(1, sections)]
    hidden_other = exchange(hidden_half, halves)
    beside = swap(first, "sec", 1)
    mine = jnp.where(sec % 2 == 0, first, beside)
    other = jnp.where(sec % 2 == 0, beside, first)

    local_width = query_weight.shape[2]
    queries = call(
        project,
        [shape_of((token_count, local_width))],
        [hidden_half, hidden_other, attn_gain, query_weight[0]],
        flops=2 * token_count * model_width * local_width,
    )[0]
    context, away, kept = call(
        attend,
        [
            shape_of((token_count, local_width)),
            shape_of((token_count, model_width // 2)),
            shape_of((token_count, model_width // 2), WIDE),
        ],
        [mine, other, queries, cotangent[0], key_weight[0], value_weight[0], hidden_half],
        [pltpu.VMEM((token_count, local_width), LOW)] * 4,
        flops=10 * token_count * model_width * local_width,
    )

    own = model_width // (sections * tp_size)
    count = sections // 2 * tp_size
    both = sections * tp_size
    blocks = call(
        gather_term,
        [shape_of((token_count, own), WIDE)] + [shape_of((token_count, own))] * (count - 1),
        [kept, swap(away, "sec", 1)],
    )
    total = blocks[0]
    for k in range(1, count):
        pairs = []
        for i in range(both):
            section, t = i // tp_size, i % tp_size
            target = (section // 2 * tp_size + t) ^ k
            pairs.append((i, (target // tp_size * 2 + section % 2) * tp_size + target % tp_size))
        total = total + lax.ppermute(blocks[k], ("sec", "tp"), pairs).astype(WIDE)
    return (context[None], total.astype(LOW))


def solution(mesh):
    placed = (
        P("sec", "exp", None),
        P("sec", "exp", None),
        P("sec", "exp", None),
        P("sec", None),
        P("sec", None),
        P("sec", "exp", None, "tp"),
        P("sec", "exp", "tp", None),
        P("sec", None, "tp"),
        P("sec", None, "tp"),
        P("sec", None, "tp"),
        P("sec", "exp", "tp"),
    )
    return jax.shard_map(
        shards,
        mesh=mesh,
        in_specs=placed,
        out_specs=(P("sec", "exp", "tp"), P("exp", ("sec", "tp"))),
        check_vma=False,
    )
```

```python
import functools
import math

import jax
import jax.numpy as jnp
from jax import lax
from jax.experimental import pallas as pl
from jax.experimental.pallas import tpu as pltpu
from jax.sharding import PartitionSpec as P

HD = 128
SEQ = 128
EPS = 1e-05

LOW = jnp.bfloat16
WIDE = jnp.float32
VMEM = pl.BlockSpec(memory_space=pltpu.VMEM)
HBM = pl.BlockSpec(memory_space=pltpu.HBM)
ANY = pl.BlockSpec(memory_space=pl.ANY)
NT = (((1,), (1,)), ((), ()))
TN = (((0,), (0,)), ((), ()))


def matmul(a, b, dims=(((1,), (0,)), ((), ()))):
    return lax.dot_general(a, b, dims, preferred_element_type=WIDE)


def call(body, out_shape, inputs, scratch=(), flops=0, limit=16, remote=(), after=(), held=()):
    def size(x):
        return math.prod(x.shape) * jnp.dtype(x.dtype).itemsize

    count, results = len(inputs), len(out_shape)
    extra = len(after) + len(held)

    def run(*refs):
        outs = refs[count + extra : count + extra + results]
        return body(*refs[:count], *outs, *refs[count + extra + results + len(held) :])

    moved = sum(size(x) for x in inputs) + sum(size(x) for x in out_shape)
    return pl.pallas_call(
        run,
        out_shape=[*out_shape, *(shape_of(x.shape, x.dtype) for x in held)],
        in_specs=[HBM if i in remote else VMEM for i in range(count)] + [ANY] * extra,
        out_specs=[VMEM] * results + [ANY] * len(held),
        scratch_shapes=list(scratch),
        input_output_aliases={count + len(after) + i: results + i for i in range(len(held))},
        compiler_params=pltpu.CompilerParams(vmem_limit_bytes=limit * 2**20),
        cost_estimate=pl.CostEstimate(flops=flops, bytes_accessed=moved, transcendentals=0),
    )(*inputs, *after, *held)


def shape_of(dims, kind=LOW):
    return jax.ShapeDtypeStruct(dims, kind)


def part(index, width):
    return pl.ds(pl.multiple_of(index * width, width), width)


def triangle(out):
    source = lax.broadcasted_iota(jnp.int32, out.shape, 0)
    target = lax.broadcasted_iota(jnp.int32, out.shape, 1)
    out[...] = jnp.where(source < target, 1.0, 0.0).astype(LOW)


def places(routes, earlier, me, rows):
    labels = lax.broadcasted_iota(jnp.int32, (rows, 1), 0) ^ me
    first = routes[0:1, :] == labels
    second = routes[1:2, :] == labels
    either = first | second
    before = matmul(jnp.where(either, 1.0, 0.0).astype(LOW), earlier)
    return jnp.where(either, before, -1.0), first, second


def table(place, k, capacity):
    slots = lax.broadcasted_iota(jnp.int32, (capacity, place.shape[1]), 0).astype(WIDE)
    return jnp.where(place[k : k + 1, :] == slots, 1.0, 0.0).astype(LOW)


def prepare(experts, tokens, routes, gain, earlier, *outs):
    far, near, own, normed_ref = outs[:-3], outs[-3], outs[-2], outs[-1]
    me = lax.axis_index("exp")
    tp = lax.axis_index("tp")
    capacity, width = own.shape
    half = width // 2
    wide = tokens[...].astype(WIDE)
    average = jnp.mean(wide, axis=-1, keepdims=True)
    centred = wide - average
    spread = jnp.mean(centred * centred, axis=-1, keepdims=True)
    normed_ref[...] = (centred * lax.rsqrt(spread + EPS) * gain[...]).astype(LOW)
    place, _, _ = places(routes[...], earlier[...], me, max(16, experts))
    normed_half = normed_ref[:, part(tp, half)]
    for k in range(experts - 1, 1, -1):
        far[k - 2][...] = matmul(table(place, k, capacity), normed_half).astype(LOW)
    normed = normed_ref[...]
    near[...] = matmul(table(place, 1, capacity), normed).astype(LOW)
    own[...] = matmul(table(place, 0, capacity), normed).astype(LOW)


def mixing(experts, routes, gates, earlier, *refs):
    count = (len(refs) - 3) // 2
    sources, (high, low), targets, arrived = refs[:count], refs[count : count + 2], refs[count + 2 : -1], refs[-1]
    loads = [
        pltpu.make_async_copy(source, target, arrived.at[i])
        for i, (source, target) in enumerate(zip(sources, targets, strict=True))
    ]
    for load in loads:
        load.start()
    me = lax.axis_index("exp")
    token_count = routes.shape[1]
    capacity = high.shape[2]
    place, first, second = places(routes[...], earlier[...], me, max(16, experts))
    gate = jnp.where(first, gates[0:1, :], 0.0) + jnp.where(second, gates[1:2, :], 0.0)
    place = place.T
    gate = gate.T
    slots = lax.broadcasted_iota(jnp.int32, (token_count, capacity), 1).astype(WIDE)
    for k in range(experts):
        weight = jnp.where(place[:, k : k + 1] == slots, gate[:, k : k + 1], 0.0)
        upper = weight.astype(LOW)
        high[k] = upper
        low[k] = (weight - upper.astype(WIDE)).astype(LOW)
    for load in loads:
        load.wait()


def expert(split, *refs):
    rows, refs = refs[: 1 + split], refs[1 + split :]
    first, second, away, kept, inner = refs
    tp = lax.axis_index("tp")
    width, hidden = first.shape
    half = width // 2
    chunk = min(512, hidden)
    for c in range(hidden // chunk):
        columns = slice(c * chunk, (c + 1) * chunk)
        if split:
            value = matmul(rows[0][...], first[part(tp, half), columns])
            value = value + matmul(rows[1][...], first[part(1 - tp, half), columns])
        else:
            value = matmul(rows[0][...], first[:, columns])
        inner[:, columns] = jnp.maximum(value, 0.0).astype(LOW)
    away[...] = matmul(inner[...], second[:, part(1 - tp, half)]).astype(LOW)
    kept[...] = matmul(inner[...], second[:, part(tp, half)])


def expert_first(rows, first, second, away, kept, first_here, second_here, inner, arrived):
    tp = lax.axis_index("tp")
    width, hidden = first.shape
    half = width // 2
    chunk = min(512, hidden)
    columns = [slice(c * chunk, (c + 1) * chunk) for c in range(hidden // chunk)]
    loads = [
        pltpu.make_async_copy(first.at[:, c], first_here.at[:, c], arrived.at[i])
        for i, c in enumerate(columns)
    ]
    loads.append(pltpu.make_async_copy(second, second_here, arrived.at[len(columns)]))
    for load in loads:
        load.start()
    for c, load in zip(columns, loads):
        load.wait()
        inner[:, c] = jnp.maximum(matmul(rows[...], first_here[:, c]), 0.0).astype(LOW)
    loads[-1].wait()
    away[...] = matmul(inner[...], second_here[:, part(1 - tp, half)]).astype(LOW)
    kept[...] = matmul(inner[...], second_here[:, part(tp, half)])


def idle():
    pass


def combine(experts, tokens, high, low, *refs):
    returned, out = refs[:-1], refs[-1]
    tp = lax.axis_index("tp")
    half = out.shape[1]
    mixed = tokens[:, part(tp, half)].astype(WIDE)
    for k in range(experts):
        rows = returned[k][...]
        mixed = mixed + (matmul(high[k], rows) + matmul(low[k], rows))
    out[...] = mixed.astype(LOW)


def project(mine, other, gain, weight, out):
    tp = lax.axis_index("tp")
    half = mine.shape[1]
    own = mine[...].astype(WIDE)
    rest = other[...].astype(WIDE)
    average = (
        jnp.sum(own, axis=-1, keepdims=True) + jnp.sum(rest, axis=-1, keepdims=True)
    ) / (2 * half)
    own = own - average
    rest = rest - average
    spread = (
        jnp.sum(own * own, axis=-1, keepdims=True) + jnp.sum(rest * rest, axis=-1, keepdims=True)
    ) / (2 * half)
    factor = lax.rsqrt(spread + EPS)
    own = (own * factor * gain[:, part(tp, half)]).astype(LOW)
    rest = (rest * factor * gain[:, part(1 - tp, half)]).astype(LOW)
    value = matmul(own, weight[part(tp, half), :]) + matmul(rest, weight[part(1 - tp, half), :])
    out[...] = value.astype(LOW)


def attend(
    mine, other, queries, upstream, key_w, value_w, hidden, context, away, kept, keys, values, dkeys, dvalues
):
    tp = lax.axis_index("tp")
    sec = lax.axis_index("sec")
    token_count, half = mine.shape
    width = 2 * half
    scale = 1.0 / math.sqrt(HD)

    @pl.when(sec != 0)
    def _():
        for weight, target in ((key_w, keys), (value_w, values)):
            value = matmul(mine[...], weight[part(tp, half), :])
            value = value + matmul(other[...], weight[part(1 - tp, half), :])
            target[...] = value.astype(LOW)
        heads = [
            (slice(s * SEQ, (s + 1) * SEQ), slice(h * HD, (h + 1) * HD))
            for s in range(token_count // SEQ)
            for h in range(queries.shape[1] // HD)
        ]
        scores = [matmul(keys[at], queries[at], NT) for at in heads]
        dprobs = [matmul(values[at], upstream[at], NT) for at in heads]
        powers = [jnp.exp(x * scale) for x in scores]
        probs = [x * (1.0 / jnp.sum(x, axis=0, keepdims=True)) for x in powers]
        lows = [x.astype(LOW) for x in probs]
        for at, low in zip(heads, lows):
            dvalues[at] = matmul(low, upstream[at]).astype(LOW)
        rowdots = [jnp.sum(x * y, axis=0, keepdims=True) for x, y in zip(dprobs, probs)]
        dscores = [
            (y * (x - z)).astype(LOW) for x, y, z in zip(dprobs, probs, rowdots)
        ]
        for at, dscore in zip(heads, dscores):
            dkeys[at] = (matmul(dscore, queries[at]) * scale).astype(LOW)
        for at, low in zip(heads, lows):
            context[at] = matmul(low, values[at], TN).astype(LOW)
        side = sec % 2
        pairs = lax.axis_size("sec") // 2
        block = width // (2 * pairs)
        for target, parity in ((away, 1 - side), (kept, side)):
            for i in range(pairs):
                rows = part(2 * i + parity, block)
                value = matmul(dkeys[...], key_w[rows, :], NT)
                value = value + matmul(dvalues[...], value_w[rows, :], NT)
                target[:, i * block : (i + 1) * block] = value.astype(target.dtype)

    @pl.when(sec == 0)
    def _():
        context[...] = hidden[...]
        away[...] = jnp.zeros_like(away)
        kept[...] = jnp.zeros_like(kept)


def gather_term(kept, arrived, own, *sent):
    tp = lax.axis_index("tp")
    here = lax.axis_index("sec") // 2 * lax.axis_size("tp") + tp
    width = own.shape[1]
    for k in range(len(sent) + 1):
        columns = part(here ^ k, width)
        value = kept[:, columns] + arrived[:, columns].astype(WIDE)
        if k == 0:
            own[...] = value
        else:
            sent[k - 1][...] = value.astype(LOW)


def swap(block, axis, step):
    size = lax.axis_size(axis)
    return lax.ppermute(block, axis, [(i, i ^ step) for i in range(size)])


def shards(
    tokens,
    routes,
    gate_weights,
    moe_gain,
    attn_gain,
    expert_in,
    expert_out,
    query_weight,
    key_weight,
    value_weight,
    cotangent,
):
    token_rows = tokens[0]
    route_rows = routes[0].T
    gate_rows = gate_weights[0].T
    token_count, model_width = token_rows.shape
    experts = lax.axis_size("exp")
    sections = lax.axis_size("sec")
    tp_size = lax.axis_size("tp")
    sec = lax.axis_index("sec")
    half = model_width // tp_size
    capacity = 3 * token_count // experts
    weight_first = expert_in[0, 0]
    weight_second = expert_out[0, 0]
    units = weight_first.shape[1]

    middle = max(2, experts // 2 + 1)
    groups = [list(range(middle - 1, 1, -1)), list(range(experts - 1, middle - 1, -1))]
    row_half, row_whole = shape_of((capacity, half)), shape_of((capacity, model_width))
    earlier = call(
        triangle,
        [shape_of((token_count, token_count))],
        [],
        flops=20 * token_count * token_count * model_width,
    )[0]
    *far_rows, near_rows, own_rows = call(
        functools.partial(prepare, experts),
        [row_half] * (experts - 2) + [row_whole] * 2,
        [token_rows, route_rows, moe_gain, earlier],
        [pltpu.VMEM((token_count, model_width), LOW)],
        flops=2 * 3 * token_count * token_count * model_width,
    )
    def hold(array, after):
        return call(idle, [], [], after=after, held=[array])[0]

    def joined(group):
        blocks = [swap(far_rows[k - 2], "exp", k) for k in group]
        return blocks[0] if len(blocks) == 1 else jnp.concatenate(blocks, axis=0)

    def total(away, kept):
        return (kept + swap(away, "tp", 1).astype(WIDE)).astype(LOW)

    def through(rows, after):
        count = rows[0].shape[0]
        return call(
            functools.partial(expert, len(rows) - 1),
            [shape_of((count, half)), shape_of((count, half), WIDE)],
            [*rows, weight_first, weight_second],
            [pltpu.VMEM((count, units), LOW)],
            flops=4 * count * model_width * units,
            limit=24,
            after=after,
        )

    arriving = [joined(groups[0])]
    later = [far_rows[k - 2] for k in groups[1]] + [near_rows]
    loads = max(1, units // 512) + 1
    own_away, own_kept, weight_first, weight_second, *later = call(
        expert_first,
        [
            row_half,
            shape_of((capacity, half), WIDE),
            shape_of(weight_first.shape),
            shape_of(weight_second.shape),
        ],
        [own_rows, weight_first, weight_second],
        [pltpu.VMEM((capacity, units), LOW), pltpu.SemaphoreType.DMA((loads,))],
        flops=4 * capacity * model_width * units,
        remote=(1, 2),
        limit=44,
        held=later,
    )
    for k, rows in zip(groups[1], later):
        far_rows[k - 2] = rows
    arriving.append(joined(groups[1]))
    near = swap(later[-1], "exp", 1)
    returned = {0: total(own_away, own_kept)}
    arriving[0] = hold(arriving[0], [own_away])
    others = [swap(arriving[0], "tp", 1)]
    sources = [query_weight[0], key_weight[0], value_weight[0], cotangent[0]]
    high, low, query_w, key_w, value_w, upstream = call(
        functools.partial(mixing, experts),
        [shape_of((experts, token_count, capacity))] * 2 + [shape_of(x.shape) for x in sources],
        [route_rows, gate_rows, earlier, *sources],
        [pltpu.SemaphoreType.DMA((len(sources),))],
        remote=(3, 4, 5, 6),
        limit=40,
        after=[arriving[0]],
    )
    others.append(swap(arriving[1], "tp", 1))

    def give_back(group, away, kept):
        mixed = total(away, kept)
        for i, k in enumerate(group):
            block = mixed if len(group) == 1 else mixed[i * capacity : (i + 1) * capacity]
            returned[k] = swap(block, "exp", k)
        return mixed

    away, kept = through([arriving[0], others[0]], [returned[0], high])
    near_away, near_kept = through([near], [away])
    mixed = give_back(groups[0], away, kept)
    returned[1] = swap(total(near_away, near_kept), "exp", 1)
    away, kept = through([arriving[1], others[1]], [near_away, mixed])
    give_back(groups[1], away, kept)

    hidden_half = call(
        functools.partial(combine, experts),
        [shape_of((token_count, half))],
        [token_rows, high, low, *(returned[k] for k in range(experts))],
        flops=4 * 3 * token_count * token_count * half,
    )[0]

    beside = swap(hidden_half, "sec", 1)
    hidden_other = swap(hidden_half, "tp", 1)
    encoder_half = jnp.where(sec == 1, beside, hidden_half)
    first = jnp.where(sec == 0, hidden_other, hidden_half)
    for i in range(1, sections // 2):
        pairs = [(t, 2 * i * tp_size + t) for t in range(tp_size)]
        pairs += [(tp_size + t, (2 * i + 1) * tp_size + (t ^ 1)) for t in range(tp_size)]
        moved = lax.ppermute(encoder_half, ("sec", "tp"), pairs)
        first = jnp.where(sec // 2 == i, moved, first)
    second = swap(first, "sec", 1)
    mine = jnp.where(sec == 1, beside, jnp.where(sec % 2 == 0, first, second))
    other = jnp.where((sec % 2 == 0) | (sec == 1), second, first)

    local_width = query_weight.shape[2]
    queries = call(
        project,
        [shape_of((token_count, local_width))],
        [hidden_half, hidden_other, attn_gain, query_w],
        flops=2 * token_count * model_width * local_width,
    )[0]
    context, away, kept = call(
        attend,
        [
            shape_of((token_count, local_width)),
            shape_of((token_count, model_width // 2)),
            shape_of((token_count, model_width // 2), WIDE),
        ],
        [mine, other, queries, upstream, key_w, value_w, hidden_half],
        [pltpu.VMEM((token_count, local_width), LOW)] * 4,
        flops=10 * token_count * model_width * local_width,
    )

    own = model_width // (sections * tp_size)
    count = sections // 2 * tp_size
    both = sections * tp_size
    blocks = call(
        gather_term,
        [shape_of((token_count, own), WIDE)] + [shape_of((token_count, own))] * (count - 1),
        [kept, swap(away, "sec", 1)],
    )
    total = blocks[0]
    for k in range(1, count):
        pairs = []
        for i in range(both):
            section, t = i // tp_size, i % tp_size
            target = (section // 2 * tp_size + t) ^ k
            pairs.append((i, (target // tp_size * 2 + section % 2) * tp_size + target % tp_size))
        total = total + lax.ppermute(blocks[k], ("sec", "tp"), pairs).astype(WIDE)
    return (context[None], total.astype(LOW))


def solution(mesh):
    placed = (
        P("sec", "exp", None),
        P("sec", "exp", None),
        P("sec", "exp", None),
        P("sec", None),
        P("sec", None),
        P("sec", "exp", None, "tp"),
        P("sec", "exp", "tp", None),
        P("sec", None, "tp"),
        P("sec", None, "tp"),
        P("sec", None, "tp"),
        P("sec", "exp", "tp"),
    )
    return jax.shard_map(
        shards,
        mesh=mesh,
        in_specs=placed,
        out_specs=(P("sec", "exp", "tp"), P("exp", ("sec", "tp"))),
        check_vma=False,
    )
```

```python
import functools
import math

import jax
import jax.numpy as jnp
from jax import lax
from jax.experimental import pallas as pl
from jax.experimental.pallas import tpu as pltpu
from jax.sharding import PartitionSpec as P

HD = 128
SEQ = 128
EPS = 1e-05

LOW = jnp.bfloat16
WIDE = jnp.float32
VMEM = pl.BlockSpec(memory_space=pltpu.VMEM)
HBM = pl.BlockSpec(memory_space=pltpu.HBM)
ANY = pl.BlockSpec(memory_space=pl.ANY)
NT = (((1,), (1,)), ((), ()))
TN = (((0,), (0,)), ((), ()))


def matmul(a, b, dims=(((1,), (0,)), ((), ()))):
    return lax.dot_general(a, b, dims, preferred_element_type=WIDE)


def call(body, out_shape, inputs, scratch=(), flops=0, limit=16, remote=(), after=(), held=()):
    def size(x):
        return math.prod(x.shape) * jnp.dtype(x.dtype).itemsize

    count, results = len(inputs), len(out_shape)
    extra = len(after) + len(held)

    def run(*refs):
        outs = refs[count + extra : count + extra + results]
        return body(*refs[:count], *outs, *refs[count + extra + results + len(held) :])

    moved = sum(size(x) for x in inputs) + sum(size(x) for x in out_shape)
    return pl.pallas_call(
        run,
        out_shape=[*out_shape, *(shape_of(x.shape, x.dtype) for x in held)],
        in_specs=[HBM if i in remote else VMEM for i in range(count)] + [ANY] * extra,
        out_specs=[VMEM] * results + [ANY] * len(held),
        scratch_shapes=list(scratch),
        input_output_aliases={count + len(after) + i: results + i for i in range(len(held))},
        compiler_params=pltpu.CompilerParams(vmem_limit_bytes=limit * 2**20),
        cost_estimate=pl.CostEstimate(flops=flops, bytes_accessed=moved, transcendentals=0),
    )(*inputs, *after, *held)


def shape_of(dims, kind=LOW):
    return jax.ShapeDtypeStruct(dims, kind)


def part(index, width):
    return pl.ds(pl.multiple_of(index * width, width), width)


def triangle(out):
    source = lax.broadcasted_iota(jnp.int32, out.shape, 0)
    target = lax.broadcasted_iota(jnp.int32, out.shape, 1)
    out[...] = jnp.where(source < target, 1.0, 0.0).astype(LOW)


def places(routes, earlier, me, rows):
    labels = lax.broadcasted_iota(jnp.int32, (rows, 1), 0) ^ me
    first = routes[0:1, :] == labels
    second = routes[1:2, :] == labels
    either = first | second
    before = matmul(jnp.where(either, 1.0, 0.0).astype(LOW), earlier)
    return jnp.where(either, before, -1.0), first, second


def table(place, k, capacity):
    slots = lax.broadcasted_iota(jnp.int32, (capacity, place.shape[1]), 0).astype(WIDE)
    return jnp.where(place[k : k + 1, :] == slots, 1.0, 0.0).astype(LOW)


def prepare(experts, tokens, routes, gain, earlier, *outs):
    far, near, own, normed_ref = outs[:-3], outs[-3], outs[-2], outs[-1]
    me = lax.axis_index("exp")
    tp = lax.axis_index("tp")
    capacity, width = own.shape
    half = width // 2
    wide = tokens[...].astype(WIDE)
    average = jnp.mean(wide, axis=-1, keepdims=True)
    centred = wide - average
    spread = jnp.mean(centred * centred, axis=-1, keepdims=True)
    normed_ref[...] = (centred * lax.rsqrt(spread + EPS) * gain[...]).astype(LOW)
    place, _, _ = places(routes[...], earlier[...], me, max(16, experts))
    normed_half = normed_ref[:, part(tp, half)]
    for k in range(experts - 1, 1, -1):
        far[k - 2][...] = matmul(table(place, k, capacity), normed_half).astype(LOW)
    normed = normed_ref[...]
    near[...] = matmul(table(place, 1, capacity), normed).astype(LOW)
    own[...] = matmul(table(place, 0, capacity), normed).astype(LOW)


def mixing(experts, routes, gates, earlier, high, low):
    me = lax.axis_index("exp")
    token_count = routes.shape[1]
    capacity = high.shape[2]
    place, first, second = places(routes[...], earlier[...], me, max(16, experts))
    gate = jnp.where(first, gates[0:1, :], 0.0) + jnp.where(second, gates[1:2, :], 0.0)
    place = place.T
    gate = gate.T
    slots = lax.broadcasted_iota(jnp.int32, (token_count, capacity), 1).astype(WIDE)
    for k in range(experts):
        weight = jnp.where(place[:, k : k + 1] == slots, gate[:, k : k + 1], 0.0)
        upper = weight.astype(LOW)
        high[k] = upper
        low[k] = (weight - upper.astype(WIDE)).astype(LOW)


def expert(split, *refs):
    rows, refs = refs[: 1 + split], refs[1 + split :]
    first, second, away, kept, inner = refs
    tp = lax.axis_index("tp")
    width, hidden = first.shape
    half = width // 2
    chunk = min(512, hidden)
    for c in range(hidden // chunk):
        columns = slice(c * chunk, (c + 1) * chunk)
        if split:
            value = matmul(rows[0][...], first[part(tp, half), columns])
            value = value + matmul(rows[1][...], first[part(1 - tp, half), columns])
        else:
            value = matmul(rows[0][...], first[:, columns])
        inner[:, columns] = jnp.maximum(value, 0.0).astype(LOW)
    away[...] = matmul(inner[...], second[:, part(1 - tp, half)]).astype(LOW)
    kept[...] = matmul(inner[...], second[:, part(tp, half)])


def expert_first(rows, first, second, away, kept, first_here, second_here, inner, arrived):
    tp = lax.axis_index("tp")
    width, hidden = first.shape
    half = width // 2
    chunk = min(512, hidden)
    columns = [slice(c * chunk, (c + 1) * chunk) for c in range(hidden // chunk)]
    loads = [
        pltpu.make_async_copy(first.at[:, c], first_here.at[:, c], arrived.at[i])
        for i, c in enumerate(columns)
    ]
    loads.append(pltpu.make_async_copy(second, second_here, arrived.at[len(columns)]))
    for load in loads:
        load.start()
    for c, load in zip(columns, loads):
        load.wait()
        inner[:, c] = jnp.maximum(matmul(rows[...], first_here[:, c]), 0.0).astype(LOW)
    loads[-1].wait()
    away[...] = matmul(inner[...], second_here[:, part(1 - tp, half)]).astype(LOW)
    kept[...] = matmul(inner[...], second_here[:, part(tp, half)])


def idle():
    pass


def combine(experts, tokens, high, low, *refs):
    returned, out = refs[:-1], refs[-1]
    tp = lax.axis_index("tp")
    half = out.shape[1]
    mixed = tokens[:, part(tp, half)].astype(WIDE)
    for k in range(experts):
        rows = returned[k][...]
        mixed = mixed + (matmul(high[k], rows) + matmul(low[k], rows))
    out[...] = mixed.astype(LOW)


def project(mine, other, gain, weight, *refs):
    count = (len(refs) - 2) // 2
    sources, out, targets, arrived = refs[:count], refs[count], refs[count + 1 : -1], refs[-1]
    loads = [
        pltpu.make_async_copy(source, target, arrived.at[i])
        for i, (source, target) in enumerate(zip(sources, targets, strict=True))
    ]
    for load in loads:
        load.start()
    tp = lax.axis_index("tp")
    half = mine.shape[1]
    own = mine[...].astype(WIDE)
    rest = other[...].astype(WIDE)
    average = (
        jnp.sum(own, axis=-1, keepdims=True) + jnp.sum(rest, axis=-1, keepdims=True)
    ) / (2 * half)
    own = own - average
    rest = rest - average
    spread = (
        jnp.sum(own * own, axis=-1, keepdims=True) + jnp.sum(rest * rest, axis=-1, keepdims=True)
    ) / (2 * half)
    factor = lax.rsqrt(spread + EPS)
    own = (own * factor * gain[:, part(tp, half)]).astype(LOW)
    rest = (rest * factor * gain[:, part(1 - tp, half)]).astype(LOW)
    value = matmul(own, weight[part(tp, half), :]) + matmul(rest, weight[part(1 - tp, half), :])
    out[...] = value.astype(LOW)
    for load in loads:
        load.wait()


def choose(own, moved, out):
    sec = lax.axis_index("sec")

    @pl.when(sec < 2)
    def _():
        out[...] = own[...]

    @pl.when(sec >= 2)
    def _():
        out[...] = moved[...]


def attend(
    first, second, beside, queries, upstream, key_w, value_w, hidden, context, away, kept, keys, values, dkeys, dvalues
):
    tp = lax.axis_index("tp")
    sec = lax.axis_index("sec")
    token_count, half = first.shape
    width = 2 * half
    scale = 1.0 / math.sqrt(HD)

    @pl.when(sec != 0)
    def _():
        even = sec % 2 == 0
        mine = jnp.where(sec == 1, beside[...], jnp.where(even, first[...], second[...]))
        other = jnp.where(even | (sec == 1), second[...], first[...])
        for weight, target in ((key_w, keys), (value_w, values)):
            value = matmul(mine, weight[part(tp, half), :])
            value = value + matmul(other, weight[part(1 - tp, half), :])
            target[...] = value.astype(LOW)
        heads = [
            (slice(s * SEQ, (s + 1) * SEQ), slice(h * HD, (h + 1) * HD))
            for s in range(token_count // SEQ)
            for h in range(queries.shape[1] // HD)
        ]
        scores = [matmul(keys[at], queries[at], NT) for at in heads]
        dprobs = [matmul(values[at], upstream[at], NT) for at in heads]
        powers = [jnp.exp(x * scale) for x in scores]
        probs = [x * (1.0 / jnp.sum(x, axis=0, keepdims=True)) for x in powers]
        lows = [x.astype(LOW) for x in probs]
        for at, low in zip(heads, lows):
            dvalues[at] = matmul(low, upstream[at]).astype(LOW)
        rowdots = [jnp.sum(x * y, axis=0, keepdims=True) for x, y in zip(dprobs, probs)]
        dscores = [
            (y * (x - z)).astype(LOW) for x, y, z in zip(dprobs, probs, rowdots)
        ]
        for at, dscore in zip(heads, dscores):
            dkeys[at] = (matmul(dscore, queries[at]) * scale).astype(LOW)
        for at, low in zip(heads, lows):
            context[at] = matmul(low, values[at], TN).astype(LOW)
        side = sec % 2
        pairs = lax.axis_size("sec") // 2
        block = width // (2 * pairs)
        for target, parity in ((away, 1 - side), (kept, side)):
            for i in range(pairs):
                rows = part(2 * i + parity, block)
                value = matmul(dkeys[...], key_w[rows, :], NT)
                value = value + matmul(dvalues[...], value_w[rows, :], NT)
                target[:, i * block : (i + 1) * block] = value.astype(target.dtype)

    @pl.when(sec == 0)
    def _():
        context[...] = hidden[...]
        away[...] = jnp.zeros_like(away)
        kept[...] = jnp.zeros_like(kept)


def gather_term(kept, arrived, own, *sent):
    tp = lax.axis_index("tp")
    here = lax.axis_index("sec") // 2 * lax.axis_size("tp") + tp
    width = own.shape[1]
    for k in range(len(sent) + 1):
        columns = part(here ^ k, width)
        value = kept[:, columns] + arrived[:, columns].astype(WIDE)
        if k == 0:
            own[...] = value
        else:
            sent[k - 1][...] = value.astype(LOW)


def swap(block, axis, step):
    size = lax.axis_size(axis)
    return lax.ppermute(block, axis, [(i, i ^ step) for i in range(size)])


def shards(
    tokens,
    routes,
    gate_weights,
    moe_gain,
    attn_gain,
    expert_in,
    expert_out,
    query_weight,
    key_weight,
    value_weight,
    cotangent,
):
    token_rows = tokens[0]
    route_rows = routes[0].T
    gate_rows = gate_weights[0].T
    token_count, model_width = token_rows.shape
    experts = lax.axis_size("exp")
    sections = lax.axis_size("sec")
    tp_size = lax.axis_size("tp")
    sec = lax.axis_index("sec")
    half = model_width // tp_size
    capacity = 3 * token_count // experts
    weight_first = expert_in[0, 0]
    weight_second = expert_out[0, 0]
    units = weight_first.shape[1]

    middle = max(2, experts // 2 + 1)
    groups = [list(range(middle - 1, 1, -1)), list(range(experts - 1, middle - 1, -1))]
    row_half, row_whole = shape_of((capacity, half)), shape_of((capacity, model_width))
    earlier = call(
        triangle,
        [shape_of((token_count, token_count))],
        [],
        flops=20 * token_count * token_count * model_width,
    )[0]
    *far_rows, near_rows, own_rows = call(
        functools.partial(prepare, experts),
        [row_half] * (experts - 2) + [row_whole] * 2,
        [token_rows, route_rows, moe_gain, earlier],
        [pltpu.VMEM((token_count, model_width), LOW)],
        flops=2 * 3 * token_count * token_count * model_width,
    )
    def hold(array, after):
        return call(idle, [], [], after=after, held=[array])[0]

    def joined(group):
        blocks = [swap(far_rows[k - 2], "exp", k) for k in group]
        return blocks[0] if len(blocks) == 1 else jnp.concatenate(blocks, axis=0)

    def total(away, kept):
        return (kept + swap(away, "tp", 1).astype(WIDE)).astype(LOW)

    def through(rows, after):
        count = rows[0].shape[0]
        return call(
            functools.partial(expert, len(rows) - 1),
            [shape_of((count, half)), shape_of((count, half), WIDE)],
            [*rows, weight_first, weight_second],
            [pltpu.VMEM((count, units), LOW)],
            flops=4 * count * model_width * units,
            limit=24,
            after=after,
        )

    arriving = [joined(groups[0])]
    later = [far_rows[k - 2] for k in groups[1]] + [near_rows]
    loads = max(1, units // 512) + 1
    own_away, own_kept, weight_first, weight_second, *later = call(
        expert_first,
        [
            row_half,
            shape_of((capacity, half), WIDE),
            shape_of(weight_first.shape),
            shape_of(weight_second.shape),
        ],
        [own_rows, weight_first, weight_second],
        [pltpu.VMEM((capacity, units), LOW), pltpu.SemaphoreType.DMA((loads,))],
        flops=4 * capacity * model_width * units,
        remote=(1, 2),
        limit=44,
        held=later,
    )
    for k, rows in zip(groups[1], later):
        far_rows[k - 2] = rows
    arriving.append(joined(groups[1]))
    near = swap(later[-1], "exp", 1)
    returned = {0: total(own_away, own_kept)}
    arriving[0] = hold(arriving[0], [own_away])
    others = [swap(arriving[0], "tp", 1)]
    high, low = call(
        functools.partial(mixing, experts),
        [shape_of((experts, token_count, capacity))] * 2,
        [route_rows, gate_rows, earlier],
        after=[arriving[0]],
    )
    others.append(swap(arriving[1], "tp", 1))

    def give_back(group, away, kept):
        mixed = total(away, kept)
        for i, k in enumerate(group):
            block = mixed if len(group) == 1 else mixed[i * capacity : (i + 1) * capacity]
            returned[k] = swap(block, "exp", k)
        return mixed

    away, kept = through([arriving[0], others[0]], [returned[0], high])
    near_away, near_kept = through([near], [away])
    mixed = give_back(groups[0], away, kept)
    returned[1] = swap(total(near_away, near_kept), "exp", 1)
    away, kept = through([arriving[1], others[1]], [near_away, mixed])
    give_back(groups[1], away, kept)

    hidden_half = call(
        functools.partial(combine, experts),
        [shape_of((token_count, half))],
        [token_rows, high, low, *(returned[k] for k in range(experts))],
        flops=4 * 3 * token_count * token_count * half,
    )[0]

    beside = swap(hidden_half, "sec", 1)
    hidden_other = swap(hidden_half, "tp", 1)
    encoder_half = jnp.where(sec == 1, beside, hidden_half)
    moved = hidden_half
    for i in range(1, sections // 2):
        targets = {j: j for j in range(sections * tp_size)}
        for t in range(tp_size):
            even, odd = 2 * i * tp_size + t, (2 * i + 1) * tp_size + (t ^ 1)
            targets |= {t: even, even: t, tp_size + t: odd, odd: tp_size + t}
        arrived = lax.ppermute(encoder_half, ("sec", "tp"), list(targets.items()))
        moved = arrived if sections == 4 else jnp.where(sec // 2 == i, arrived, moved)
    first = call(choose, [shape_of(hidden_half.shape)], [hidden_other, moved])[0]
    second = swap(first, "sec", 1)

    local_width = query_weight.shape[2]
    sources = [key_weight[0], value_weight[0], cotangent[0]]
    queries, key_w, value_w, upstream = call(
        project,
        [shape_of((token_count, local_width))] + [shape_of(x.shape) for x in sources],
        [hidden_half, hidden_other, attn_gain, query_weight[0], *sources],
        [pltpu.SemaphoreType.DMA((len(sources),))],
        flops=2 * token_count * model_width * local_width,
        remote=(4, 5, 6),
    )
    context, away, kept = call(
        attend,
        [
            shape_of((token_count, local_width)),
            shape_of((token_count, model_width // 2)),
            shape_of((token_count, model_width // 2), WIDE),
        ],
        [first, second, beside, queries, upstream, key_w, value_w, hidden_half],
        [pltpu.VMEM((token_count, local_width), LOW)] * 4,
        flops=10 * token_count * model_width * local_width,
    )

    own = model_width // (sections * tp_size)
    count = sections // 2 * tp_size
    both = sections * tp_size
    blocks = call(
        gather_term,
        [shape_of((token_count, own), WIDE)] + [shape_of((token_count, own))] * (count - 1),
        [kept, swap(away, "sec", 1)],
    )
    total = blocks[0]
    for k in range(1, count):
        pairs = []
        for i in range(both):
            section, t = i // tp_size, i % tp_size
            target = (section // 2 * tp_size + t) ^ k
            pairs.append((i, (target // tp_size * 2 + section % 2) * tp_size + target % tp_size))
        total = total + lax.ppermute(blocks[k], ("sec", "tp"), pairs).astype(WIDE)
    return (context[None], total.astype(LOW))


def solution(mesh):
    placed = (
        P("sec", "exp", None),
        P("sec", "exp", None),
        P("sec", "exp", None),
        P("sec", None),
        P("sec", None),
        P("sec", "exp", None, "tp"),
        P("sec", "exp", "tp", None),
        P("sec", None, "tp"),
        P("sec", None, "tp"),
        P("sec", None, "tp"),
        P("sec", "exp", "tp"),
    )
    return jax.shard_map(
        shards,
        mesh=mesh,
        in_specs=placed,
        out_specs=(P("sec", "exp", "tp"), P("exp", ("sec", "tp"))),
        check_vma=False,
    )
```

```python
import functools
import math

import jax
import jax.numpy as jnp
from jax import lax
from jax.experimental import pallas as pl
from jax.experimental.pallas import tpu as pltpu
from jax.sharding import PartitionSpec as P

HD = 128
SEQ = 128
EPS = 1e-05

LOW = jnp.bfloat16
WIDE = jnp.float32
VMEM = pl.BlockSpec(memory_space=pltpu.VMEM)
HBM = pl.BlockSpec(memory_space=pltpu.HBM)
ANY = pl.BlockSpec(memory_space=pl.ANY)
NT = (((1,), (1,)), ((), ()))
TN = (((0,), (0,)), ((), ()))


def matmul(a, b, dims=(((1,), (0,)), ((), ()))):
    return lax.dot_general(a, b, dims, preferred_element_type=WIDE)


def call(body, out_shape, inputs, scratch=(), flops=0, limit=16, remote=(), after=(), held=()):
    def size(x):
        return math.prod(x.shape) * jnp.dtype(x.dtype).itemsize

    count, results = len(inputs), len(out_shape)
    extra = len(after) + len(held)

    def run(*refs):
        outs = refs[count + extra : count + extra + results]
        return body(*refs[:count], *outs, *refs[count + extra + results + len(held) :])

    moved = sum(size(x) for x in inputs) + sum(size(x) for x in out_shape)
    return pl.pallas_call(
        run,
        out_shape=[*out_shape, *(shape_of(x.shape, x.dtype) for x in held)],
        in_specs=[HBM if i in remote else VMEM for i in range(count)] + [ANY] * extra,
        out_specs=[VMEM] * results + [ANY] * len(held),
        scratch_shapes=list(scratch),
        input_output_aliases={count + len(after) + i: results + i for i in range(len(held))},
        compiler_params=pltpu.CompilerParams(vmem_limit_bytes=limit * 2**20),
        cost_estimate=pl.CostEstimate(flops=flops, bytes_accessed=moved, transcendentals=0),
    )(*inputs, *after, *held)


def shape_of(dims, kind=LOW):
    return jax.ShapeDtypeStruct(dims, kind)


def part(index, width):
    return pl.ds(pl.multiple_of(index * width, width), width)


def triangle(out):
    source = lax.broadcasted_iota(jnp.int32, out.shape, 0)
    target = lax.broadcasted_iota(jnp.int32, out.shape, 1)
    out[...] = jnp.where(source < target, 1.0, 0.0).astype(LOW)


def places(routes, earlier, me, rows):
    labels = lax.broadcasted_iota(jnp.int32, (rows, 1), 0) ^ me
    first = routes[0:1, :] == labels
    second = routes[1:2, :] == labels
    either = first | second
    before = matmul(jnp.where(either, 1.0, 0.0).astype(LOW), earlier)
    return jnp.where(either, before, -1.0), first, second


def table(place, k, capacity):
    slots = lax.broadcasted_iota(jnp.int32, (capacity, place.shape[1]), 0).astype(WIDE)
    return jnp.where(place[k : k + 1, :] == slots, 1.0, 0.0).astype(LOW)


def prepare(experts, tokens, routes, gain, earlier, *outs):
    far, near, own, normed_ref = outs[:-3], outs[-3], outs[-2], outs[-1]
    me = lax.axis_index("exp")
    tp = lax.axis_index("tp")
    capacity, width = own.shape
    half = width // 2
    wide = tokens[...].astype(WIDE)
    average = jnp.mean(wide, axis=-1, keepdims=True)
    centred = wide - average
    spread = jnp.mean(centred * centred, axis=-1, keepdims=True)
    normed_ref[...] = (centred * lax.rsqrt(spread + EPS) * gain[...]).astype(LOW)
    place, _, _ = places(routes[...], earlier[...], me, max(16, experts))
    normed_half = normed_ref[:, part(tp, half)]
    for k in range(experts - 1, 1, -1):
        far[k - 2][...] = matmul(table(place, k, capacity), normed_half).astype(LOW)
    normed = normed_ref[...]
    near[...] = matmul(table(place, 1, capacity), normed).astype(LOW)
    own[...] = matmul(table(place, 0, capacity), normed).astype(LOW)


def mixing(experts, routes, gates, earlier, upstream, high, low, upstream_here, arrived):
    load = pltpu.make_async_copy(upstream, upstream_here, arrived)
    load.start()
    me = lax.axis_index("exp")
    token_count = routes.shape[1]
    capacity = high.shape[2]
    place, first, second = places(routes[...], earlier[...], me, max(16, experts))
    gate = jnp.where(first, gates[0:1, :], 0.0) + jnp.where(second, gates[1:2, :], 0.0)
    place = place.T
    gate = gate.T
    slots = lax.broadcasted_iota(jnp.int32, (token_count, capacity), 1).astype(WIDE)
    for k in range(experts):
        weight = jnp.where(place[:, k : k + 1] == slots, gate[:, k : k + 1], 0.0)
        upper = weight.astype(LOW)
        high[k] = upper
        low[k] = (weight - upper.astype(WIDE)).astype(LOW)
    load.wait()


def expert(split, *refs):
    rows, refs = refs[: 1 + split], refs[1 + split :]
    first, second, away, kept, inner = refs
    tp = lax.axis_index("tp")
    width, hidden = first.shape
    half = width // 2
    chunk = min(512, hidden)
    for c in range(hidden // chunk):
        columns = slice(c * chunk, (c + 1) * chunk)
        if split:
            value = matmul(rows[0][...], first[part(tp, half), columns])
            value = value + matmul(rows[1][...], first[part(1 - tp, half), columns])
        else:
            value = matmul(rows[0][...], first[:, columns])
        inner[:, columns] = jnp.maximum(value, 0.0).astype(LOW)
    away[...] = matmul(inner[...], second[:, part(1 - tp, half)]).astype(LOW)
    kept[...] = matmul(inner[...], second[:, part(tp, half)])


def expert_first(rows, first, second, away, kept, first_here, second_here, inner, arrived):
    tp = lax.axis_index("tp")
    width, hidden = first.shape
    half = width // 2
    chunk = min(512, hidden)
    columns = [slice(c * chunk, (c + 1) * chunk) for c in range(hidden // chunk)]
    loads = [
        pltpu.make_async_copy(first.at[:, c], first_here.at[:, c], arrived.at[i])
        for i, c in enumerate(columns)
    ]
    loads.append(pltpu.make_async_copy(second, second_here, arrived.at[len(columns)]))
    for load in loads:
        load.start()
    for c, load in zip(columns, loads):
        load.wait()
        inner[:, c] = jnp.maximum(matmul(rows[...], first_here[:, c]), 0.0).astype(LOW)
    loads[-1].wait()
    away[...] = matmul(inner[...], second_here[:, part(1 - tp, half)]).astype(LOW)
    kept[...] = matmul(inner[...], second_here[:, part(tp, half)])


def idle():
    pass


def combine(experts, tokens, high, low, *refs):
    returned, out = refs[:-1], refs[-1]
    tp = lax.axis_index("tp")
    half = out.shape[1]
    mixed = tokens[:, part(tp, half)].astype(WIDE)
    for k in range(experts):
        rows = returned[k][...]
        mixed = mixed + (matmul(high[k], rows) + matmul(low[k], rows))
    out[...] = mixed.astype(LOW)


def project(mine, other, gain, weight, out):
    tp = lax.axis_index("tp")
    half = mine.shape[1]
    own = mine[...].astype(WIDE)
    rest = other[...].astype(WIDE)
    average = (
        jnp.sum(own, axis=-1, keepdims=True) + jnp.sum(rest, axis=-1, keepdims=True)
    ) / (2 * half)
    own = own - average
    rest = rest - average
    spread = (
        jnp.sum(own * own, axis=-1, keepdims=True) + jnp.sum(rest * rest, axis=-1, keepdims=True)
    ) / (2 * half)
    factor = lax.rsqrt(spread + EPS)
    own = (own * factor * gain[:, part(tp, half)]).astype(LOW)
    rest = (rest * factor * gain[:, part(1 - tp, half)]).astype(LOW)
    value = matmul(own, weight[part(tp, half), :]) + matmul(rest, weight[part(1 - tp, half), :])
    out[...] = value.astype(LOW)


def choose(own, moved, beside, out):
    sec = lax.axis_index("sec")

    @pl.when(sec == 0)
    def _():
        out[...] = own[...]

    @pl.when(sec == 1)
    def _():
        out[...] = beside[...]

    @pl.when(sec >= 2)
    def _():
        out[...] = moved[...]


def attend(
    first, second, queries, upstream, key_w, value_w, away, kept, low_ref, values, keys, dkeys, dvalues
):
    tp = lax.axis_index("tp")
    sec = lax.axis_index("sec")
    token_count, half = first.shape
    width = 2 * half
    scale = 1.0 / math.sqrt(HD)

    @pl.when(sec != 0)
    def _():
        crossed = ((sec > 1) & (sec % 2 == 1)).astype(jnp.int32)
        place = tp ^ crossed
        for weight, target in ((key_w, keys), (value_w, values)):
            value = matmul(first[...], weight[part(place, half), :])
            value = value + matmul(second[...], weight[part(1 - place, half), :])
            target[...] = value.astype(LOW)
        heads = [
            (slice(s * SEQ, (s + 1) * SEQ), slice(h * HD, (h + 1) * HD))
            for s in range(token_count // SEQ)
            for h in range(queries.shape[1] // HD)
        ]
        scores = [matmul(keys[at], queries[at], NT) for at in heads]
        dprobs = [matmul(values[at], upstream[at], NT) for at in heads]
        powers = [jnp.exp(x * scale) for x in scores]
        probs = [x * (1.0 / jnp.sum(x, axis=0, keepdims=True)) for x in powers]
        lows = [x.astype(LOW) for x in probs]
        for at, low in zip(heads, lows):
            dvalues[at] = matmul(low, upstream[at]).astype(LOW)
        rowdots = [jnp.sum(x * y, axis=0, keepdims=True) for x, y in zip(dprobs, probs)]
        dscores = [
            (y * (x - z)).astype(LOW) for x, y, z in zip(dprobs, probs, rowdots)
        ]
        for at, dscore in zip(heads, dscores):
            dkeys[at] = (matmul(dscore, queries[at]) * scale).astype(LOW)
        for i, low in enumerate(lows):
            low_ref[i] = low
        side = sec % 2
        pairs = lax.axis_size("sec") // 2
        block = width // (2 * pairs)
        for target, parity in ((away, 1 - side), (kept, side)):
            for i in range(pairs):
                rows = part(2 * i + parity, block)
                value = matmul(dkeys[...], key_w[rows, :], NT)
                value = value + matmul(dvalues[...], value_w[rows, :], NT)
                target[:, i * block : (i + 1) * block] = value.astype(target.dtype)

    @pl.when(sec == 0)
    def _():
        away[...] = jnp.zeros_like(away)
        kept[...] = jnp.zeros_like(kept)


def contexts(low_ref, values, hidden, out):
    sec = lax.axis_index("sec")
    head_count = values.shape[1] // HD

    @pl.when(sec == 0)
    def _():
        out[...] = hidden[...]

    @pl.when(sec != 0)
    def _():
        for i in range(low_ref.shape[0]):
            s, h = i // head_count, i % head_count
            at = slice(s * SEQ, (s + 1) * SEQ), slice(h * HD, (h + 1) * HD)
            out[at] = matmul(low_ref[i], values[at], TN).astype(LOW)


def gather_term(kept, arrived, own, *sent):
    tp = lax.axis_index("tp")
    here = lax.axis_index("sec") // 2 * lax.axis_size("tp") + tp
    width = own.shape[1]
    for k in range(len(sent) + 1):
        columns = part(here ^ k, width)
        value = kept[:, columns] + arrived[:, columns].astype(WIDE)
        if k == 0:
            own[...] = value
        else:
            sent[k - 1][...] = value.astype(LOW)


def swap(block, axis, step):
    size = lax.axis_size(axis)
    return lax.ppermute(block, axis, [(i, i ^ step) for i in range(size)])


def shards(
    tokens,
    routes,
    gate_weights,
    moe_gain,
    attn_gain,
    expert_in,
    expert_out,
    query_weight,
    key_weight,
    value_weight,
    cotangent,
):
    token_rows = tokens[0]
    route_rows = routes[0].T
    gate_rows = gate_weights[0].T
    token_count, model_width = token_rows.shape
    experts = lax.axis_size("exp")
    sections = lax.axis_size("sec")
    tp_size = lax.axis_size("tp")
    sec = lax.axis_index("sec")
    half = model_width // tp_size
    capacity = 3 * token_count // experts
    weight_first = expert_in[0, 0]
    weight_second = expert_out[0, 0]
    units = weight_first.shape[1]

    middle = max(2, experts // 2 + 1)
    groups = [list(range(middle - 1, 1, -1)), list(range(experts - 1, middle - 1, -1))]
    row_half, row_whole = shape_of((capacity, half)), shape_of((capacity, model_width))
    earlier = call(
        triangle,
        [shape_of((token_count, token_count))],
        [],
        flops=20 * token_count * token_count * model_width,
    )[0]
    *far_rows, near_rows, own_rows = call(
        functools.partial(prepare, experts),
        [row_half] * (experts - 2) + [row_whole] * 2,
        [token_rows, route_rows, moe_gain, earlier],
        [pltpu.VMEM((token_count, model_width), LOW)],
        flops=2 * 3 * token_count * token_count * model_width,
    )
    def hold(array, after):
        return call(idle, [], [], after=after, held=[array])[0]

    def joined(group):
        blocks = [swap(far_rows[k - 2], "exp", k) for k in group]
        return blocks[0] if len(blocks) == 1 else jnp.concatenate(blocks, axis=0)

    def total(away, kept):
        return (kept + swap(away, "tp", 1).astype(WIDE)).astype(LOW)

    def through(rows, after):
        count = rows[0].shape[0]
        return call(
            functools.partial(expert, len(rows) - 1),
            [shape_of((count, half)), shape_of((count, half), WIDE)],
            [*rows, weight_first, weight_second],
            [pltpu.VMEM((count, units), LOW)],
            flops=4 * count * model_width * units,
            limit=24,
            after=after,
        )

    arriving = [joined(groups[0])]
    later = [near_rows] + [far_rows[k - 2] for k in groups[1]]
    loads = max(1, units // 512) + 1
    own_away, own_kept, weight_first, weight_second, *later = call(
        expert_first,
        [
            row_half,
            shape_of((capacity, half), WIDE),
            shape_of(weight_first.shape),
            shape_of(weight_second.shape),
        ],
        [own_rows, weight_first, weight_second],
        [pltpu.VMEM((capacity, units), LOW), pltpu.SemaphoreType.DMA((loads,))],
        flops=4 * capacity * model_width * units,
        remote=(1, 2),
        limit=44,
        held=later,
    )
    near = swap(later[0], "exp", 1)
    for k, rows in zip(groups[1], later[1:]):
        far_rows[k - 2] = rows
    arriving.append(joined(groups[1]))
    returned = {0: total(own_away, own_kept)}
    arriving[0] = hold(arriving[0], [own_away])
    others = [swap(arriving[0], "tp", 1)]
    high, low, upstream = call(
        functools.partial(mixing, experts),
        [shape_of((experts, token_count, capacity))] * 2 + [shape_of(cotangent.shape[1:])],
        [route_rows, gate_rows, earlier, cotangent[0]],
        [pltpu.SemaphoreType.DMA],
        remote=(3,),
        after=[arriving[0]],
    )
    others.append(swap(arriving[1], "tp", 1))

    def give_back(group, away, kept):
        mixed = total(away, kept)
        for i, k in enumerate(group):
            block = mixed if len(group) == 1 else mixed[i * capacity : (i + 1) * capacity]
            returned[k] = swap(block, "exp", k)
        return mixed

    away, kept = through([arriving[0], others[0]], [returned[0], high])
    near_away, near_kept = through([near], [away])
    mixed = give_back(groups[0], away, kept)
    returned[1] = swap(total(near_away, near_kept), "exp", 1)
    away, kept = through([arriving[1], others[1]], [near_away, mixed])
    give_back(groups[1], away, kept)

    hidden_half = call(
        functools.partial(combine, experts),
        [shape_of((token_count, half))],
        [token_rows, high, low, *(returned[k] for k in range(experts))],
        flops=4 * 3 * token_count * token_count * half,
    )[0]

    beside = swap(hidden_half, "sec", 1)
    hidden_other = swap(hidden_half, "tp", 1)
    encoder_half = jnp.where(sec == 1, beside, hidden_half)
    moved = hidden_half
    for i in range(1, sections // 2):
        targets = {j: j for j in range(sections * tp_size)}
        for t in range(tp_size):
            even, odd = 2 * i * tp_size + t, (2 * i + 1) * tp_size + (t ^ 1)
            targets |= {t: even, even: t, tp_size + t: odd, odd: tp_size + (t ^ 1)}
        arrived = lax.ppermute(encoder_half, ("sec", "tp"), list(targets.items()))
        moved = arrived if sections == 4 else jnp.where(sec // 2 == i, arrived, moved)
    first = call(choose, [shape_of(hidden_half.shape)], [hidden_other, moved, beside])[0]
    second = swap(first, "sec", 1)

    local_width = query_weight.shape[2]
    queries = call(
        project,
        [shape_of((token_count, local_width))],
        [hidden_half, hidden_other, attn_gain, query_weight[0]],
        flops=2 * token_count * model_width * local_width,
    )[0]
    heads = token_count // SEQ * (local_width // HD)
    away, kept, lows, values = call(
        attend,
        [
            shape_of((token_count, model_width // 2)),
            shape_of((token_count, model_width // 2), WIDE),
            shape_of((heads, SEQ, SEQ)),
            shape_of((token_count, local_width)),
        ],
        [first, second, queries, upstream, key_weight[0], value_weight[0]],
        [pltpu.VMEM((token_count, local_width), LOW)] * 3,
        flops=10 * token_count * model_width * local_width,
    )
    context = call(
        contexts,
        [shape_of((token_count, local_width))],
        [lows, values, hidden_half],
        flops=2 * token_count * SEQ * local_width,
    )[0]

    own = model_width // (sections * tp_size)
    count = sections // 2 * tp_size
    both = sections * tp_size
    blocks = call(
        gather_term,
        [shape_of((token_count, own), WIDE)] + [shape_of((token_count, own))] * (count - 1),
        [kept, swap(away, "sec", 1)],
    )
    total = blocks[0]
    for k in range(1, count):
        pairs = []
        for i in range(both):
            section, t = i // tp_size, i % tp_size
            target = (section // 2 * tp_size + t) ^ k
            pairs.append((i, (target // tp_size * 2 + section % 2) * tp_size + target % tp_size))
        total = total + lax.ppermute(blocks[k], ("sec", "tp"), pairs).astype(WIDE)
    return (context[None], total.astype(LOW))


def solution(mesh):
    placed = (
        P("sec", "exp", None),
        P("sec", "exp", None),
        P("sec", "exp", None),
        P("sec", None),
        P("sec", None),
        P("sec", "exp", None, "tp"),
        P("sec", "exp", "tp", None),
        P("sec", None, "tp"),
        P("sec", None, "tp"),
        P("sec", None, "tp"),
        P("sec", "exp", "tp"),
    )
    return jax.shard_map(
        shards,
        mesh=mesh,
        in_specs=placed,
        out_specs=(P("sec", "exp", "tp"), P("exp", ("sec", "tp"))),
        check_vma=False,
    )
```

```python
import functools
import math

import jax
import jax.numpy as jnp
from jax import lax
from jax.experimental import pallas as pl
from jax.experimental.pallas import tpu as pltpu
from jax.sharding import PartitionSpec as P

HD = 128
SEQ = 128
EPS = 1e-05

WEIGHT = 2

LOW = jnp.bfloat16
WIDE = jnp.float32
VMEM = pl.BlockSpec(memory_space=pltpu.VMEM)
HBM = pl.BlockSpec(memory_space=pltpu.HBM)
ANY = pl.BlockSpec(memory_space=pl.ANY)
NT = (((1,), (1,)), ((), ()))
TN = (((0,), (0,)), ((), ()))


def matmul(a, b, dims=(((1,), (0,)), ((), ()))):
    return lax.dot_general(a, b, dims, preferred_element_type=WIDE)


def call(body, out_shape, inputs, scratch=(), flops=0, limit=16, remote=(), after=(), held=()):
    def size(x):
        return math.prod(x.shape) * jnp.dtype(x.dtype).itemsize

    count, results = len(inputs), len(out_shape)
    extra = len(after) + len(held)

    def run(*refs):
        outs = refs[count + extra : count + extra + results]
        return body(*refs[:count], *outs, *refs[count + extra + results + len(held) :])

    moved = sum(size(x) for x in inputs) + sum(size(x) for x in out_shape)
    return pl.pallas_call(
        run,
        out_shape=[*out_shape, *(shape_of(x.shape, x.dtype) for x in held)],
        in_specs=[HBM if i in remote else VMEM for i in range(count)] + [ANY] * extra,
        out_specs=[VMEM] * results + [ANY] * len(held),
        scratch_shapes=list(scratch),
        input_output_aliases={count + len(after) + i: results + i for i in range(len(held))},
        compiler_params=pltpu.CompilerParams(vmem_limit_bytes=limit * 2**20),
        cost_estimate=pl.CostEstimate(
            flops=WEIGHT * flops, bytes_accessed=WEIGHT * moved, transcendentals=0
        ),
    )(*inputs, *after, *held)


def shape_of(dims, kind=LOW):
    return jax.ShapeDtypeStruct(dims, kind)


def part(index, width):
    return pl.ds(pl.multiple_of(index * width, width), width)


def triangle(out):
    source = lax.broadcasted_iota(jnp.int32, out.shape, 0)
    target = lax.broadcasted_iota(jnp.int32, out.shape, 1)
    out[...] = jnp.where(source < target, 1.0, 0.0).astype(LOW)


def places(routes, earlier, me, rows):
    labels = lax.broadcasted_iota(jnp.int32, (rows, 1), 0) ^ me
    first = routes[0:1, :] == labels
    second = routes[1:2, :] == labels
    either = first | second
    before = matmul(jnp.where(either, 1.0, 0.0).astype(LOW), earlier)
    return jnp.where(either, before, -1.0), first, second


def table(place, k, capacity):
    slots = lax.broadcasted_iota(jnp.int32, (capacity, place.shape[1]), 0).astype(WIDE)
    return jnp.where(place[k : k + 1, :] == slots, 1.0, 0.0).astype(LOW)


def prepare(experts, tokens, routes, gain, earlier, *outs):
    far, near, own, normed_ref = outs[:-3], outs[-3], outs[-2], outs[-1]
    me = lax.axis_index("exp")
    tp = lax.axis_index("tp")
    capacity, width = own.shape
    half = width // 2
    wide = tokens[...].astype(WIDE)
    average = jnp.mean(wide, axis=-1, keepdims=True)
    centred = wide - average
    spread = jnp.mean(centred * centred, axis=-1, keepdims=True)
    normed_ref[...] = (centred * lax.rsqrt(spread + EPS) * gain[...]).astype(LOW)
    place, _, _ = places(routes[...], earlier[...], me, max(16, experts))
    normed_half = normed_ref[:, part(tp, half)]
    for k in range(experts - 1, 1, -1):
        far[k - 2][...] = matmul(table(place, k, capacity), normed_half).astype(LOW)
    normed = normed_ref[...]
    near[...] = matmul(table(place, 1, capacity), normed).astype(LOW)
    own[...] = matmul(table(place, 0, capacity), normed).astype(LOW)


def mixing(experts, routes, gates, earlier, upstream, high, low, upstream_here, arrived):
    load = pltpu.make_async_copy(upstream, upstream_here, arrived)
    load.start()
    me = lax.axis_index("exp")
    token_count = routes.shape[1]
    capacity = high.shape[2]
    place, first, second = places(routes[...], earlier[...], me, max(16, experts))
    gate = jnp.where(first, gates[0:1, :], 0.0) + jnp.where(second, gates[1:2, :], 0.0)
    place = place.T
    gate = gate.T
    slots = lax.broadcasted_iota(jnp.int32, (token_count, capacity), 1).astype(WIDE)
    for k in range(experts):
        weight = jnp.where(place[:, k : k + 1] == slots, gate[:, k : k + 1], 0.0)
        upper = weight.astype(LOW)
        high[k] = upper
        low[k] = (weight - upper.astype(WIDE)).astype(LOW)
    load.wait()


def expert(split, *refs):
    rows, refs = refs[: 1 + split], refs[1 + split :]
    first, second, away, kept, inner = refs
    tp = lax.axis_index("tp")
    width, hidden = first.shape
    half = width // 2
    chunk = min(512, hidden)
    for c in range(hidden // chunk):
        columns = slice(c * chunk, (c + 1) * chunk)
        if split:
            value = matmul(rows[0][...], first[part(tp, half), columns])
            value = value + matmul(rows[1][...], first[part(1 - tp, half), columns])
        else:
            value = matmul(rows[0][...], first[:, columns])
        inner[:, columns] = jnp.maximum(value, 0.0).astype(LOW)
    away[...] = matmul(inner[...], second[:, part(1 - tp, half)]).astype(LOW)
    kept[...] = matmul(inner[...], second[:, part(tp, half)])


def expert_first(rows, first, second, away, kept, first_here, second_here, inner, arrived):
    tp = lax.axis_index("tp")
    width, hidden = first.shape
    half = width // 2
    chunk = min(512, hidden)
    columns = [slice(c * chunk, (c + 1) * chunk) for c in range(hidden // chunk)]
    loads = [
        pltpu.make_async_copy(first.at[:, c], first_here.at[:, c], arrived.at[i])
        for i, c in enumerate(columns)
    ]
    loads.append(pltpu.make_async_copy(second, second_here, arrived.at[len(columns)]))
    for load in loads:
        load.start()
    for c, load in zip(columns, loads):
        load.wait()
        inner[:, c] = jnp.maximum(matmul(rows[...], first_here[:, c]), 0.0).astype(LOW)
    loads[-1].wait()
    away[...] = matmul(inner[...], second_here[:, part(1 - tp, half)]).astype(LOW)
    kept[...] = matmul(inner[...], second_here[:, part(tp, half)])


def idle():
    pass


def add(kept, arrived, out):
    out[...] = (kept[...] + arrived[...].astype(WIDE)).astype(LOW)


def combine(experts, tokens, high, low, *refs):
    returned, out = refs[:-1], refs[-1]
    tp = lax.axis_index("tp")
    half = out.shape[1]
    mixed = tokens[:, part(tp, half)].astype(WIDE)
    for k in range(experts):
        rows = returned[k][...]
        mixed = mixed + (matmul(high[k], rows) + matmul(low[k], rows))
    out[...] = mixed.astype(LOW)


def project(mine, other, gain, weight, out):
    tp = lax.axis_index("tp")
    half = mine.shape[1]
    own = mine[...].astype(WIDE)
    rest = other[...].astype(WIDE)
    average = (
        jnp.sum(own, axis=-1, keepdims=True) + jnp.sum(rest, axis=-1, keepdims=True)
    ) / (2 * half)
    own = own - average
    rest = rest - average
    spread = (
        jnp.sum(own * own, axis=-1, keepdims=True) + jnp.sum(rest * rest, axis=-1, keepdims=True)
    ) / (2 * half)
    factor = lax.rsqrt(spread + EPS)
    own = (own * factor * gain[:, part(tp, half)]).astype(LOW)
    rest = (rest * factor * gain[:, part(1 - tp, half)]).astype(LOW)
    value = matmul(own, weight[part(tp, half), :]) + matmul(rest, weight[part(1 - tp, half), :])
    out[...] = value.astype(LOW)


def encoder_part(own, beside, out):
    sec = lax.axis_index("sec")

    @pl.when(sec == 1)
    def _():
        out[...] = beside[...]

    @pl.when(sec != 1)
    def _():
        out[...] = own[...]


def choose(own, moved, beside, out):
    sec = lax.axis_index("sec")

    @pl.when(sec == 0)
    def _():
        out[...] = own[...]

    @pl.when(sec == 1)
    def _():
        out[...] = beside[...]

    @pl.when(sec >= 2)
    def _():
        out[...] = moved[...]


def attend(
    first, second, queries, upstream, key_w, value_w, away, kept, low_ref, values, keys, dkeys, dvalues
):
    tp = lax.axis_index("tp")
    sec = lax.axis_index("sec")
    token_count, half = first.shape
    width = 2 * half
    scale = 1.0 / math.sqrt(HD)

    @pl.when(sec != 0)
    def _():
        crossed = ((sec > 1) & (sec % 2 == 1)).astype(jnp.int32)
        place = tp ^ crossed
        for weight, target in ((key_w, keys), (value_w, values)):
            value = matmul(first[...], weight[part(place, half), :])
            value = value + matmul(second[...], weight[part(1 - place, half), :])
            target[...] = value.astype(LOW)
        heads = [
            (slice(s * SEQ, (s + 1) * SEQ), slice(h * HD, (h + 1) * HD))
            for s in range(token_count // SEQ)
            for h in range(queries.shape[1] // HD)
        ]
        scores = [matmul(keys[at], queries[at], NT) for at in heads]
        dprobs = [matmul(values[at], upstream[at], NT) for at in heads]
        powers = [jnp.exp(x * scale) for x in scores]
        probs = [x * (1.0 / jnp.sum(x, axis=0, keepdims=True)) for x in powers]
        lows = [x.astype(LOW) for x in probs]
        for at, low in zip(heads, lows):
            dvalues[at] = matmul(low, upstream[at]).astype(LOW)
        rowdots = [jnp.sum(x * y, axis=0, keepdims=True) for x, y in zip(dprobs, probs)]
        dscores = [
            (y * (x - z)).astype(LOW) for x, y, z in zip(dprobs, probs, rowdots)
        ]
        for at, dscore in zip(heads, dscores):
            dkeys[at] = (matmul(dscore, queries[at]) * scale).astype(LOW)
        for i, low in enumerate(lows):
            low_ref[i] = low
        side = sec % 2
        pairs = lax.axis_size("sec") // 2
        block = width // (2 * pairs)
        for target, parity in ((away, 1 - side), (kept, side)):
            for i in range(pairs):
                rows = part(2 * i + parity, block)
                value = matmul(dkeys[...], key_w[rows, :], NT)
                value = value + matmul(dvalues[...], value_w[rows, :], NT)
                target[:, i * block : (i + 1) * block] = value.astype(target.dtype)

    @pl.when(sec == 0)
    def _():
        away[...] = jnp.zeros_like(away)
        kept[...] = jnp.zeros_like(kept)


def contexts(low_ref, values, hidden, out):
    sec = lax.axis_index("sec")
    head_count = values.shape[1] // HD

    @pl.when(sec == 0)
    def _():
        out[...] = hidden[...]

    @pl.when(sec != 0)
    def _():
        for i in range(low_ref.shape[0]):
            s, h = i // head_count, i % head_count
            at = slice(s * SEQ, (s + 1) * SEQ), slice(h * HD, (h + 1) * HD)
            out[at] = matmul(low_ref[i], values[at], TN).astype(LOW)


def gather_term(kept, arrived, own, *sent):
    tp = lax.axis_index("tp")
    here = lax.axis_index("sec") // 2 * lax.axis_size("tp") + tp
    width = own.shape[1]
    for k in range(len(sent) + 1):
        columns = part(here ^ k, width)
        value = kept[:, columns] + arrived[:, columns].astype(WIDE)
        if k == 0:
            own[...] = value
        else:
            sent[k - 1][...] = value.astype(LOW)


def swap(block, axis, step):
    size = lax.axis_size(axis)
    return lax.ppermute(block, axis, [(i, i ^ step) for i in range(size)])


def shards(
    tokens,
    routes,
    gate_weights,
    moe_gain,
    attn_gain,
    expert_in,
    expert_out,
    query_weight,
    key_weight,
    value_weight,
    cotangent,
):
    token_rows = tokens[0]
    route_rows = routes[0].T
    gate_rows = gate_weights[0].T
    token_count, model_width = token_rows.shape
    experts = lax.axis_size("exp")
    sections = lax.axis_size("sec")
    tp_size = lax.axis_size("tp")
    sec = lax.axis_index("sec")
    half = model_width // tp_size
    capacity = 3 * token_count // experts
    weight_first = expert_in[0, 0]
    weight_second = expert_out[0, 0]
    units = weight_first.shape[1]

    middle = max(2, experts // 2 + 1)
    groups = [list(range(middle - 1, 1, -1)), list(range(experts - 1, middle - 1, -1))]
    row_half, row_whole = shape_of((capacity, half)), shape_of((capacity, model_width))
    earlier = call(
        triangle,
        [shape_of((token_count, token_count))],
        [],
        flops=20 * token_count * token_count * model_width,
    )[0]
    *far_rows, near_rows, own_rows = call(
        functools.partial(prepare, experts),
        [row_half] * (experts - 2) + [row_whole] * 2,
        [token_rows, route_rows, moe_gain, earlier],
        [pltpu.VMEM((token_count, model_width), LOW)],
        flops=2 * 3 * token_count * token_count * model_width,
    )
    def hold(array, after):
        return call(idle, [], [], after=after, held=[array])[0]

    def joined(group):
        blocks = [swap(far_rows[k - 2], "exp", k) for k in group]
        return blocks[0] if len(blocks) == 1 else jnp.concatenate(blocks, axis=0)

    def total(away, kept):
        return call(add, [shape_of(away.shape)], [kept, swap(away, "tp", 1)])[0]

    def through(rows, after):
        count = rows[0].shape[0]
        return call(
            functools.partial(expert, len(rows) - 1),
            [shape_of((count, half)), shape_of((count, half), WIDE)],
            [*rows, weight_first, weight_second],
            [pltpu.VMEM((count, units), LOW)],
            flops=4 * count * model_width * units,
            limit=24,
            after=after,
        )

    arriving = [joined(groups[0])]
    later = [near_rows] + [far_rows[k - 2] for k in groups[1]]
    loads = max(1, units // 512) + 1
    own_away, own_kept, weight_first, weight_second, *later = call(
        expert_first,
        [
            row_half,
            shape_of((capacity, half), WIDE),
            shape_of(weight_first.shape),
            shape_of(weight_second.shape),
        ],
        [own_rows, weight_first, weight_second],
        [pltpu.VMEM((capacity, units), LOW), pltpu.SemaphoreType.DMA((loads,))],
        flops=4 * capacity * model_width * units,
        remote=(1, 2),
        limit=44,
        held=later,
    )
    near = swap(later[0], "exp", 1)
    for k, rows in zip(groups[1], later[1:]):
        far_rows[k - 2] = rows
    arriving.append(joined(groups[1]))
    returned = {0: total(own_away, own_kept)}
    arriving[0] = hold(arriving[0], [own_away])
    others = [swap(arriving[0], "tp", 1)]
    high, low, upstream = call(
        functools.partial(mixing, experts),
        [shape_of((experts, token_count, capacity))] * 2 + [shape_of(cotangent.shape[1:])],
        [route_rows, gate_rows, earlier, cotangent[0]],
        [pltpu.SemaphoreType.DMA],
        remote=(3,),
        after=[arriving[0]],
    )
    others.append(swap(arriving[1], "tp", 1))

    def give_back(group, away, kept):
        mixed = total(away, kept)
        for i, k in enumerate(group):
            block = mixed if len(group) == 1 else mixed[i * capacity : (i + 1) * capacity]
            returned[k] = swap(block, "exp", k)
        return mixed

    away, kept = through([arriving[0], others[0]], [returned[0], high])
    near_away, near_kept = through([near], [away])
    mixed = give_back(groups[0], away, kept)
    near_total = (near_kept + swap(near_away, "tp", 1).astype(WIDE)).astype(LOW)
    returned[1] = swap(near_total, "exp", 1)
    away, kept = through([arriving[1], others[1]], [near_away, mixed])
    give_back(groups[1], away, kept)

    hidden_half = call(
        functools.partial(combine, experts),
        [shape_of((token_count, half))],
        [token_rows, high, low, *(returned[k] for k in range(experts))],
        flops=4 * 3 * token_count * token_count * half,
    )[0]

    beside = lax.ppermute(hidden_half, "sec", [(0, 1), (1, 0)] + [(i, i) for i in range(2, sections)])
    hidden_other = swap(hidden_half, "tp", 1)
    encoder_half = call(encoder_part, [shape_of(hidden_half.shape)], [hidden_half, beside])[0]
    moved = hidden_half
    for i in range(1, sections // 2):
        targets = {j: j for j in range(sections * tp_size)}
        for t in range(tp_size):
            even, odd = 2 * i * tp_size + t, (2 * i + 1) * tp_size + (t ^ 1)
            targets |= {t: even, even: t, tp_size + t: odd, odd: tp_size + (t ^ 1)}
        arrived = lax.ppermute(encoder_half, ("sec", "tp"), list(targets.items()))
        moved = arrived if sections == 4 else jnp.where(sec // 2 == i, arrived, moved)
    first = call(choose, [shape_of(hidden_half.shape)], [hidden_other, moved, beside])[0]
    second = swap(first, "sec", 1)

    local_width = query_weight.shape[2]
    queries = call(
        project,
        [shape_of((token_count, local_width))],
        [hidden_half, hidden_other, attn_gain, query_weight[0]],
        flops=2 * token_count * model_width * local_width,
    )[0]
    heads = token_count // SEQ * (local_width // HD)
    away, kept, lows, values = call(
        attend,
        [
            shape_of((token_count, model_width // 2)),
            shape_of((token_count, model_width // 2), WIDE),
            shape_of((heads, SEQ, SEQ)),
            shape_of((token_count, local_width)),
        ],
        [first, second, queries, upstream, key_weight[0], value_weight[0]],
        [pltpu.VMEM((token_count, local_width), LOW)] * 3,
        flops=10 * token_count * model_width * local_width,
    )
    context = call(
        contexts,
        [shape_of((token_count, local_width))],
        [lows, values, hidden_half],
        flops=2 * token_count * SEQ * local_width,
    )[0]

    own = model_width // (sections * tp_size)
    count = sections // 2 * tp_size
    both = sections * tp_size
    blocks = call(
        gather_term,
        [shape_of((token_count, own), WIDE)] + [shape_of((token_count, own))] * (count - 1),
        [kept, swap(away, "sec", 1)],
    )
    total = blocks[0]
    for k in range(1, count):
        pairs = []
        for i in range(both):
            section, t = i // tp_size, i % tp_size
            target = (section // 2 * tp_size + t) ^ k
            pairs.append((i, (target // tp_size * 2 + section % 2) * tp_size + target % tp_size))
        total = total + lax.ppermute(blocks[k], ("sec", "tp"), pairs).astype(WIDE)
    return (context[None], total.astype(LOW))


def solution(mesh):
    placed = (
        P("sec", "exp", None),
        P("sec", "exp", None),
        P("sec", "exp", None),
        P("sec", None),
        P("sec", None),
        P("sec", "exp", None, "tp"),
        P("sec", "exp", "tp", None),
        P("sec", None, "tp"),
        P("sec", None, "tp"),
        P("sec", None, "tp"),
        P("sec", "exp", "tp"),
    )
    return jax.shard_map(
        shards,
        mesh=mesh,
        in_specs=placed,
        out_specs=(P("sec", "exp", "tp"), P("exp", ("sec", "tp"))),
        check_vma=False,
    )
```

```python
import functools
import math

import jax
import jax.numpy as jnp
from jax import lax
from jax.experimental import pallas as pl
from jax.experimental.pallas import tpu as pltpu
from jax.sharding import PartitionSpec as P

HD = 128
SEQ = 128
EPS = 1e-05

LOW = jnp.bfloat16
WIDE = jnp.float32
VMEM = pl.BlockSpec(memory_space=pltpu.VMEM)
HBM = pl.BlockSpec(memory_space=pltpu.HBM)
ANY = pl.BlockSpec(memory_space=pl.ANY)
NT = (((1,), (1,)), ((), ()))
TN = (((0,), (0,)), ((), ()))


def matmul(a, b, dims=(((1,), (0,)), ((), ()))):
    return lax.dot_general(a, b, dims, preferred_element_type=WIDE)


def call(body, out_shape, inputs, scratch=(), flops=0, limit=16, remote=(), after=(), held=()):
    def size(x):
        return math.prod(x.shape) * jnp.dtype(x.dtype).itemsize

    count, results = len(inputs), len(out_shape)
    extra = len(after) + len(held)

    def run(*refs):
        outs = refs[count + extra : count + extra + results]
        return body(*refs[:count], *outs, *refs[count + extra + results + len(held) :])

    moved = sum(size(x) for x in inputs) + sum(size(x) for x in out_shape)
    return pl.pallas_call(
        run,
        out_shape=[*out_shape, *(shape_of(x.shape, x.dtype) for x in held)],
        in_specs=[HBM if i in remote else VMEM for i in range(count)] + [ANY] * extra,
        out_specs=[VMEM] * results + [ANY] * len(held),
        scratch_shapes=list(scratch),
        input_output_aliases={count + len(after) + i: results + i for i in range(len(held))},
        compiler_params=pltpu.CompilerParams(vmem_limit_bytes=limit * 2**20),
        cost_estimate=pl.CostEstimate(flops=flops, bytes_accessed=moved, transcendentals=0),
    )(*inputs, *after, *held)


def shape_of(dims, kind=LOW):
    return jax.ShapeDtypeStruct(dims, kind)


def part(index, width):
    return pl.ds(pl.multiple_of(index * width, width), width)


def triangle(out):
    source = lax.broadcasted_iota(jnp.int32, out.shape, 0)
    target = lax.broadcasted_iota(jnp.int32, out.shape, 1)
    out[...] = jnp.where(source < target, 1.0, 0.0).astype(LOW)


def places(routes, earlier, me, rows):
    labels = lax.broadcasted_iota(jnp.int32, (rows, 1), 0) ^ me
    first = routes[0:1, :] == labels
    second = routes[1:2, :] == labels
    either = first | second
    before = matmul(jnp.where(either, 1.0, 0.0).astype(LOW), earlier)
    return jnp.where(either, before, -1.0), first, second


def table(place, k, capacity):
    slots = lax.broadcasted_iota(jnp.int32, (capacity, place.shape[1]), 0).astype(WIDE)
    return jnp.where(place[k : k + 1, :] == slots, 1.0, 0.0).astype(LOW)


def prepare(experts, tokens, routes, gain, earlier, *outs):
    far, near, own, normed_ref = outs[:-3], outs[-3], outs[-2], outs[-1]
    me = lax.axis_index("exp")
    tp = lax.axis_index("tp")
    capacity, width = own.shape
    half = width // 2
    wide = tokens[...].astype(WIDE)
    average = jnp.mean(wide, axis=-1, keepdims=True)
    centred = wide - average
    spread = jnp.mean(centred * centred, axis=-1, keepdims=True)
    normed_ref[...] = (centred * lax.rsqrt(spread + EPS) * gain[...]).astype(LOW)
    place, _, _ = places(routes[...], earlier[...], me, max(16, experts))
    normed_half = normed_ref[:, part(tp, half)]
    for k in range(experts - 1, 1, -1):
        far[k - 2][...] = matmul(table(place, k, capacity), normed_half).astype(LOW)
    normed = normed_ref[...]
    near[...] = matmul(table(place, 1, capacity), normed).astype(LOW)
    own[...] = matmul(table(place, 0, capacity), normed).astype(LOW)


def mixing(experts, routes, gates, earlier, upstream, high, low, upstream_here, arrived):
    load = pltpu.make_async_copy(upstream, upstream_here, arrived)
    load.start()
    me = lax.axis_index("exp")
    token_count = routes.shape[1]
    capacity = high.shape[2]
    place, first, second = places(routes[...], earlier[...], me, max(16, experts))
    gate = jnp.where(first, gates[0:1, :], 0.0) + jnp.where(second, gates[1:2, :], 0.0)
    place = place.T
    gate = gate.T
    slots = lax.broadcasted_iota(jnp.int32, (token_count, capacity), 1).astype(WIDE)
    for k in range(experts):
        weight = jnp.where(place[:, k : k + 1] == slots, gate[:, k : k + 1], 0.0)
        upper = weight.astype(LOW)
        high[k] = upper
        low[k] = (weight - upper.astype(WIDE)).astype(LOW)
    load.wait()


def expert(split, *refs):
    rows, refs = refs[: 1 + split], refs[1 + split :]
    first, second, away, kept, inner = refs
    tp = lax.axis_index("tp")
    width, hidden = first.shape
    half = width // 2
    chunk = min(512, hidden)
    for c in range(hidden // chunk):
        columns = slice(c * chunk, (c + 1) * chunk)
        if split:
            value = matmul(rows[0][...], first[part(tp, half), columns])
            value = value + matmul(rows[1][...], first[part(1 - tp, half), columns])
        else:
            value = matmul(rows[0][...], first[:, columns])
        inner[:, columns] = jnp.maximum(value, 0.0).astype(LOW)
    away[...] = matmul(inner[...], second[:, part(1 - tp, half)]).astype(LOW)
    kept[...] = matmul(inner[...], second[:, part(tp, half)])


def expert_first(rows, first, second, away, kept, first_here, second_here, inner, arrived):
    tp = lax.axis_index("tp")
    width, hidden = first.shape
    half = width // 2
    chunk = min(512, hidden)
    columns = [slice(c * chunk, (c + 1) * chunk) for c in range(hidden // chunk)]
    loads = [
        pltpu.make_async_copy(first.at[:, c], first_here.at[:, c], arrived.at[i])
        for i, c in enumerate(columns)
    ]
    loads.append(pltpu.make_async_copy(second, second_here, arrived.at[len(columns)]))
    for load in loads:
        load.start()
    for c, load in zip(columns, loads):
        load.wait()
        inner[:, c] = jnp.maximum(matmul(rows[...], first_here[:, c]), 0.0).astype(LOW)
    loads[-1].wait()
    away[...] = matmul(inner[...], second_here[:, part(1 - tp, half)]).astype(LOW)
    kept[...] = matmul(inner[...], second_here[:, part(tp, half)])


def idle():
    pass


def add(kept, arrived, out):
    out[...] = (kept[...] + arrived[...].astype(WIDE)).astype(LOW)


def combine(experts, tokens, high, low, *refs):
    returned, out = refs[:-1], refs[-1]
    tp = lax.axis_index("tp")
    half = out.shape[1]
    mixed = tokens[:, part(tp, half)].astype(WIDE)
    for k in range(experts):
        rows = returned[k][...]
        mixed = mixed + (matmul(high[k], rows) + matmul(low[k], rows))
    out[...] = mixed.astype(LOW)


def project(mine, other, gain, weight, out):
    tp = lax.axis_index("tp")
    half = mine.shape[1]
    own = mine[...].astype(WIDE)
    rest = other[...].astype(WIDE)
    average = (
        jnp.sum(own, axis=-1, keepdims=True) + jnp.sum(rest, axis=-1, keepdims=True)
    ) / (2 * half)
    own = own - average
    rest = rest - average
    spread = (
        jnp.sum(own * own, axis=-1, keepdims=True) + jnp.sum(rest * rest, axis=-1, keepdims=True)
    ) / (2 * half)
    factor = lax.rsqrt(spread + EPS)
    own = (own * factor * gain[:, part(tp, half)]).astype(LOW)
    rest = (rest * factor * gain[:, part(1 - tp, half)]).astype(LOW)
    value = matmul(own, weight[part(tp, half), :]) + matmul(rest, weight[part(1 - tp, half), :])
    out[...] = value.astype(LOW)


def encoder_part(own, beside, out):
    sec = lax.axis_index("sec")

    @pl.when(sec == 1)
    def _():
        out[...] = beside[...]

    @pl.when(sec != 1)
    def _():
        out[...] = own[...]


def choose(own, moved, beside, out):
    sec = lax.axis_index("sec")

    @pl.when(sec == 0)
    def _():
        out[...] = own[...]

    @pl.when(sec == 1)
    def _():
        out[...] = beside[...]

    @pl.when(sec >= 2)
    def _():
        out[...] = moved[...]


def attend(
    first, second, queries, upstream, key_w, value_w, away, kept, low_ref, values, keys, dkeys, dvalues
):
    tp = lax.axis_index("tp")
    sec = lax.axis_index("sec")
    token_count, half = first.shape
    width = 2 * half
    scale = 1.0 / math.sqrt(HD)

    @pl.when(sec != 0)
    def _():
        crossed = ((sec > 1) & (sec % 2 == 1)).astype(jnp.int32)
        place = tp ^ crossed
        for weight, target in ((key_w, keys), (value_w, values)):
            value = matmul(first[...], weight[part(place, half), :])
            value = value + matmul(second[...], weight[part(1 - place, half), :])
            target[...] = value.astype(LOW)
        heads = [
            (slice(s * SEQ, (s + 1) * SEQ), slice(h * HD, (h + 1) * HD))
            for s in range(token_count // SEQ)
            for h in range(queries.shape[1] // HD)
        ]
        scores = [matmul(keys[at], queries[at], NT) for at in heads]
        dprobs = [matmul(values[at], upstream[at], NT) for at in heads]
        powers = [jnp.exp(x * scale) for x in scores]
        probs = [x * (1.0 / jnp.sum(x, axis=0, keepdims=True)) for x in powers]
        lows = [x.astype(LOW) for x in probs]
        for at, low in zip(heads, lows):
            dvalues[at] = matmul(low, upstream[at]).astype(LOW)
        rowdots = [jnp.sum(x * y, axis=0, keepdims=True) for x, y in zip(dprobs, probs)]
        dscores = [
            (y * (x - z)).astype(LOW) for x, y, z in zip(dprobs, probs, rowdots)
        ]
        for at, dscore in zip(heads, dscores):
            dkeys[at] = (matmul(dscore, queries[at]) * scale).astype(LOW)
        for i, low in enumerate(lows):
            low_ref[i] = low
        side = sec % 2
        pairs = lax.axis_size("sec") // 2
        block = width // (2 * pairs)
        for target, parity in ((away, 1 - side), (kept, side)):
            for i in range(pairs):
                rows = part(2 * i + parity, block)
                value = matmul(dkeys[...], key_w[rows, :], NT)
                value = value + matmul(dvalues[...], value_w[rows, :], NT)
                target[:, i * block : (i + 1) * block] = value.astype(target.dtype)

    @pl.when(sec == 0)
    def _():
        away[...] = jnp.zeros_like(away)
        kept[...] = jnp.zeros_like(kept)


def contexts(low_ref, values, hidden, out):
    sec = lax.axis_index("sec")
    head_count = values.shape[1] // HD

    @pl.when(sec == 0)
    def _():
        out[...] = hidden[...]

    @pl.when(sec != 0)
    def _():
        for i in range(low_ref.shape[0]):
            s, h = i // head_count, i % head_count
            at = slice(s * SEQ, (s + 1) * SEQ), slice(h * HD, (h + 1) * HD)
            out[at] = matmul(low_ref[i], values[at], TN).astype(LOW)


def gather_term(kept, arrived, own, *sent):
    tp = lax.axis_index("tp")
    here = lax.axis_index("sec") // 2 * lax.axis_size("tp") + tp
    width = own.shape[1]
    for k in range(len(sent) + 1):
        columns = part(here ^ k, width)
        value = kept[:, columns] + arrived[:, columns].astype(WIDE)
        if k == 0:
            own[...] = value
        else:
            sent[k - 1][...] = value.astype(LOW)


def swap(block, axis, step):
    size = lax.axis_size(axis)
    return lax.ppermute(block, axis, [(i, i ^ step) for i in range(size)])


def shards(
    tokens,
    routes,
    gate_weights,
    moe_gain,
    attn_gain,
    expert_in,
    expert_out,
    query_weight,
    key_weight,
    value_weight,
    cotangent,
):
    token_rows = tokens[0]
    route_rows = routes[0].T
    gate_rows = gate_weights[0].T
    token_count, model_width = token_rows.shape
    experts = lax.axis_size("exp")
    sections = lax.axis_size("sec")
    tp_size = lax.axis_size("tp")
    sec = lax.axis_index("sec")
    half = model_width // tp_size
    capacity = 3 * token_count // experts
    weight_first = expert_in[0, 0]
    weight_second = expert_out[0, 0]
    units = weight_first.shape[1]

    middle = max(2, experts // 2 + 1)
    groups = [list(range(middle - 1, 1, -1)), list(range(experts - 1, middle - 1, -1))]
    row_half, row_whole = shape_of((capacity, half)), shape_of((capacity, model_width))
    earlier = call(
        triangle,
        [shape_of((token_count, token_count))],
        [],
        flops=20 * token_count * token_count * model_width,
    )[0]
    *far_rows, near_rows, own_rows = call(
        functools.partial(prepare, experts),
        [row_half] * (experts - 2) + [row_whole] * 2,
        [token_rows, route_rows, moe_gain, earlier],
        [pltpu.VMEM((token_count, model_width), LOW)],
        flops=2 * 3 * token_count * token_count * model_width,
    )
    def hold(array, after):
        return call(idle, [], [], after=after, held=[array])[0]

    def joined(group):
        blocks = [swap(far_rows[k - 2], "exp", k) for k in group]
        return blocks[0] if len(blocks) == 1 else jnp.concatenate(blocks, axis=0)

    def total(away, kept, plain=False):
        arrived = swap(away, "tp", 1)
        if plain:
            return (kept + arrived.astype(WIDE)).astype(LOW)
        return call(add, [shape_of(away.shape)], [kept, arrived])[0]

    def through(rows, after):
        count = rows[0].shape[0]
        return call(
            functools.partial(expert, len(rows) - 1),
            [shape_of((count, half)), shape_of((count, half), WIDE)],
            [*rows, weight_first, weight_second],
            [pltpu.VMEM((count, units), LOW)],
            flops=4 * count * model_width * units,
            limit=24,
            after=after,
        )

    arriving = [joined(groups[0])]
    later = [near_rows] + [far_rows[k - 2] for k in groups[1]]
    loads = max(1, units // 512) + 1
    own_away, own_kept, weight_first, weight_second, *later = call(
        expert_first,
        [
            row_half,
            shape_of((capacity, half), WIDE),
            shape_of(weight_first.shape),
            shape_of(weight_second.shape),
        ],
        [own_rows, weight_first, weight_second],
        [pltpu.VMEM((capacity, units), LOW), pltpu.SemaphoreType.DMA((loads,))],
        flops=4 * capacity * model_width * units,
        remote=(1, 2),
        limit=44,
        held=later,
    )
    near = swap(later[0], "exp", 1)
    for k, rows in zip(groups[1], later[1:]):
        far_rows[k - 2] = rows
    arriving.append(joined(groups[1]))
    returned = {0: total(own_away, own_kept, plain=True)}
    arriving[0] = hold(arriving[0], [own_away])
    others = [swap(arriving[0], "tp", 1)]
    high, low, upstream = call(
        functools.partial(mixing, experts),
        [shape_of((experts, token_count, capacity))] * 2 + [shape_of(cotangent.shape[1:])],
        [route_rows, gate_rows, earlier, cotangent[0]],
        [pltpu.SemaphoreType.DMA],
        remote=(3,),
        after=[arriving[0]],
    )
    others.append(swap(arriving[1], "tp", 1))

    def give_back(group, away, kept):
        mixed = total(away, kept)
        for i, k in enumerate(group):
            block = mixed if len(group) == 1 else mixed[i * capacity : (i + 1) * capacity]
            returned[k] = swap(block, "exp", k)
        return mixed

    away, kept = through([arriving[0], others[0]], [returned[0], high])
    near_away, near_kept = through([near], [away])
    mixed = give_back(groups[0], away, kept)
    returned[1] = swap(total(near_away, near_kept, plain=True), "exp", 1)
    away, kept = through([arriving[1], others[1]], [near_away, mixed])
    give_back(groups[1], away, kept)

    hidden_half = call(
        functools.partial(combine, experts),
        [shape_of((token_count, half))],
        [token_rows, high, low, *(returned[k] for k in range(experts))],
        flops=4 * 3 * token_count * token_count * half,
    )[0]

    beside = lax.ppermute(hidden_half, "sec", [(0, 1), (1, 0)] + [(i, i) for i in range(2, sections)])
    hidden_other = swap(hidden_half, "tp", 1)
    encoder_half = call(encoder_part, [shape_of(hidden_half.shape)], [hidden_half, beside])[0]
    moved = hidden_half
    for i in range(1, sections // 2):
        targets = {j: j for j in range(sections * tp_size)}
        for t in range(tp_size):
            even, odd = 2 * i * tp_size + t, (2 * i + 1) * tp_size + (t ^ 1)
            targets |= {t: even, even: t, tp_size + t: odd, odd: tp_size + (t ^ 1)}
        arrived = lax.ppermute(encoder_half, ("sec", "tp"), list(targets.items()))
        moved = arrived if sections == 4 else jnp.where(sec // 2 == i, arrived, moved)
    first = call(choose, [shape_of(hidden_half.shape)], [hidden_other, moved, beside])[0]
    second = swap(first, "sec", 1)

    local_width = query_weight.shape[2]
    queries = call(
        project,
        [shape_of((token_count, local_width))],
        [hidden_half, hidden_other, attn_gain, query_weight[0]],
        flops=2 * token_count * model_width * local_width,
    )[0]
    heads = token_count // SEQ * (local_width // HD)
    away, kept, lows, values = call(
        attend,
        [
            shape_of((token_count, model_width // 2)),
            shape_of((token_count, model_width // 2), WIDE),
            shape_of((heads, SEQ, SEQ)),
            shape_of((token_count, local_width)),
        ],
        [first, second, queries, upstream, key_weight[0], value_weight[0]],
        [pltpu.VMEM((token_count, local_width), LOW)] * 3,
        flops=10 * token_count * model_width * local_width,
    )
    context = call(
        contexts,
        [shape_of((token_count, local_width))],
        [lows, values, hidden_half],
        flops=2 * token_count * SEQ * local_width,
    )[0]

    own = model_width // (sections * tp_size)
    count = sections // 2 * tp_size
    both = sections * tp_size
    blocks = call(
        gather_term,
        [shape_of((token_count, own), WIDE)] + [shape_of((token_count, own))] * (count - 1),
        [kept, swap(away, "sec", 1)],
    )
    total = blocks[0]
    for k in range(1, count):
        pairs = []
        for i in range(both):
            section, t = i // tp_size, i % tp_size
            target = (section // 2 * tp_size + t) ^ k
            pairs.append((i, (target // tp_size * 2 + section % 2) * tp_size + target % tp_size))
        total = total + lax.ppermute(blocks[k], ("sec", "tp"), pairs).astype(WIDE)
    return (context[None], total.astype(LOW))


def solution(mesh):
    placed = (
        P("sec", "exp", None),
        P("sec", "exp", None),
        P("sec", "exp", None),
        P("sec", None),
        P("sec", None),
        P("sec", "exp", None, "tp"),
        P("sec", "exp", "tp", None),
        P("sec", None, "tp"),
        P("sec", None, "tp"),
        P("sec", None, "tp"),
        P("sec", "exp", "tp"),
    )
    return jax.shard_map(
        shards,
        mesh=mesh,
        in_specs=placed,
        out_specs=(P("sec", "exp", "tp"), P("exp", ("sec", "tp"))),
        check_vma=False,
    )
```

```python
import functools
import math

import jax
import jax.numpy as jnp
from jax import lax
from jax.experimental import pallas as pl
from jax.experimental.pallas import tpu as pltpu
from jax.sharding import PartitionSpec as P

HD = 128
SEQ = 128
EPS = 1e-05

LOW = jnp.bfloat16
WIDE = jnp.float32
VMEM = pl.BlockSpec(memory_space=pltpu.VMEM)
HBM = pl.BlockSpec(memory_space=pltpu.HBM)
ANY = pl.BlockSpec(memory_space=pl.ANY)
NT = (((1,), (1,)), ((), ()))
TN = (((0,), (0,)), ((), ()))


def matmul(a, b, dims=(((1,), (0,)), ((), ()))):
    return lax.dot_general(a, b, dims, preferred_element_type=WIDE)


def call(body, out_shape, inputs, scratch=(), flops=0, limit=16, remote=(), after=(), held=()):
    def size(x):
        return math.prod(x.shape) * jnp.dtype(x.dtype).itemsize

    count, results = len(inputs), len(out_shape)
    extra = len(after) + len(held)

    def run(*refs):
        outs = refs[count + extra : count + extra + results]
        return body(*refs[:count], *outs, *refs[count + extra + results + len(held) :])

    moved = sum(size(x) for x in inputs) + sum(size(x) for x in out_shape)
    return pl.pallas_call(
        run,
        out_shape=[*out_shape, *(shape_of(x.shape, x.dtype) for x in held)],
        in_specs=[HBM if i in remote else VMEM for i in range(count)] + [ANY] * extra,
        out_specs=[VMEM] * results + [ANY] * len(held),
        scratch_shapes=list(scratch),
        input_output_aliases={count + len(after) + i: results + i for i in range(len(held))},
        compiler_params=pltpu.CompilerParams(vmem_limit_bytes=limit * 2**20),
        cost_estimate=pl.CostEstimate(flops=flops, bytes_accessed=moved, transcendentals=0),
    )(*inputs, *after, *held)


def shape_of(dims, kind=LOW):
    return jax.ShapeDtypeStruct(dims, kind)


def part(index, width):
    return pl.ds(pl.multiple_of(index * width, width), width)


def triangle(out):
    source = lax.broadcasted_iota(jnp.int32, out.shape, 0)
    target = lax.broadcasted_iota(jnp.int32, out.shape, 1)
    out[...] = jnp.where(source < target, 1.0, 0.0).astype(LOW)


def places(routes, earlier, me, rows):
    labels = lax.broadcasted_iota(jnp.int32, (rows, 1), 0) ^ me
    first = routes[0:1, :] == labels
    second = routes[1:2, :] == labels
    either = first | second
    before = matmul(jnp.where(either, 1.0, 0.0).astype(LOW), earlier)
    return jnp.where(either, before, -1.0), first, second


def table(place, k, capacity):
    slots = lax.broadcasted_iota(jnp.int32, (capacity, place.shape[1]), 0).astype(WIDE)
    return jnp.where(place[k : k + 1, :] == slots, 1.0, 0.0).astype(LOW)


def prepare(experts, tokens, routes, gain, earlier, *outs):
    far, near, own, normed_ref = outs[:-3], outs[-3], outs[-2], outs[-1]
    me = lax.axis_index("exp")
    tp = lax.axis_index("tp")
    capacity, width = own.shape
    half = width // 2
    wide = tokens[...].astype(WIDE)
    average = jnp.mean(wide, axis=-1, keepdims=True)
    centred = wide - average
    spread = jnp.mean(centred * centred, axis=-1, keepdims=True)
    normed_ref[...] = (centred * lax.rsqrt(spread + EPS) * gain[...]).astype(LOW)
    place, _, _ = places(routes[...], earlier[...], me, max(16, experts))
    normed_half = normed_ref[:, part(tp, half)]
    for k in range(experts - 1, 1, -1):
        far[k - 2][...] = matmul(table(place, k, capacity), normed_half).astype(LOW)
    normed = normed_ref[...]
    near[...] = matmul(table(place, 1, capacity), normed).astype(LOW)
    own[...] = matmul(table(place, 0, capacity), normed).astype(LOW)


def mixing(experts, routes, gates, earlier, upstream, high, low, upstream_here, arrived):
    load = pltpu.make_async_copy(upstream, upstream_here, arrived)
    load.start()
    me = lax.axis_index("exp")
    token_count = routes.shape[1]
    capacity = high.shape[2]
    place, first, second = places(routes[...], earlier[...], me, max(16, experts))
    gate = jnp.where(first, gates[0:1, :], 0.0) + jnp.where(second, gates[1:2, :], 0.0)
    place = place.T
    gate = gate.T
    slots = lax.broadcasted_iota(jnp.int32, (token_count, capacity), 1).astype(WIDE)
    for k in range(experts):
        weight = jnp.where(place[:, k : k + 1] == slots, gate[:, k : k + 1], 0.0)
        upper = weight.astype(LOW)
        high[k] = upper
        low[k] = (weight - upper.astype(WIDE)).astype(LOW)
    load.wait()


def expert(split, *refs):
    rows, refs = refs[: 1 + split], refs[1 + split :]
    first, second, away, kept, inner = refs
    tp = lax.axis_index("tp")
    width, hidden = first.shape
    half = width // 2
    chunk = min(512, hidden)
    for c in range(hidden // chunk):
        columns = slice(c * chunk, (c + 1) * chunk)
        if split:
            value = matmul(rows[0][...], first[part(tp, half), columns])
            value = value + matmul(rows[1][...], first[part(1 - tp, half), columns])
        else:
            value = matmul(rows[0][...], first[:, columns])
        inner[:, columns] = jnp.maximum(value, 0.0).astype(LOW)
    away[...] = matmul(inner[...], second[:, part(1 - tp, half)]).astype(LOW)
    kept[...] = matmul(inner[...], second[:, part(tp, half)])


def expert_first(rows, first, second, away, kept, first_here, second_here, inner, arrived):
    tp = lax.axis_index("tp")
    width, hidden = first.shape
    half = width // 2
    chunk = min(512, hidden)
    columns = [slice(c * chunk, (c + 1) * chunk) for c in range(hidden // chunk)]
    loads = [
        pltpu.make_async_copy(first.at[:, c], first_here.at[:, c], arrived.at[i])
        for i, c in enumerate(columns)
    ]
    loads.append(pltpu.make_async_copy(second, second_here, arrived.at[len(columns)]))
    for load in loads:
        load.start()
    for c, load in zip(columns, loads):
        load.wait()
        inner[:, c] = jnp.maximum(matmul(rows[...], first_here[:, c]), 0.0).astype(LOW)
    loads[-1].wait()
    away[...] = matmul(inner[...], second_here[:, part(1 - tp, half)]).astype(LOW)
    kept[...] = matmul(inner[...], second_here[:, part(tp, half)])


def idle():
    pass


def add(kept, arrived, out):
    out[...] = (kept[...] + arrived[...].astype(WIDE)).astype(LOW)


def combine(experts, tokens, high, low, *refs):
    returned, out = refs[:-1], refs[-1]
    tp = lax.axis_index("tp")
    half = out.shape[1]
    mixed = tokens[:, part(tp, half)].astype(WIDE)
    for k in range(experts):
        rows = returned[k][...]
        mixed = mixed + (matmul(high[k], rows) + matmul(low[k], rows))
    out[...] = mixed.astype(LOW)


def project(mine, other, gain, weight, out):
    tp = lax.axis_index("tp")
    half = mine.shape[1]
    own = mine[...].astype(WIDE)
    rest = other[...].astype(WIDE)
    average = (
        jnp.sum(own, axis=-1, keepdims=True) + jnp.sum(rest, axis=-1, keepdims=True)
    ) / (2 * half)
    own = own - average
    rest = rest - average
    spread = (
        jnp.sum(own * own, axis=-1, keepdims=True) + jnp.sum(rest * rest, axis=-1, keepdims=True)
    ) / (2 * half)
    factor = lax.rsqrt(spread + EPS)
    own = (own * factor * gain[:, part(tp, half)]).astype(LOW)
    rest = (rest * factor * gain[:, part(1 - tp, half)]).astype(LOW)
    value = matmul(own, weight[part(tp, half), :]) + matmul(rest, weight[part(1 - tp, half), :])
    out[...] = value.astype(LOW)


def choose(own, beside, *refs):
    sec = lax.axis_index("sec")
    moved, out = refs[:-1], refs[-1]
    for i, source in enumerate((own, beside, *moved)):

        @pl.when(sec == i)
        def _():
            out[...] = source[...]


def attend(
    first, second, queries, upstream, key_w, value_w, away, kept, low_ref, values, keys, dkeys, dvalues
):
    tp = lax.axis_index("tp")
    sec = lax.axis_index("sec")
    token_count, half = first.shape
    width = 2 * half
    scale = 1.0 / math.sqrt(HD)

    @pl.when(sec != 0)
    def _():
        crossed = ((sec > 1) & (sec % 2 == 1)).astype(jnp.int32)
        place = tp ^ crossed
        for weight, target in ((key_w, keys), (value_w, values)):
            value = matmul(first[...], weight[part(place, half), :])
            value = value + matmul(second[...], weight[part(1 - place, half), :])
            target[...] = value.astype(LOW)
        heads = [
            (slice(s * SEQ, (s + 1) * SEQ), slice(h * HD, (h + 1) * HD))
            for s in range(token_count // SEQ)
            for h in range(queries.shape[1] // HD)
        ]
        scores = [matmul(keys[at], queries[at], NT) for at in heads]
        dprobs = [matmul(values[at], upstream[at], NT) for at in heads]
        powers = [jnp.exp(x * scale) for x in scores]
        probs = [x * (1.0 / jnp.sum(x, axis=0, keepdims=True)) for x in powers]
        lows = [x.astype(LOW) for x in probs]
        for at, low in zip(heads, lows):
            dvalues[at] = matmul(low, upstream[at]).astype(LOW)
        rowdots = [jnp.sum(x * y, axis=0, keepdims=True) for x, y in zip(dprobs, probs)]
        dscores = [
            (y * (x - z)).astype(LOW) for x, y, z in zip(dprobs, probs, rowdots)
        ]
        for at, dscore in zip(heads, dscores):
            dkeys[at] = (matmul(dscore, queries[at]) * scale).astype(LOW)
        for i, low in enumerate(lows):
            low_ref[i] = low
        side = sec % 2
        pairs = lax.axis_size("sec") // 2
        block = width // (2 * pairs)
        for target, parity in ((away, 1 - side), (kept, side)):
            for i in range(pairs):
                rows = part(2 * i + parity, block)
                value = matmul(dkeys[...], key_w[rows, :], NT)
                value = value + matmul(dvalues[...], value_w[rows, :], NT)
                target[:, i * block : (i + 1) * block] = value.astype(target.dtype)

    @pl.when(sec == 0)
    def _():
        away[...] = jnp.zeros_like(away)
        kept[...] = jnp.zeros_like(kept)


def contexts(low_ref, values, hidden, out):
    sec = lax.axis_index("sec")
    head_count = values.shape[1] // HD

    @pl.when(sec == 0)
    def _():
        out[...] = hidden[...]

    @pl.when(sec != 0)
    def _():
        for i in range(low_ref.shape[0]):
            s, h = i // head_count, i % head_count
            at = slice(s * SEQ, (s + 1) * SEQ), slice(h * HD, (h + 1) * HD)
            out[at] = matmul(low_ref[i], values[at], TN).astype(LOW)


def gather_term(kept, arrived, own, *sent):
    tp = lax.axis_index("tp")
    here = lax.axis_index("sec") // 2 * lax.axis_size("tp") + tp
    width = own.shape[1]
    for k in range(len(sent) + 1):
        columns = part(here ^ k, width)
        value = kept[:, columns] + arrived[:, columns].astype(WIDE)
        if k == 0:
            own[...] = value
        else:
            sent[k - 1][...] = value.astype(LOW)


def swap(block, axis, step):
    size = lax.axis_size(axis)
    return lax.ppermute(block, axis, [(i, i ^ step) for i in range(size)])


def shards(
    tokens,
    routes,
    gate_weights,
    moe_gain,
    attn_gain,
    expert_in,
    expert_out,
    query_weight,
    key_weight,
    value_weight,
    cotangent,
):
    token_rows = tokens[0]
    route_rows = routes[0].T
    gate_rows = gate_weights[0].T
    token_count, model_width = token_rows.shape
    experts = lax.axis_size("exp")
    sections = lax.axis_size("sec")
    tp_size = lax.axis_size("tp")
    sec = lax.axis_index("sec")
    half = model_width // tp_size
    capacity = 3 * token_count // experts
    weight_first = expert_in[0, 0]
    weight_second = expert_out[0, 0]
    units = weight_first.shape[1]

    middle = max(2, experts // 2 + 1)
    groups = [list(range(middle - 1, 1, -1)), list(range(experts - 1, middle - 1, -1))]
    row_half, row_whole = shape_of((capacity, half)), shape_of((capacity, model_width))
    earlier = call(
        triangle,
        [shape_of((token_count, token_count))],
        [],
        flops=20 * token_count * token_count * model_width,
    )[0]
    *far_rows, near_rows, own_rows = call(
        functools.partial(prepare, experts),
        [row_half] * (experts - 2) + [row_whole] * 2,
        [token_rows, route_rows, moe_gain, earlier],
        [pltpu.VMEM((token_count, model_width), LOW)],
        flops=2 * 3 * token_count * token_count * model_width,
    )
    def hold(array, after):
        return call(idle, [], [], after=after, held=[array])[0]

    def joined(group):
        blocks = [swap(far_rows[k - 2], "exp", k) for k in group]
        return blocks[0] if len(blocks) == 1 else jnp.concatenate(blocks, axis=0)

    def total(away, kept, plain=False):
        arrived = swap(away, "tp", 1)
        if plain:
            return (kept + arrived.astype(WIDE)).astype(LOW)
        return call(add, [shape_of(away.shape)], [kept, arrived])[0]

    def through(rows, after):
        count = rows[0].shape[0]
        return call(
            functools.partial(expert, len(rows) - 1),
            [shape_of((count, half)), shape_of((count, half), WIDE)],
            [*rows, weight_first, weight_second],
            [pltpu.VMEM((count, units), LOW)],
            flops=4 * count * model_width * units,
            limit=24,
            after=after,
        )

    arriving = [joined(groups[0])]
    later = [near_rows] + [far_rows[k - 2] for k in groups[1]]
    loads = max(1, units // 512) + 1
    own_away, own_kept, weight_first, weight_second, *later = call(
        expert_first,
        [
            row_half,
            shape_of((capacity, half), WIDE),
            shape_of(weight_first.shape),
            shape_of(weight_second.shape),
        ],
        [own_rows, weight_first, weight_second],
        [pltpu.VMEM((capacity, units), LOW), pltpu.SemaphoreType.DMA((loads,))],
        flops=4 * capacity * model_width * units,
        remote=(1, 2),
        limit=44,
        held=later,
    )
    near = swap(later[0], "exp", 1)
    for k, rows in zip(groups[1], later[1:]):
        far_rows[k - 2] = rows
    arriving.append(joined(groups[1]))
    returned = {0: total(own_away, own_kept, plain=True)}
    arriving[0] = hold(arriving[0], [own_away])
    others = [swap(arriving[0], "tp", 1)]
    high, low, upstream = call(
        functools.partial(mixing, experts),
        [shape_of((experts, token_count, capacity))] * 2 + [shape_of(cotangent.shape[1:])],
        [route_rows, gate_rows, earlier, cotangent[0]],
        [pltpu.SemaphoreType.DMA],
        remote=(3,),
        after=[arriving[0]],
    )
    others.append(swap(arriving[1], "tp", 1))

    def give_back(group, away, kept):
        mixed = total(away, kept)
        for i, k in enumerate(group):
            block = mixed if len(group) == 1 else mixed[i * capacity : (i + 1) * capacity]
            returned[k] = swap(block, "exp", k)
        return mixed

    away, kept = through([arriving[0], others[0]], [returned[0], high])
    near_away, near_kept = through([near], [away])
    mixed = give_back(groups[0], away, kept)
    returned[1] = swap(total(near_away, near_kept, plain=True), "exp", 1)
    away, kept = through([arriving[1], others[1]], [near_away, mixed])
    give_back(groups[1], away, kept)

    hidden_half = call(
        functools.partial(combine, experts),
        [shape_of((token_count, half))],
        [token_rows, high, low, *(returned[k] for k in range(experts))],
        flops=4 * 3 * token_count * token_count * half,
    )[0]

    hidden_other = swap(hidden_half, "tp", 1)

    def cycle(order, crossed):
        pairs = [(i, i ^ 1) for i in range(sections * tp_size)]
        targets = dict(pairs)
        for a, b in zip(order, order[1:] + order[:1]):
            for t in range(tp_size):
                targets[a * tp_size + t] = b * tp_size + (t ^ crossed if a == 0 else t)
        return lax.ppermute(hidden_half, ("sec", "tp"), list(targets.items()))

    moved = [[cycle([0, 2 * i, 2 * i + 1, 1], 0), cycle([0, 2 * i + 1, 2 * i, 1], 1)] for i in range(1, sections // 2)]
    beside = swap(hidden_half, "sec", 1)
    first = call(choose, [shape_of(hidden_half.shape)], [hidden_other, beside, *sum(moved, [])])[0]
    second = swap(first, "sec", 1)

    local_width = query_weight.shape[2]
    queries = call(
        project,
        [shape_of((token_count, local_width))],
        [hidden_half, hidden_other, attn_gain, query_weight[0]],
        flops=2 * token_count * model_width * local_width,
    )[0]
    heads = token_count // SEQ * (local_width // HD)
    away, kept, lows, values = call(
        attend,
        [
            shape_of((token_count, model_width // 2)),
            shape_of((token_count, model_width // 2), WIDE),
            shape_of((heads, SEQ, SEQ)),
            shape_of((token_count, local_width)),
        ],
        [first, second, queries, upstream, key_weight[0], value_weight[0]],
        [pltpu.VMEM((token_count, local_width), LOW)] * 3,
        flops=10 * token_count * model_width * local_width,
    )
    context = call(
        contexts,
        [shape_of((token_count, local_width))],
        [lows, values, hidden_half],
        flops=2 * token_count * SEQ * local_width,
    )[0]

    own = model_width // (sections * tp_size)
    count = sections // 2 * tp_size
    both = sections * tp_size
    blocks = call(
        gather_term,
        [shape_of((token_count, own), WIDE)] + [shape_of((token_count, own))] * (count - 1),
        [kept, swap(away, "sec", 1)],
    )
    total = blocks[0]
    for k in range(1, count):
        pairs = []
        for i in range(both):
            section, t = i // tp_size, i % tp_size
            target = (section // 2 * tp_size + t) ^ k
            pairs.append((i, (target // tp_size * 2 + section % 2) * tp_size + target % tp_size))
        total = total + lax.ppermute(blocks[k], ("sec", "tp"), pairs).astype(WIDE)
    return (context[None], total.astype(LOW))


def solution(mesh):
    placed = (
        P("sec", "exp", None),
        P("sec", "exp", None),
        P("sec", "exp", None),
        P("sec", None),
        P("sec", None),
        P("sec", "exp", None, "tp"),
        P("sec", "exp", "tp", None),
        P("sec", None, "tp"),
        P("sec", None, "tp"),
        P("sec", None, "tp"),
        P("sec", "exp", "tp"),
    )
    return jax.shard_map(
        shards,
        mesh=mesh,
        in_specs=placed,
        out_specs=(P("sec", "exp", "tp"), P("exp", ("sec", "tp"))),
        check_vma=False,
    )
```

```python
import functools
import math

import jax
import jax.numpy as jnp
from jax import lax
from jax.experimental import pallas as pl
from jax.experimental.pallas import tpu as pltpu
from jax.sharding import PartitionSpec as P

HD = 128
SEQ = 128
EPS = 1e-05

LOW = jnp.bfloat16
WIDE = jnp.float32
VMEM = pl.BlockSpec(memory_space=pltpu.VMEM)
HBM = pl.BlockSpec(memory_space=pltpu.HBM)
ANY = pl.BlockSpec(memory_space=pl.ANY)
NT = (((1,), (1,)), ((), ()))
TN = (((0,), (0,)), ((), ()))


def matmul(a, b, dims=(((1,), (0,)), ((), ()))):
    return lax.dot_general(a, b, dims, preferred_element_type=WIDE)


def call(body, out_shape, inputs, scratch=(), flops=0, limit=16, remote=(), after=(), held=()):
    def size(x):
        return math.prod(x.shape) * jnp.dtype(x.dtype).itemsize

    count, results = len(inputs), len(out_shape)
    extra = len(after) + len(held)

    def run(*refs):
        outs = refs[count + extra : count + extra + results]
        return body(*refs[:count], *outs, *refs[count + extra + results + len(held) :])

    moved = sum(size(x) for x in inputs) + sum(size(x) for x in out_shape)
    return pl.pallas_call(
        run,
        out_shape=[*out_shape, *(shape_of(x.shape, x.dtype) for x in held)],
        in_specs=[HBM if i in remote else VMEM for i in range(count)] + [ANY] * extra,
        out_specs=[VMEM] * results + [ANY] * len(held),
        scratch_shapes=list(scratch),
        input_output_aliases={count + len(after) + i: results + i for i in range(len(held))},
        compiler_params=pltpu.CompilerParams(vmem_limit_bytes=limit * 2**20),
        cost_estimate=pl.CostEstimate(flops=flops, bytes_accessed=moved, transcendentals=0),
    )(*inputs, *after, *held)


def shape_of(dims, kind=LOW):
    return jax.ShapeDtypeStruct(dims, kind)


def part(index, width):
    return pl.ds(pl.multiple_of(index * width, width), width)


def triangle(out):
    source = lax.broadcasted_iota(jnp.int32, out.shape, 0)
    target = lax.broadcasted_iota(jnp.int32, out.shape, 1)
    out[...] = jnp.where(source < target, 1.0, 0.0).astype(LOW)


def places(routes, earlier, me, rows):
    labels = lax.broadcasted_iota(jnp.int32, (rows, 1), 0) ^ me
    first = routes[0:1, :] == labels
    second = routes[1:2, :] == labels
    either = first | second
    before = matmul(jnp.where(either, 1.0, 0.0).astype(LOW), earlier)
    return jnp.where(either, before, -1.0), first, second


def table(place, k, capacity):
    slots = lax.broadcasted_iota(jnp.int32, (capacity, place.shape[1]), 0).astype(WIDE)
    return jnp.where(place[k : k + 1, :] == slots, 1.0, 0.0).astype(LOW)


def prepare(experts, tokens, routes, gain, earlier, *outs):
    far, near, own, normed_ref = outs[:-3], outs[-3], outs[-2], outs[-1]
    me = lax.axis_index("exp")
    tp = lax.axis_index("tp")
    capacity, width = own.shape
    half = width // 2
    wide = tokens[...].astype(WIDE)
    average = jnp.mean(wide, axis=-1, keepdims=True)
    centred = wide - average
    spread = jnp.mean(centred * centred, axis=-1, keepdims=True)
    normed_ref[...] = (centred * lax.rsqrt(spread + EPS) * gain[...]).astype(LOW)
    place, _, _ = places(routes[...], earlier[...], me, max(16, experts))
    normed_half = normed_ref[:, part(tp, half)]
    for k in range(experts - 1, 1, -1):
        far[k - 2][...] = matmul(table(place, k, capacity), normed_half).astype(LOW)
    normed = normed_ref[...]
    near[...] = matmul(table(place, 1, capacity), normed).astype(LOW)
    own[...] = matmul(table(place, 0, capacity), normed).astype(LOW)


def mixing(experts, routes, gates, earlier, upstream, high, low, upstream_here, arrived):
    load = pltpu.make_async_copy(upstream, upstream_here, arrived)
    load.start()
    me = lax.axis_index("exp")
    token_count = routes.shape[1]
    capacity = high.shape[2]
    place, first, second = places(routes[...], earlier[...], me, max(16, experts))
    gate = jnp.where(first, gates[0:1, :], 0.0) + jnp.where(second, gates[1:2, :], 0.0)
    place = place.T
    gate = gate.T
    slots = lax.broadcasted_iota(jnp.int32, (token_count, capacity), 1).astype(WIDE)
    for k in range(experts):
        weight = jnp.where(place[:, k : k + 1] == slots, gate[:, k : k + 1], 0.0)
        upper = weight.astype(LOW)
        high[k] = upper
        low[k] = (weight - upper.astype(WIDE)).astype(LOW)
    load.wait()


def expert(split, *refs):
    rows, refs = refs[: 1 + split], refs[1 + split :]
    first, second, away, kept, inner = refs
    tp = lax.axis_index("tp")
    width, hidden = first.shape
    half = width // 2
    chunk = min(512, hidden)
    for c in range(hidden // chunk):
        columns = slice(c * chunk, (c + 1) * chunk)
        if split:
            value = matmul(rows[0][...], first[part(tp, half), columns])
            value = value + matmul(rows[1][...], first[part(1 - tp, half), columns])
        else:
            value = matmul(rows[0][...], first[:, columns])
        inner[:, columns] = jnp.maximum(value, 0.0).astype(LOW)
    away[...] = matmul(inner[...], second[:, part(1 - tp, half)]).astype(LOW)
    kept[...] = matmul(inner[...], second[:, part(tp, half)])


def expert_first(rows, first, second, away, kept, first_here, second_here, inner, arrived):
    tp = lax.axis_index("tp")
    width, hidden = first.shape
    half = width // 2
    chunk = min(512, hidden)
    columns = [slice(c * chunk, (c + 1) * chunk) for c in range(hidden // chunk)]
    loads = [
        pltpu.make_async_copy(first.at[:, c], first_here.at[:, c], arrived.at[i])
        for i, c in enumerate(columns)
    ]
    loads.append(pltpu.make_async_copy(second, second_here, arrived.at[len(columns)]))
    for load in loads:
        load.start()
    for c, load in zip(columns, loads):
        load.wait()
        inner[:, c] = jnp.maximum(matmul(rows[...], first_here[:, c]), 0.0).astype(LOW)
    loads[-1].wait()
    away[...] = matmul(inner[...], second_here[:, part(1 - tp, half)]).astype(LOW)
    kept[...] = matmul(inner[...], second_here[:, part(tp, half)])


def idle():
    pass


def add(kept, arrived, out):
    out[...] = (kept[...] + arrived[...].astype(WIDE)).astype(LOW)


def combine(experts, tokens, high, low, *refs):
    returned, out = refs[:-1], refs[-1]
    tp = lax.axis_index("tp")
    half = out.shape[1]
    mixed = tokens[:, part(tp, half)].astype(WIDE)
    for k in range(experts):
        rows = returned[k][...]
        mixed = mixed + (matmul(high[k], rows) + matmul(low[k], rows))
    out[...] = mixed.astype(LOW)


def project(mine, other, gain, weight, out):
    tp = lax.axis_index("tp")
    half = mine.shape[1]
    own = mine[...].astype(WIDE)
    rest = other[...].astype(WIDE)
    average = (
        jnp.sum(own, axis=-1, keepdims=True) + jnp.sum(rest, axis=-1, keepdims=True)
    ) / (2 * half)
    own = own - average
    rest = rest - average
    spread = (
        jnp.sum(own * own, axis=-1, keepdims=True) + jnp.sum(rest * rest, axis=-1, keepdims=True)
    ) / (2 * half)
    factor = lax.rsqrt(spread + EPS)
    own = (own * factor * gain[:, part(tp, half)]).astype(LOW)
    rest = (rest * factor * gain[:, part(1 - tp, half)]).astype(LOW)
    value = matmul(own, weight[part(tp, half), :]) + matmul(rest, weight[part(1 - tp, half), :])
    out[...] = value.astype(LOW)


def choose(own, beside, *refs):
    sec = lax.axis_index("sec")
    moved, out = refs[:-1], refs[-1]
    for i, source in enumerate((own, beside, *moved)):

        @pl.when(sec == i)
        def _():
            out[...] = source[...]


def attend(
    first, second, queries, upstream, key_w, value_w, away, kept, low_ref, values, keys, dkeys, dvalues
):
    tp = lax.axis_index("tp")
    sec = lax.axis_index("sec")
    token_count, half = first.shape
    width = 2 * half
    scale = 1.0 / math.sqrt(HD)

    @pl.when(sec != 0)
    def _():
        crossed = ((sec > 1) & (sec % 2 == 1)).astype(jnp.int32)
        place = tp ^ crossed
        for weight, target in ((key_w, keys), (value_w, values)):
            value = matmul(first[...], weight[part(place, half), :])
            value = value + matmul(second[...], weight[part(1 - place, half), :])
            target[...] = value.astype(LOW)
        heads = [
            (slice(s * SEQ, (s + 1) * SEQ), slice(h * HD, (h + 1) * HD))
            for s in range(token_count // SEQ)
            for h in range(queries.shape[1] // HD)
        ]
        scores = [matmul(keys[at], queries[at], NT) for at in heads]
        dprobs = [matmul(values[at], upstream[at], NT) for at in heads]
        powers = [jnp.exp(x * scale) for x in scores]
        probs = [x * (1.0 / jnp.sum(x, axis=0, keepdims=True)) for x in powers]
        lows = [x.astype(LOW) for x in probs]
        for at, low in zip(heads, lows):
            dvalues[at] = matmul(low, upstream[at]).astype(LOW)
        rowdots = [jnp.sum(x * y, axis=0, keepdims=True) for x, y in zip(dprobs, probs)]
        dscores = [
            (y * (x - z)).astype(LOW) for x, y, z in zip(dprobs, probs, rowdots)
        ]
        for at, dscore in zip(heads, dscores):
            dkeys[at] = (matmul(dscore, queries[at]) * scale).astype(LOW)
        for i, low in enumerate(lows):
            low_ref[i] = low
        side = sec % 2
        pairs = lax.axis_size("sec") // 2
        block = width // (2 * pairs)
        for target, parity in ((away, 1 - side), (kept, side)):
            for i in range(pairs):
                rows = part(2 * i + parity, block)
                value = matmul(dkeys[...], key_w[rows, :], NT)
                value = value + matmul(dvalues[...], value_w[rows, :], NT)
                target[:, i * block : (i + 1) * block] = value.astype(target.dtype)

    @pl.when(sec == 0)
    def _():
        away[...] = jnp.zeros_like(away)
        kept[...] = jnp.zeros_like(kept)


def contexts(low_ref, values, hidden, out):
    sec = lax.axis_index("sec")
    head_count = values.shape[1] // HD

    @pl.when(sec == 0)
    def _():
        out[...] = hidden[...]

    @pl.when(sec != 0)
    def _():
        for i in range(low_ref.shape[0]):
            s, h = i // head_count, i % head_count
            at = slice(s * SEQ, (s + 1) * SEQ), slice(h * HD, (h + 1) * HD)
            out[at] = matmul(low_ref[i], values[at], TN).astype(LOW)


def gather_term(kept, arrived, own, *sent):
    tp = lax.axis_index("tp")
    here = lax.axis_index("sec") // 2 * lax.axis_size("tp") + tp
    width = own.shape[1]
    for k in range(len(sent) + 1):
        columns = part(here ^ k, width)
        value = kept[:, columns] + arrived[:, columns].astype(WIDE)
        if k == 0:
            own[...] = value
        else:
            sent[k - 1][...] = value.astype(LOW)


def swap(block, axis, step):
    size = lax.axis_size(axis)
    return lax.ppermute(block, axis, [(i, i ^ step) for i in range(size)])


def shards(
    tokens,
    routes,
    gate_weights,
    moe_gain,
    attn_gain,
    expert_in,
    expert_out,
    query_weight,
    key_weight,
    value_weight,
    cotangent,
):
    token_rows = tokens[0]
    route_rows = routes[0].T
    gate_rows = gate_weights[0].T
    token_count, model_width = token_rows.shape
    experts = lax.axis_size("exp")
    sections = lax.axis_size("sec")
    tp_size = lax.axis_size("tp")
    sec = lax.axis_index("sec")
    half = model_width // tp_size
    capacity = 3 * token_count // experts
    weight_first = expert_in[0, 0]
    weight_second = expert_out[0, 0]
    units = weight_first.shape[1]

    middle = max(2, experts // 2 + 1)
    groups = [list(range(middle - 1, 1, -1)), list(range(experts - 1, middle - 1, -1))]
    row_half, row_whole = shape_of((capacity, half)), shape_of((capacity, model_width))
    earlier = call(
        triangle,
        [shape_of((token_count, token_count))],
        [],
        flops=20 * token_count * token_count * model_width,
    )[0]
    *far_rows, near_rows, own_rows = call(
        functools.partial(prepare, experts),
        [row_half] * (experts - 2) + [row_whole] * 2,
        [token_rows, route_rows, moe_gain, earlier],
        [pltpu.VMEM((token_count, model_width), LOW)],
        flops=2 * 3 * token_count * token_count * model_width,
    )
    def hold(array, after):
        return call(idle, [], [], after=after, held=[array])[0]

    def joined(group):
        blocks = [swap(far_rows[k - 2], "exp", k) for k in group]
        return blocks[0] if len(blocks) == 1 else jnp.concatenate(blocks, axis=0)

    def total(away, kept, plain=False):
        arrived = swap(away, "tp", 1)
        if plain:
            return (kept + arrived.astype(WIDE)).astype(LOW)
        return call(add, [shape_of(away.shape)], [kept, arrived])[0]

    def through(rows, after):
        count = rows[0].shape[0]
        return call(
            functools.partial(expert, len(rows) - 1),
            [shape_of((count, half)), shape_of((count, half), WIDE)],
            [*rows, weight_first, weight_second],
            [pltpu.VMEM((count, units), LOW)],
            flops=4 * count * model_width * units,
            limit=24,
            after=after,
        )

    arriving = [joined(groups[0])]
    near = swap(near_rows, "exp", 1)
    later = [far_rows[k - 2] for k in groups[1]]
    loads = max(1, units // 512) + 1
    own_away, own_kept, weight_first, weight_second, *later = call(
        expert_first,
        [
            row_half,
            shape_of((capacity, half), WIDE),
            shape_of(weight_first.shape),
            shape_of(weight_second.shape),
        ],
        [own_rows, weight_first, weight_second],
        [pltpu.VMEM((capacity, units), LOW), pltpu.SemaphoreType.DMA((loads,))],
        flops=4 * capacity * model_width * units,
        remote=(1, 2),
        limit=44,
        held=later,
    )
    for k, rows in zip(groups[1], later):
        far_rows[k - 2] = rows
    arriving.append(joined(groups[1]))
    returned = {0: total(own_away, own_kept)}
    arriving[0] = hold(arriving[0], [own_away])
    others = [swap(arriving[0], "tp", 1)]
    high, low, upstream = call(
        functools.partial(mixing, experts),
        [shape_of((experts, token_count, capacity))] * 2 + [shape_of(cotangent.shape[1:])],
        [route_rows, gate_rows, earlier, cotangent[0]],
        [pltpu.SemaphoreType.DMA],
        remote=(3,),
        after=[arriving[0]],
    )
    others.append(swap(arriving[1], "tp", 1))

    def give_back(group, away, kept):
        mixed = total(away, kept)
        for i, k in enumerate(group):
            block = mixed if len(group) == 1 else mixed[i * capacity : (i + 1) * capacity]
            returned[k] = swap(block, "exp", k)
        return mixed

    away, kept = through([arriving[0], others[0]], [returned[0], high])
    near_away, near_kept = through([near], [away])
    mixed = give_back(groups[0], away, kept)
    returned[1] = swap(total(near_away, near_kept, plain=True), "exp", 1)
    away, kept = through([arriving[1], others[1]], [near_away, mixed])
    give_back(groups[1], away, kept)

    hidden_half = call(
        functools.partial(combine, experts),
        [shape_of((token_count, half))],
        [token_rows, high, low, *(returned[k] for k in range(experts))],
        flops=4 * 3 * token_count * token_count * half,
    )[0]

    hidden_other = swap(hidden_half, "tp", 1)

    def cycle(order, crossed):
        pairs = [(i, i ^ 1) for i in range(sections * tp_size)]
        targets = dict(pairs)
        for a, b in zip(order, order[1:] + order[:1]):
            for t in range(tp_size):
                targets[a * tp_size + t] = b * tp_size + (t ^ crossed if a == 0 else t)
        return lax.ppermute(hidden_half, ("sec", "tp"), list(targets.items()))

    moved = [[cycle([0, 2 * i, 2 * i + 1, 1], 0), cycle([0, 2 * i + 1, 2 * i, 1], 1)] for i in range(1, sections // 2)]
    beside = swap(hidden_half, "sec", 1)
    first = call(choose, [shape_of(hidden_half.shape)], [hidden_other, beside, *sum(moved, [])])[0]
    second = swap(first, "sec", 1)

    local_width = query_weight.shape[2]
    queries = call(
        project,
        [shape_of((token_count, local_width))],
        [hidden_half, hidden_other, attn_gain, query_weight[0]],
        flops=2 * token_count * model_width * local_width,
    )[0]
    heads = token_count // SEQ * (local_width // HD)
    away, kept, lows, values = call(
        attend,
        [
            shape_of((token_count, model_width // 2)),
            shape_of((token_count, model_width // 2), WIDE),
            shape_of((heads, SEQ, SEQ)),
            shape_of((token_count, local_width)),
        ],
        [first, second, queries, upstream, key_weight[0], value_weight[0]],
        [pltpu.VMEM((token_count, local_width), LOW)] * 3,
        flops=10 * token_count * model_width * local_width,
    )
    context = call(
        contexts,
        [shape_of((token_count, local_width))],
        [lows, values, hidden_half],
        flops=2 * token_count * SEQ * local_width,
    )[0]

    own = model_width // (sections * tp_size)
    count = sections // 2 * tp_size
    both = sections * tp_size
    blocks = call(
        gather_term,
        [shape_of((token_count, own), WIDE)] + [shape_of((token_count, own))] * (count - 1),
        [kept, swap(away, "sec", 1)],
    )
    total = blocks[0]
    for k in range(1, count):
        pairs = []
        for i in range(both):
            section, t = i // tp_size, i % tp_size
            target = (section // 2 * tp_size + t) ^ k
            pairs.append((i, (target // tp_size * 2 + section % 2) * tp_size + target % tp_size))
        total = total + lax.ppermute(blocks[k], ("sec", "tp"), pairs).astype(WIDE)
    return (context[None], total.astype(LOW))


def solution(mesh):
    placed = (
        P("sec", "exp", None),
        P("sec", "exp", None),
        P("sec", "exp", None),
        P("sec", None),
        P("sec", None),
        P("sec", "exp", None, "tp"),
        P("sec", "exp", "tp", None),
        P("sec", None, "tp"),
        P("sec", None, "tp"),
        P("sec", None, "tp"),
        P("sec", "exp", "tp"),
    )
    return jax.shard_map(
        shards,
        mesh=mesh,
        in_specs=placed,
        out_specs=(P("sec", "exp", "tp"), P("exp", ("sec", "tp"))),
        check_vma=False,
    )
```

```python
import functools
import math

import jax
import jax.numpy as jnp
from jax import lax
from jax.experimental import pallas as pl
from jax.experimental.pallas import tpu as pltpu
from jax.sharding import PartitionSpec as P

HD = 128
SEQ = 128
EPS = 1e-05

LOW = jnp.bfloat16
WIDE = jnp.float32
VMEM = pl.BlockSpec(memory_space=pltpu.VMEM)
HBM = pl.BlockSpec(memory_space=pltpu.HBM)
ANY = pl.BlockSpec(memory_space=pl.ANY)
NT = (((1,), (1,)), ((), ()))
TN = (((0,), (0,)), ((), ()))


def matmul(a, b, dims=(((1,), (0,)), ((), ()))):
    return lax.dot_general(a, b, dims, preferred_element_type=WIDE)


def call(body, out_shape, inputs, scratch=(), flops=0, limit=16, remote=(), after=(), held=()):
    def size(x):
        return math.prod(x.shape) * jnp.dtype(x.dtype).itemsize

    count, results = len(inputs), len(out_shape)
    extra = len(after) + len(held)

    def run(*refs):
        outs = refs[count + extra : count + extra + results]
        return body(*refs[:count], *outs, *refs[count + extra + results + len(held) :])

    moved = sum(size(x) for x in inputs) + sum(size(x) for x in out_shape)
    return pl.pallas_call(
        run,
        out_shape=[*out_shape, *(shape_of(x.shape, x.dtype) for x in held)],
        in_specs=[HBM if i in remote else VMEM for i in range(count)] + [ANY] * extra,
        out_specs=[VMEM] * results + [ANY] * len(held),
        scratch_shapes=list(scratch),
        input_output_aliases={count + len(after) + i: results + i for i in range(len(held))},
        compiler_params=pltpu.CompilerParams(vmem_limit_bytes=limit * 2**20),
        cost_estimate=pl.CostEstimate(flops=flops, bytes_accessed=moved, transcendentals=0),
    )(*inputs, *after, *held)


def shape_of(dims, kind=LOW):
    return jax.ShapeDtypeStruct(dims, kind)


def part(index, width):
    return pl.ds(pl.multiple_of(index * width, width), width)


def triangle(out):
    source = lax.broadcasted_iota(jnp.int32, out.shape, 0)
    target = lax.broadcasted_iota(jnp.int32, out.shape, 1)
    out[...] = jnp.where(source < target, 1.0, 0.0).astype(LOW)


def places(routes, earlier, me, rows):
    labels = lax.broadcasted_iota(jnp.int32, (rows, 1), 0) ^ me
    first = routes[0:1, :] == labels
    second = routes[1:2, :] == labels
    either = first | second
    before = matmul(jnp.where(either, 1.0, 0.0).astype(LOW), earlier)
    return jnp.where(either, before, -1.0), first, second


def table(place, k, capacity):
    slots = lax.broadcasted_iota(jnp.int32, (capacity, place.shape[1]), 0).astype(WIDE)
    return jnp.where(place[k : k + 1, :] == slots, 1.0, 0.0).astype(LOW)


def prepare(experts, tokens, routes, gain, earlier, *outs):
    far, near, own, normed_ref = outs[:-3], outs[-3], outs[-2], outs[-1]
    me = lax.axis_index("exp")
    tp = lax.axis_index("tp")
    capacity, width = own.shape
    half = width // 2
    wide = tokens[...].astype(WIDE)
    average = jnp.mean(wide, axis=-1, keepdims=True)
    centred = wide - average
    spread = jnp.mean(centred * centred, axis=-1, keepdims=True)
    normed_ref[...] = (centred * lax.rsqrt(spread + EPS) * gain[...]).astype(LOW)
    place, _, _ = places(routes[...], earlier[...], me, max(16, experts))
    normed_half = normed_ref[:, part(tp, half)]
    for k in range(experts - 1, 1, -1):
        far[k - 2][...] = matmul(table(place, k, capacity), normed_half).astype(LOW)
    normed = normed_ref[...]
    near[...] = matmul(table(place, 1, capacity), normed).astype(LOW)
    own[...] = matmul(table(place, 0, capacity), normed).astype(LOW)


def mixing(experts, routes, gates, earlier, upstream, high, low, upstream_here, arrived):
    load = pltpu.make_async_copy(upstream, upstream_here, arrived)
    load.start()
    me = lax.axis_index("exp")
    token_count = routes.shape[1]
    capacity = high.shape[2]
    place, first, second = places(routes[...], earlier[...], me, max(16, experts))
    gate = jnp.where(first, gates[0:1, :], 0.0) + jnp.where(second, gates[1:2, :], 0.0)
    place = place.T
    gate = gate.T
    slots = lax.broadcasted_iota(jnp.int32, (token_count, capacity), 1).astype(WIDE)
    for k in range(experts):
        weight = jnp.where(place[:, k : k + 1] == slots, gate[:, k : k + 1], 0.0)
        upper = weight.astype(LOW)
        high[k] = upper
        low[k] = (weight - upper.astype(WIDE)).astype(LOW)
    load.wait()


def expert(split, *refs):
    rows, refs = refs[: 1 + split], refs[1 + split :]
    first, second, away, kept, inner = refs
    tp = lax.axis_index("tp")
    width, hidden = first.shape
    half = width // 2
    chunk = min(512, hidden)
    for c in range(hidden // chunk):
        columns = slice(c * chunk, (c + 1) * chunk)
        if split:
            value = matmul(rows[0][...], first[part(tp, half), columns])
            value = value + matmul(rows[1][...], first[part(1 - tp, half), columns])
        else:
            value = matmul(rows[0][...], first[:, columns])
        inner[:, columns] = jnp.maximum(value, 0.0).astype(LOW)
    away[...] = matmul(inner[...], second[:, part(1 - tp, half)]).astype(LOW)
    kept[...] = matmul(inner[...], second[:, part(tp, half)])


def expert_first(rows, first, second, away, kept, first_here, second_here, inner, arrived):
    tp = lax.axis_index("tp")
    width, hidden = first.shape
    half = width // 2
    chunk = min(512, hidden)
    columns = [slice(c * chunk, (c + 1) * chunk) for c in range(hidden // chunk)]
    loads = [
        pltpu.make_async_copy(first.at[:, c], first_here.at[:, c], arrived.at[i])
        for i, c in enumerate(columns)
    ]
    loads.append(pltpu.make_async_copy(second, second_here, arrived.at[len(columns)]))
    for load in loads:
        load.start()
    for c, load in zip(columns, loads):
        load.wait()
        inner[:, c] = jnp.maximum(matmul(rows[...], first_here[:, c]), 0.0).astype(LOW)
    loads[-1].wait()
    away[...] = matmul(inner[...], second_here[:, part(1 - tp, half)]).astype(LOW)
    kept[...] = matmul(inner[...], second_here[:, part(tp, half)])


def idle():
    pass


def add(kept, arrived, out):
    out[...] = (kept[...] + arrived[...].astype(WIDE)).astype(LOW)


def combine(order, base, high, low, *refs):
    returned, out = refs[:-1], refs[-1]
    half = out.shape[1]
    if base.shape[1] == half:
        mixed = base[...]
    else:
        mixed = base[:, part(lax.axis_index("tp"), half)].astype(WIDE)
    for k, block in zip(order, returned, strict=True):
        rows = block[...]
        mixed = mixed + (matmul(high[k], rows) + matmul(low[k], rows))
    out[...] = mixed.astype(out.dtype)


def project(mine, other, gain, weight, out):
    tp = lax.axis_index("tp")
    half = mine.shape[1]
    own = mine[...].astype(WIDE)
    rest = other[...].astype(WIDE)
    average = (
        jnp.sum(own, axis=-1, keepdims=True) + jnp.sum(rest, axis=-1, keepdims=True)
    ) / (2 * half)
    own = own - average
    rest = rest - average
    spread = (
        jnp.sum(own * own, axis=-1, keepdims=True) + jnp.sum(rest * rest, axis=-1, keepdims=True)
    ) / (2 * half)
    factor = lax.rsqrt(spread + EPS)
    own = (own * factor * gain[:, part(tp, half)]).astype(LOW)
    rest = (rest * factor * gain[:, part(1 - tp, half)]).astype(LOW)
    value = matmul(own, weight[part(tp, half), :]) + matmul(rest, weight[part(1 - tp, half), :])
    out[...] = value.astype(LOW)


def choose(own, beside, *refs):
    sec = lax.axis_index("sec")
    moved, out = refs[:-1], refs[-1]
    for i, source in enumerate((own, beside, *moved)):

        @pl.when(sec == i)
        def _():
            out[...] = source[...]


def attend(
    first, second, queries, upstream, key_w, value_w, away, kept, low_ref, values, keys, dkeys, dvalues
):
    tp = lax.axis_index("tp")
    sec = lax.axis_index("sec")
    token_count, half = first.shape
    width = 2 * half
    scale = 1.0 / math.sqrt(HD)

    @pl.when(sec != 0)
    def _():
        crossed = ((sec > 1) & (sec % 2 == 1)).astype(jnp.int32)
        place = tp ^ crossed
        for weight, target in ((key_w, keys), (value_w, values)):
            value = matmul(first[...], weight[part(place, half), :])
            value = value + matmul(second[...], weight[part(1 - place, half), :])
            target[...] = value.astype(LOW)
        heads = [
            (slice(s * SEQ, (s + 1) * SEQ), slice(h * HD, (h + 1) * HD))
            for s in range(token_count // SEQ)
            for h in range(queries.shape[1] // HD)
        ]
        scores = [matmul(keys[at], queries[at], NT) for at in heads]
        dprobs = [matmul(values[at], upstream[at], NT) for at in heads]
        powers = [jnp.exp(x * scale) for x in scores]
        probs = [x * (1.0 / jnp.sum(x, axis=0, keepdims=True)) for x in powers]
        lows = [x.astype(LOW) for x in probs]
        for at, low in zip(heads, lows):
            dvalues[at] = matmul(low, upstream[at]).astype(LOW)
        rowdots = [jnp.sum(x * y, axis=0, keepdims=True) for x, y in zip(dprobs, probs)]
        dscores = [
            (y * (x - z)).astype(LOW) for x, y, z in zip(dprobs, probs, rowdots)
        ]
        for at, dscore in zip(heads, dscores):
            dkeys[at] = (matmul(dscore, queries[at]) * scale).astype(LOW)
        for i, low in enumerate(lows):
            low_ref[i] = low
        side = sec % 2
        pairs = lax.axis_size("sec") // 2
        block = width // (2 * pairs)
        for target, parity in ((away, 1 - side), (kept, side)):
            for i in range(pairs):
                rows = part(2 * i + parity, block)
                value = matmul(dkeys[...], key_w[rows, :], NT)
                value = value + matmul(dvalues[...], value_w[rows, :], NT)
                target[:, i * block : (i + 1) * block] = value.astype(target.dtype)

    @pl.when(sec == 0)
    def _():
        away[...] = jnp.zeros_like(away)
        kept[...] = jnp.zeros_like(kept)


def contexts(low_ref, values, hidden, out):
    sec = lax.axis_index("sec")
    head_count = values.shape[1] // HD

    @pl.when(sec == 0)
    def _():
        out[...] = hidden[...]

    @pl.when(sec != 0)
    def _():
        for i in range(low_ref.shape[0]):
            s, h = i // head_count, i % head_count
            at = slice(s * SEQ, (s + 1) * SEQ), slice(h * HD, (h + 1) * HD)
            out[at] = matmul(low_ref[i], values[at], TN).astype(LOW)


def gather_term(kept, arrived, own, *sent):
    tp = lax.axis_index("tp")
    here = lax.axis_index("sec") // 2 * lax.axis_size("tp") + tp
    width = own.shape[1]
    for k in range(len(sent) + 1):
        columns = part(here ^ k, width)
        value = kept[:, columns] + arrived[:, columns].astype(WIDE)
        if k == 0:
            own[...] = value
        else:
            sent[k - 1][...] = value.astype(LOW)


def swap(block, axis, step):
    size = lax.axis_size(axis)
    return lax.ppermute(block, axis, [(i, i ^ step) for i in range(size)])


def shards(
    tokens,
    routes,
    gate_weights,
    moe_gain,
    attn_gain,
    expert_in,
    expert_out,
    query_weight,
    key_weight,
    value_weight,
    cotangent,
):
    token_rows = tokens[0]
    route_rows = routes[0].T
    gate_rows = gate_weights[0].T
    token_count, model_width = token_rows.shape
    experts = lax.axis_size("exp")
    sections = lax.axis_size("sec")
    tp_size = lax.axis_size("tp")
    sec = lax.axis_index("sec")
    half = model_width // tp_size
    capacity = 3 * token_count // experts
    weight_first = expert_in[0, 0]
    weight_second = expert_out[0, 0]
    units = weight_first.shape[1]

    middle = max(2, experts // 2 + 1)
    groups = [list(range(middle - 1, 1, -1)), list(range(experts - 1, middle - 1, -1))]
    row_half, row_whole = shape_of((capacity, half)), shape_of((capacity, model_width))
    earlier = call(
        triangle,
        [shape_of((token_count, token_count))],
        [],
        flops=20 * token_count * token_count * model_width,
    )[0]
    *far_rows, near_rows, own_rows = call(
        functools.partial(prepare, experts),
        [row_half] * (experts - 2) + [row_whole] * 2,
        [token_rows, route_rows, moe_gain, earlier],
        [pltpu.VMEM((token_count, model_width), LOW)],
        flops=2 * 3 * token_count * token_count * model_width,
    )
    def hold(array, after):
        return call(idle, [], [], after=after, held=[array])[0]

    def joined(group):
        blocks = [swap(far_rows[k - 2], "exp", k) for k in group]
        return blocks[0] if len(blocks) == 1 else jnp.concatenate(blocks, axis=0)

    def total(away, kept, plain=False):
        arrived = swap(away, "tp", 1)
        if plain:
            return (kept + arrived.astype(WIDE)).astype(LOW)
        return call(add, [shape_of(away.shape)], [kept, arrived])[0]

    def through(rows, after):
        count = rows[0].shape[0]
        return call(
            functools.partial(expert, len(rows) - 1),
            [shape_of((count, half)), shape_of((count, half), WIDE)],
            [*rows, weight_first, weight_second],
            [pltpu.VMEM((count, units), LOW)],
            flops=4 * count * model_width * units,
            limit=24,
            after=after,
        )

    arriving = [joined(groups[0])]
    near = swap(near_rows, "exp", 1)
    later = [far_rows[k - 2] for k in groups[1]]
    loads = max(1, units // 512) + 1
    own_away, own_kept, weight_first, weight_second, *later = call(
        expert_first,
        [
            row_half,
            shape_of((capacity, half), WIDE),
            shape_of(weight_first.shape),
            shape_of(weight_second.shape),
        ],
        [own_rows, weight_first, weight_second],
        [pltpu.VMEM((capacity, units), LOW), pltpu.SemaphoreType.DMA((loads,))],
        flops=4 * capacity * model_width * units,
        remote=(1, 2),
        limit=44,
        held=later,
    )
    for k, rows in zip(groups[1], later):
        far_rows[k - 2] = rows
    arriving.append(joined(groups[1]))
    returned = {0: total(own_away, own_kept, plain=True)}
    arriving[0] = hold(arriving[0], [own_away])
    others = [swap(arriving[0], "tp", 1)]
    high, low, upstream = call(
        functools.partial(mixing, experts),
        [shape_of((experts, token_count, capacity))] * 2 + [shape_of(cotangent.shape[1:])],
        [route_rows, gate_rows, earlier, cotangent[0]],
        [pltpu.SemaphoreType.DMA],
        remote=(3,),
        after=[arriving[0]],
    )
    others.append(swap(arriving[1], "tp", 1))

    def give_back(group, away, kept):
        mixed = total(away, kept, plain=True)
        for i, k in enumerate(group):
            block = mixed if len(group) == 1 else mixed[i * capacity : (i + 1) * capacity]
            returned[k] = swap(block, "exp", k)
        return mixed

    away, kept = through([arriving[0], others[0]], [returned[0], high])
    mixed = give_back(groups[0], away, kept)
    away, kept = through([arriving[1], others[1]], [mixed])
    near_away, near_kept = through([near], [away])
    give_back(groups[1], away, kept)
    there, rest = [0, *groups[0]], [1, *groups[1]]
    so_far, near_away = call(
        functools.partial(combine, there),
        [shape_of((token_count, half), WIDE)],
        [token_rows, high, low, *(returned[k] for k in there)],
        flops=4 * len(there) * token_count * capacity * half,
        held=[near_away],
    )
    returned[1] = swap(total(near_away, near_kept), "exp", 1)
    hidden_half = call(
        functools.partial(combine, rest),
        [shape_of((token_count, half))],
        [so_far, high, low, *(returned[k] for k in rest)],
        flops=4 * len(rest) * token_count * capacity * half,
    )[0]

    hidden_other = swap(hidden_half, "tp", 1)

    def cycle(order, crossed):
        pairs = [(i, i ^ 1) for i in range(sections * tp_size)]
        targets = dict(pairs)
        for a, b in zip(order, order[1:] + order[:1]):
            for t in range(tp_size):
                targets[a * tp_size + t] = b * tp_size + (t ^ crossed if a == 0 else t)
        return lax.ppermute(hidden_half, ("sec", "tp"), list(targets.items()))

    moved = [[cycle([0, 2 * i, 2 * i + 1, 1], 0), cycle([0, 2 * i + 1, 2 * i, 1], 1)] for i in range(1, sections // 2)]
    beside = swap(hidden_half, "sec", 1)
    first = call(choose, [shape_of(hidden_half.shape)], [hidden_other, beside, *sum(moved, [])])[0]
    second = swap(first, "sec", 1)

    local_width = query_weight.shape[2]
    queries = call(
        project,
        [shape_of((token_count, local_width))],
        [hidden_half, hidden_other, attn_gain, query_weight[0]],
        flops=2 * token_count * model_width * local_width,
    )[0]
    heads = token_count // SEQ * (local_width // HD)
    away, kept, lows, values = call(
        attend,
        [
            shape_of((token_count, model_width // 2)),
            shape_of((token_count, model_width // 2), WIDE),
            shape_of((heads, SEQ, SEQ)),
            shape_of((token_count, local_width)),
        ],
        [first, second, queries, upstream, key_weight[0], value_weight[0]],
        [pltpu.VMEM((token_count, local_width), LOW)] * 3,
        flops=10 * token_count * model_width * local_width,
    )
    context = call(
        contexts,
        [shape_of((token_count, local_width))],
        [lows, values, hidden_half],
        flops=2 * token_count * SEQ * local_width,
    )[0]

    own = model_width // (sections * tp_size)
    count = sections // 2 * tp_size
    both = sections * tp_size
    blocks = call(
        gather_term,
        [shape_of((token_count, own), WIDE)] + [shape_of((token_count, own))] * (count - 1),
        [kept, swap(away, "sec", 1)],
    )
    total = blocks[0]
    for k in range(1, count):
        pairs = []
        for i in range(both):
            section, t = i // tp_size, i % tp_size
            target = (section // 2 * tp_size + t) ^ k
            pairs.append((i, (target // tp_size * 2 + section % 2) * tp_size + target % tp_size))
        total = total + lax.ppermute(blocks[k], ("sec", "tp"), pairs).astype(WIDE)
    return (context[None], total.astype(LOW))


def solution(mesh):
    placed = (
        P("sec", "exp", None),
        P("sec", "exp", None),
        P("sec", "exp", None),
        P("sec", None),
        P("sec", None),
        P("sec", "exp", None, "tp"),
        P("sec", "exp", "tp", None),
        P("sec", None, "tp"),
        P("sec", None, "tp"),
        P("sec", None, "tp"),
        P("sec", "exp", "tp"),
    )
    return jax.shard_map(
        shards,
        mesh=mesh,
        in_specs=placed,
        out_specs=(P("sec", "exp", "tp"), P("exp", ("sec", "tp"))),
        check_vma=False,
    )
```

```python
import functools
import math

import jax
import jax.numpy as jnp
from jax import lax
from jax.experimental import pallas as pl
from jax.experimental.pallas import tpu as pltpu
from jax.sharding import PartitionSpec as P

HD = 128
SEQ = 128
EPS = 1e-05

LOW = jnp.bfloat16
WIDE = jnp.float32
VMEM = pl.BlockSpec(memory_space=pltpu.VMEM)
HBM = pl.BlockSpec(memory_space=pltpu.HBM)
ANY = pl.BlockSpec(memory_space=pl.ANY)
NT = (((1,), (1,)), ((), ()))
TN = (((0,), (0,)), ((), ()))


def matmul(a, b, dims=(((1,), (0,)), ((), ()))):
    return lax.dot_general(a, b, dims, preferred_element_type=WIDE)


def call(body, out_shape, inputs, scratch=(), flops=0, limit=16, remote=(), after=(), held=()):
    def size(x):
        return math.prod(x.shape) * jnp.dtype(x.dtype).itemsize

    count, results = len(inputs), len(out_shape)
    extra = len(after) + len(held)

    def run(*refs):
        outs = refs[count + extra : count + extra + results]
        return body(*refs[:count], *outs, *refs[count + extra + results + len(held) :])

    moved = sum(size(x) for x in inputs) + sum(size(x) for x in out_shape)
    return pl.pallas_call(
        run,
        out_shape=[*out_shape, *(shape_of(x.shape, x.dtype) for x in held)],
        in_specs=[HBM if i in remote else VMEM for i in range(count)] + [ANY] * extra,
        out_specs=[VMEM] * results + [ANY] * len(held),
        scratch_shapes=list(scratch),
        input_output_aliases={count + len(after) + i: results + i for i in range(len(held))},
        compiler_params=pltpu.CompilerParams(vmem_limit_bytes=limit * 2**20),
        cost_estimate=pl.CostEstimate(flops=flops, bytes_accessed=moved, transcendentals=0),
    )(*inputs, *after, *held)


def shape_of(dims, kind=LOW):
    return jax.ShapeDtypeStruct(dims, kind)


def part(index, width):
    return pl.ds(pl.multiple_of(index * width, width), width)


def triangle(out):
    source = lax.broadcasted_iota(jnp.int32, out.shape, 0)
    target = lax.broadcasted_iota(jnp.int32, out.shape, 1)
    out[...] = jnp.where(source < target, 1.0, 0.0).astype(LOW)


def places(routes, earlier, me, rows):
    labels = lax.broadcasted_iota(jnp.int32, (rows, 1), 0) ^ me
    first = routes[0:1, :] == labels
    second = routes[1:2, :] == labels
    either = first | second
    before = matmul(jnp.where(either, 1.0, 0.0).astype(LOW), earlier)
    return jnp.where(either, before, -1.0), first, second


def table(place, k, capacity):
    slots = lax.broadcasted_iota(jnp.int32, (capacity, place.shape[1]), 0).astype(WIDE)
    return jnp.where(place[k : k + 1, :] == slots, 1.0, 0.0).astype(LOW)


def prepare(experts, tokens, routes, gain, earlier, *outs):
    far, near, own, normed_ref = outs[:-3], outs[-3], outs[-2], outs[-1]
    me = lax.axis_index("exp")
    tp = lax.axis_index("tp")
    capacity, width = own.shape
    half = width // 2
    wide = tokens[...].astype(WIDE)
    average = jnp.mean(wide, axis=-1, keepdims=True)
    centred = wide - average
    spread = jnp.mean(centred * centred, axis=-1, keepdims=True)
    normed_ref[...] = (centred * lax.rsqrt(spread + EPS) * gain[...]).astype(LOW)
    place, _, _ = places(routes[...], earlier[...], me, max(16, experts))
    normed_half = normed_ref[:, part(tp, half)]
    for k in range(experts - 1, 1, -1):
        far[k - 2][...] = matmul(table(place, k, capacity), normed_half).astype(LOW)
    normed = normed_ref[...]
    near[...] = matmul(table(place, 1, capacity), normed).astype(LOW)
    own[...] = matmul(table(place, 0, capacity), normed).astype(LOW)


def mixing(experts, routes, gates, earlier, upstream, high, low, upstream_here, arrived):
    load = pltpu.make_async_copy(upstream, upstream_here, arrived)
    load.start()
    me = lax.axis_index("exp")
    token_count = routes.shape[1]
    capacity = high.shape[2]
    place, first, second = places(routes[...], earlier[...], me, max(16, experts))
    gate = jnp.where(first, gates[0:1, :], 0.0) + jnp.where(second, gates[1:2, :], 0.0)
    place = place.T
    gate = gate.T
    slots = lax.broadcasted_iota(jnp.int32, (token_count, capacity), 1).astype(WIDE)
    for k in range(experts):
        weight = jnp.where(place[:, k : k + 1] == slots, gate[:, k : k + 1], 0.0)
        upper = weight.astype(LOW)
        high[k] = upper
        low[k] = (weight - upper.astype(WIDE)).astype(LOW)
    load.wait()


def expert(split, *refs):
    rows, refs = refs[: 1 + split], refs[1 + split :]
    first, second, away, kept, inner = refs
    tp = lax.axis_index("tp")
    width, hidden = first.shape
    half = width // 2
    chunk = min(512, hidden)
    for c in range(hidden // chunk):
        columns = slice(c * chunk, (c + 1) * chunk)
        if split:
            value = matmul(rows[0][...], first[part(tp, half), columns])
            value = value + matmul(rows[1][...], first[part(1 - tp, half), columns])
        else:
            value = matmul(rows[0][...], first[:, columns])
        inner[:, columns] = jnp.maximum(value, 0.0).astype(LOW)
    away[...] = matmul(inner[...], second[:, part(1 - tp, half)]).astype(LOW)
    kept[...] = matmul(inner[...], second[:, part(tp, half)])


def expert_first(rows, first, second, away, kept, first_here, second_here, inner, arrived):
    tp = lax.axis_index("tp")
    width, hidden = first.shape
    half = width // 2
    chunk = min(512, hidden)
    columns = [slice(c * chunk, (c + 1) * chunk) for c in range(hidden // chunk)]
    loads = [
        pltpu.make_async_copy(first.at[:, c], first_here.at[:, c], arrived.at[i])
        for i, c in enumerate(columns)
    ]
    loads.append(pltpu.make_async_copy(second, second_here, arrived.at[len(columns)]))
    for load in loads:
        load.start()
    for c, load in zip(columns, loads):
        load.wait()
        inner[:, c] = jnp.maximum(matmul(rows[...], first_here[:, c]), 0.0).astype(LOW)
    loads[-1].wait()
    away[...] = matmul(inner[...], second_here[:, part(1 - tp, half)]).astype(LOW)
    kept[...] = matmul(inner[...], second_here[:, part(tp, half)])


def idle():
    pass


def add(kept, arrived, out):
    out[...] = (kept[...] + arrived[...].astype(WIDE)).astype(LOW)


def combine(order, base, high, low, *refs):
    returned, out = refs[:-1], refs[-1]
    half = out.shape[1]
    if base.shape[1] == half:
        mixed = base[...]
    else:
        mixed = base[:, part(lax.axis_index("tp"), half)].astype(WIDE)
    for k, block in zip(order, returned, strict=True):
        rows = block[...]
        mixed = mixed + (matmul(high[k], rows) + matmul(low[k], rows))
    out[...] = mixed.astype(out.dtype)


def project(mine, other, gain, weight, out):
    tp = lax.axis_index("tp")
    half = mine.shape[1]
    own = mine[...].astype(WIDE)
    rest = other[...].astype(WIDE)
    average = (
        jnp.sum(own, axis=-1, keepdims=True) + jnp.sum(rest, axis=-1, keepdims=True)
    ) / (2 * half)
    own = own - average
    rest = rest - average
    spread = (
        jnp.sum(own * own, axis=-1, keepdims=True) + jnp.sum(rest * rest, axis=-1, keepdims=True)
    ) / (2 * half)
    factor = lax.rsqrt(spread + EPS)
    own = (own * factor * gain[:, part(tp, half)]).astype(LOW)
    rest = (rest * factor * gain[:, part(1 - tp, half)]).astype(LOW)
    value = matmul(own, weight[part(tp, half), :]) + matmul(rest, weight[part(1 - tp, half), :])
    out[...] = value.astype(LOW)


def choose(own, beside, *refs):
    sec = lax.axis_index("sec")
    moved, out = refs[:-1], refs[-1]
    for i, source in enumerate((own, beside, *moved)):

        @pl.when(sec == i)
        def _():
            out[...] = source[...]


def attend(
    first, second, queries, upstream, key_w, value_w, away, kept, low_ref, values, keys, dkeys, dvalues
):
    tp = lax.axis_index("tp")
    sec = lax.axis_index("sec")
    token_count, half = first.shape
    width = 2 * half
    scale = 1.0 / math.sqrt(HD)

    @pl.when(sec != 0)
    def _():
        crossed = ((sec > 1) & (sec % 2 == 1)).astype(jnp.int32)
        place = tp ^ crossed
        for weight, target in ((key_w, keys), (value_w, values)):
            value = matmul(first[...], weight[part(place, half), :])
            value = value + matmul(second[...], weight[part(1 - place, half), :])
            target[...] = value.astype(LOW)
        heads = [
            (slice(s * SEQ, (s + 1) * SEQ), slice(h * HD, (h + 1) * HD))
            for s in range(token_count // SEQ)
            for h in range(queries.shape[1] // HD)
        ]
        scores = [matmul(keys[at], queries[at], NT) for at in heads]
        dprobs = [matmul(values[at], upstream[at], NT) for at in heads]
        powers = [jnp.exp(x * scale) for x in scores]
        probs = [x * (1.0 / jnp.sum(x, axis=0, keepdims=True)) for x in powers]
        lows = [x.astype(LOW) for x in probs]
        for at, low in zip(heads, lows):
            dvalues[at] = matmul(low, upstream[at]).astype(LOW)
        rowdots = [jnp.sum(x * y, axis=0, keepdims=True) for x, y in zip(dprobs, probs)]
        dscores = [
            (y * (x - z)).astype(LOW) for x, y, z in zip(dprobs, probs, rowdots)
        ]
        for at, dscore in zip(heads, dscores):
            dkeys[at] = (matmul(dscore, queries[at]) * scale).astype(LOW)
        for i, low in enumerate(lows):
            low_ref[i] = low
        side = sec % 2
        pairs = lax.axis_size("sec") // 2
        block = width // (2 * pairs)
        for target, parity in ((away, 1 - side), (kept, side)):
            for i in range(pairs):
                rows = part(2 * i + parity, block)
                value = matmul(dkeys[...], key_w[rows, :], NT)
                value = value + matmul(dvalues[...], value_w[rows, :], NT)
                target[:, i * block : (i + 1) * block] = value.astype(target.dtype)

    @pl.when(sec == 0)
    def _():
        away[...] = jnp.zeros_like(away)
        kept[...] = jnp.zeros_like(kept)


def contexts(low_ref, values, hidden, out):
    sec = lax.axis_index("sec")
    head_count = values.shape[1] // HD

    @pl.when(sec == 0)
    def _():
        out[...] = hidden[...]

    @pl.when(sec != 0)
    def _():
        for i in range(low_ref.shape[0]):
            s, h = i // head_count, i % head_count
            at = slice(s * SEQ, (s + 1) * SEQ), slice(h * HD, (h + 1) * HD)
            out[at] = matmul(low_ref[i], values[at], TN).astype(LOW)


def gather_term(kept, arrived, own, *sent):
    tp = lax.axis_index("tp")
    here = lax.axis_index("sec") // 2 * lax.axis_size("tp") + tp
    width = own.shape[1]
    for k in range(len(sent) + 1):
        columns = part(here ^ k, width)
        value = kept[:, columns] + arrived[:, columns].astype(WIDE)
        if k == 0:
            own[...] = value
        else:
            sent[k - 1][...] = value.astype(LOW)


def swap(block, axis, step):
    size = lax.axis_size(axis)
    return lax.ppermute(block, axis, [(i, i ^ step) for i in range(size)])


def shards(
    tokens,
    routes,
    gate_weights,
    moe_gain,
    attn_gain,
    expert_in,
    expert_out,
    query_weight,
    key_weight,
    value_weight,
    cotangent,
):
    token_rows = tokens[0]
    route_rows = routes[0].T
    gate_rows = gate_weights[0].T
    token_count, model_width = token_rows.shape
    experts = lax.axis_size("exp")
    sections = lax.axis_size("sec")
    tp_size = lax.axis_size("tp")
    sec = lax.axis_index("sec")
    half = model_width // tp_size
    capacity = 3 * token_count // experts
    weight_first = expert_in[0, 0]
    weight_second = expert_out[0, 0]
    units = weight_first.shape[1]

    middle = max(2, experts // 2 + 1)
    groups = [list(range(middle - 1, 1, -1)), list(range(experts - 1, middle - 1, -1))]
    row_half, row_whole = shape_of((capacity, half)), shape_of((capacity, model_width))
    earlier = call(
        triangle,
        [shape_of((token_count, token_count))],
        [],
        flops=20 * token_count * token_count * model_width,
    )[0]
    *far_rows, near_rows, own_rows = call(
        functools.partial(prepare, experts),
        [row_half] * (experts - 2) + [row_whole] * 2,
        [token_rows, route_rows, moe_gain, earlier],
        [pltpu.VMEM((token_count, model_width), LOW)],
        flops=2 * 3 * token_count * token_count * model_width,
    )
    def hold(array, after):
        return call(idle, [], [], after=after, held=[array])[0]

    def joined(group):
        blocks = [swap(far_rows[k - 2], "exp", k) for k in group]
        return blocks[0] if len(blocks) == 1 else jnp.concatenate(blocks, axis=0)

    def total(away, kept, plain=False):
        arrived = swap(away, "tp", 1)
        if plain:
            return (kept + arrived.astype(WIDE)).astype(LOW)
        return call(add, [shape_of(away.shape)], [kept, arrived])[0]

    def through(rows, after):
        count = rows[0].shape[0]
        return call(
            functools.partial(expert, len(rows) - 1),
            [shape_of((count, half)), shape_of((count, half), WIDE)],
            [*rows, weight_first, weight_second],
            [pltpu.VMEM((count, units), LOW)],
            flops=4 * count * model_width * units,
            limit=24,
            after=after,
        )

    arriving = [joined(groups[0])]
    near = swap(near_rows, "exp", 1)
    later = [far_rows[k - 2] for k in groups[1]]
    loads = max(1, units // 512) + 1
    own_away, own_kept, weight_first, weight_second, *later = call(
        expert_first,
        [
            row_half,
            shape_of((capacity, half), WIDE),
            shape_of(weight_first.shape),
            shape_of(weight_second.shape),
        ],
        [own_rows, weight_first, weight_second],
        [pltpu.VMEM((capacity, units), LOW), pltpu.SemaphoreType.DMA((loads,))],
        flops=4 * capacity * model_width * units,
        remote=(1, 2),
        limit=44,
        held=later,
    )
    for k, rows in zip(groups[1], later):
        far_rows[k - 2] = rows
    arriving.append(joined(groups[1]))
    returned = {0: total(own_away, own_kept)}
    arriving[0] = hold(arriving[0], [own_away])
    others = [swap(arriving[0], "tp", 1)]
    high, low, upstream = call(
        functools.partial(mixing, experts),
        [shape_of((experts, token_count, capacity))] * 2 + [shape_of(cotangent.shape[1:])],
        [route_rows, gate_rows, earlier, cotangent[0]],
        [pltpu.SemaphoreType.DMA],
        remote=(3,),
        after=[arriving[0]],
    )
    others.append(swap(arriving[1], "tp", 1))

    def give_back(group, block):
        for i, k in enumerate(group):
            rows = block if len(group) == 1 else block[i * capacity : (i + 1) * capacity]
            returned[k] = swap(rows, "exp", k)

    near_away, near_kept = through([near], [returned[0], high])
    away, kept = through([arriving[0], others[0]], [near_away])
    mixed = total(away, kept)
    give_back(groups[0], mixed)
    near_total = total(near_away, near_kept, plain=True)
    returned[1] = swap(near_total, "exp", 1)
    away, kept = through([arriving[1], others[1]], [mixed])
    last = total(away, kept)
    there, rest = [0, *groups[0]], [1, *groups[1]]
    so_far, last = call(
        functools.partial(combine, there),
        [shape_of((token_count, half), WIDE)],
        [token_rows, high, low, *(returned[k] for k in there)],
        flops=4 * len(there) * token_count * capacity * half,
        held=[last],
    )
    give_back(groups[1], last)
    hidden_half = call(
        functools.partial(combine, rest),
        [shape_of((token_count, half))],
        [so_far, high, low, *(returned[k] for k in rest)],
        flops=4 * len(rest) * token_count * capacity * half,
    )[0]

    hidden_other = swap(hidden_half, "tp", 1)

    def cycle(order, crossed):
        pairs = [(i, i ^ 1) for i in range(sections * tp_size)]
        targets = dict(pairs)
        for a, b in zip(order, order[1:] + order[:1]):
            for t in range(tp_size):
                targets[a * tp_size + t] = b * tp_size + (t ^ crossed if a == 0 else t)
        return lax.ppermute(hidden_half, ("sec", "tp"), list(targets.items()))

    moved = [[cycle([0, 2 * i, 2 * i + 1, 1], 0), cycle([0, 2 * i + 1, 2 * i, 1], 1)] for i in range(1, sections // 2)]
    beside = swap(hidden_half, "sec", 1)
    first = call(choose, [shape_of(hidden_half.shape)], [hidden_other, beside, *sum(moved, [])])[0]
    second = swap(first, "sec", 1)

    local_width = query_weight.shape[2]
    queries = call(
        project,
        [shape_of((token_count, local_width))],
        [hidden_half, hidden_other, attn_gain, query_weight[0]],
        flops=2 * token_count * model_width * local_width,
    )[0]
    heads = token_count // SEQ * (local_width // HD)
    away, kept, lows, values = call(
        attend,
        [
            shape_of((token_count, model_width // 2)),
            shape_of((token_count, model_width // 2), WIDE),
            shape_of((heads, SEQ, SEQ)),
            shape_of((token_count, local_width)),
        ],
        [first, second, queries, upstream, key_weight[0], value_weight[0]],
        [pltpu.VMEM((token_count, local_width), LOW)] * 3,
        flops=10 * token_count * model_width * local_width,
    )
    context = call(
        contexts,
        [shape_of((token_count, local_width))],
        [lows, values, hidden_half],
        flops=2 * token_count * SEQ * local_width,
    )[0]

    own = model_width // (sections * tp_size)
    count = sections // 2 * tp_size
    both = sections * tp_size
    blocks = call(
        gather_term,
        [shape_of((token_count, own), WIDE)] + [shape_of((token_count, own))] * (count - 1),
        [kept, swap(away, "sec", 1)],
    )
    total = blocks[0]
    for k in range(1, count):
        pairs = []
        for i in range(both):
            section, t = i // tp_size, i % tp_size
            target = (section // 2 * tp_size + t) ^ k
            pairs.append((i, (target // tp_size * 2 + section % 2) * tp_size + target % tp_size))
        total = total + lax.ppermute(blocks[k], ("sec", "tp"), pairs).astype(WIDE)
    return (context[None], total.astype(LOW))


def solution(mesh):
    placed = (
        P("sec", "exp", None),
        P("sec", "exp", None),
        P("sec", "exp", None),
        P("sec", None),
        P("sec", None),
        P("sec", "exp", None, "tp"),
        P("sec", "exp", "tp", None),
        P("sec", None, "tp"),
        P("sec", None, "tp"),
        P("sec", None, "tp"),
        P("sec", "exp", "tp"),
    )
    return jax.shard_map(
        shards,
        mesh=mesh,
        in_specs=placed,
        out_specs=(P("sec", "exp", "tp"), P("exp", ("sec", "tp"))),
        check_vma=False,
    )
```

```python
import functools
import math

import jax
import jax.numpy as jnp
from jax import lax
from jax.experimental import pallas as pl
from jax.experimental.pallas import tpu as pltpu
from jax.sharding import PartitionSpec as P

HD = 128
SEQ = 128
EPS = 1e-05

LOW = jnp.bfloat16
WIDE = jnp.float32
VMEM = pl.BlockSpec(memory_space=pltpu.VMEM)
HBM = pl.BlockSpec(memory_space=pltpu.HBM)
ANY = pl.BlockSpec(memory_space=pl.ANY)
NT = (((1,), (1,)), ((), ()))
TN = (((0,), (0,)), ((), ()))


def matmul(a, b, dims=(((1,), (0,)), ((), ()))):
    return lax.dot_general(a, b, dims, preferred_element_type=WIDE)


def call(body, out_shape, inputs, scratch=(), flops=0, limit=16, remote=(), after=(), held=()):
    def size(x):
        return math.prod(x.shape) * jnp.dtype(x.dtype).itemsize

    count, results = len(inputs), len(out_shape)
    extra = len(after) + len(held)

    def run(*refs):
        outs = refs[count + extra : count + extra + results]
        return body(*refs[:count], *outs, *refs[count + extra + results + len(held) :])

    moved = sum(size(x) for x in inputs) + sum(size(x) for x in out_shape)
    return pl.pallas_call(
        run,
        out_shape=[*out_shape, *(shape_of(x.shape, x.dtype) for x in held)],
        in_specs=[HBM if i in remote else VMEM for i in range(count)] + [ANY] * extra,
        out_specs=[VMEM] * results + [ANY] * len(held),
        scratch_shapes=list(scratch),
        input_output_aliases={count + len(after) + i: results + i for i in range(len(held))},
        compiler_params=pltpu.CompilerParams(vmem_limit_bytes=limit * 2**20),
        cost_estimate=pl.CostEstimate(flops=flops, bytes_accessed=moved, transcendentals=0),
    )(*inputs, *after, *held)


def shape_of(dims, kind=LOW):
    return jax.ShapeDtypeStruct(dims, kind)


def part(index, width):
    return pl.ds(pl.multiple_of(index * width, width), width)


def triangle(out):
    source = lax.broadcasted_iota(jnp.int32, out.shape, 0)
    target = lax.broadcasted_iota(jnp.int32, out.shape, 1)
    out[...] = jnp.where(source < target, 1.0, 0.0).astype(LOW)


def places(routes, earlier, me, rows):
    labels = lax.broadcasted_iota(jnp.int32, (rows, 1), 0) ^ me
    first = routes[0:1, :] == labels
    second = routes[1:2, :] == labels
    either = first | second
    before = matmul(jnp.where(either, 1.0, 0.0).astype(LOW), earlier)
    return jnp.where(either, before, -1.0), first, second


def table(place, k, capacity):
    slots = lax.broadcasted_iota(jnp.int32, (capacity, place.shape[1]), 0).astype(WIDE)
    return jnp.where(place[k : k + 1, :] == slots, 1.0, 0.0).astype(LOW)


def prepare(experts, tokens, routes, gain, earlier, *outs):
    far, near, own, normed_ref = outs[:-3], outs[-3], outs[-2], outs[-1]
    me = lax.axis_index("exp")
    tp = lax.axis_index("tp")
    capacity, width = own.shape
    half = width // 2
    wide = tokens[...].astype(WIDE)
    average = jnp.mean(wide, axis=-1, keepdims=True)
    centred = wide - average
    spread = jnp.mean(centred * centred, axis=-1, keepdims=True)
    normed_ref[...] = (centred * lax.rsqrt(spread + EPS) * gain[...]).astype(LOW)
    place, _, _ = places(routes[...], earlier[...], me, max(16, experts))
    normed_half = normed_ref[:, part(tp, half)]
    for k in range(experts - 1, 1, -1):
        far[k - 2][...] = matmul(table(place, k, capacity), normed_half).astype(LOW)
    normed = normed_ref[...]
    near[...] = matmul(table(place, 1, capacity), normed).astype(LOW)
    own[...] = matmul(table(place, 0, capacity), normed).astype(LOW)


def mixing(experts, routes, gates, earlier, upstream, high, low, upstream_here, arrived):
    load = pltpu.make_async_copy(upstream, upstream_here, arrived)
    load.start()
    me = lax.axis_index("exp")
    token_count = routes.shape[1]
    capacity = high.shape[2]
    place, first, second = places(routes[...], earlier[...], me, max(16, experts))
    gate = jnp.where(first, gates[0:1, :], 0.0) + jnp.where(second, gates[1:2, :], 0.0)
    place = place.T
    gate = gate.T
    slots = lax.broadcasted_iota(jnp.int32, (token_count, capacity), 1).astype(WIDE)
    for k in range(experts):
        weight = jnp.where(place[:, k : k + 1] == slots, gate[:, k : k + 1], 0.0)
        upper = weight.astype(LOW)
        high[k] = upper
        low[k] = (weight - upper.astype(WIDE)).astype(LOW)
    load.wait()


def expert(split, *refs):
    rows, refs = refs[: 1 + split], refs[1 + split :]
    first, second, away, kept, inner = refs
    tp = lax.axis_index("tp")
    width, hidden = first.shape
    half = width // 2
    chunk = min(512, hidden)
    for c in range(hidden // chunk):
        columns = slice(c * chunk, (c + 1) * chunk)
        if split:
            value = matmul(rows[0][...], first[part(tp, half), columns])
            value = value + matmul(rows[1][...], first[part(1 - tp, half), columns])
        else:
            value = matmul(rows[0][...], first[:, columns])
        inner[:, columns] = jnp.maximum(value, 0.0).astype(LOW)
    away[...] = matmul(inner[...], second[:, part(1 - tp, half)]).astype(LOW)
    kept[...] = matmul(inner[...], second[:, part(tp, half)])


def expert_first(rows, first, second, away, kept, first_here, second_here, inner, arrived):
    tp = lax.axis_index("tp")
    width, hidden = first.shape
    half = width // 2
    chunk = min(512, hidden)
    columns = [slice(c * chunk, (c + 1) * chunk) for c in range(hidden // chunk)]
    loads = [
        pltpu.make_async_copy(first.at[:, c], first_here.at[:, c], arrived.at[i])
        for i, c in enumerate(columns)
    ]
    loads.append(pltpu.make_async_copy(second, second_here, arrived.at[len(columns)]))
    for load in loads:
        load.start()
    for c, load in zip(columns, loads):
        load.wait()
        inner[:, c] = jnp.maximum(matmul(rows[...], first_here[:, c]), 0.0).astype(LOW)
    loads[-1].wait()
    away[...] = matmul(inner[...], second_here[:, part(1 - tp, half)]).astype(LOW)
    kept[...] = matmul(inner[...], second_here[:, part(tp, half)])


def idle():
    pass


def add(kept, arrived, out):
    out[...] = (kept[...] + arrived[...].astype(WIDE)).astype(LOW)


def combine(experts, tokens, high, low, *refs):
    returned, out = refs[:-1], refs[-1]
    tp = lax.axis_index("tp")
    half = out.shape[1]
    mixed = tokens[:, part(tp, half)].astype(WIDE)
    for k in range(experts):
        rows = returned[k][...]
        mixed = mixed + (matmul(high[k], rows) + matmul(low[k], rows))
    out[...] = mixed.astype(LOW)


def project(mine, other, gain, weight, out):
    tp = lax.axis_index("tp")
    half = mine.shape[1]
    own = mine[...].astype(WIDE)
    rest = other[...].astype(WIDE)
    average = (
        jnp.sum(own, axis=-1, keepdims=True) + jnp.sum(rest, axis=-1, keepdims=True)
    ) / (2 * half)
    own = own - average
    rest = rest - average
    spread = (
        jnp.sum(own * own, axis=-1, keepdims=True) + jnp.sum(rest * rest, axis=-1, keepdims=True)
    ) / (2 * half)
    factor = lax.rsqrt(spread + EPS)
    own = (own * factor * gain[:, part(tp, half)]).astype(LOW)
    rest = (rest * factor * gain[:, part(1 - tp, half)]).astype(LOW)
    value = matmul(own, weight[part(tp, half), :]) + matmul(rest, weight[part(1 - tp, half), :])
    out[...] = value.astype(LOW)


def choose(own, beside, *refs):
    sec = lax.axis_index("sec")
    moved, out = refs[:-1], refs[-1]
    for i, source in enumerate((own, beside, *moved)):

        @pl.when(sec == i)
        def _():
            out[...] = source[...]


def attend(
    first, second, queries, upstream, key_w, value_w, away, low_ref, values, dkeys, dvalues, keys
):
    tp = lax.axis_index("tp")
    sec = lax.axis_index("sec")
    token_count, half = first.shape
    scale = 1.0 / math.sqrt(HD)

    @pl.when(sec != 0)
    def _():
        crossed = ((sec > 1) & (sec % 2 == 1)).astype(jnp.int32)
        place = tp ^ crossed
        for weight, target in ((key_w, keys), (value_w, values)):
            value = matmul(first[...], weight[part(place, half), :])
            value = value + matmul(second[...], weight[part(1 - place, half), :])
            target[...] = value.astype(LOW)
        heads = [
            (slice(s * SEQ, (s + 1) * SEQ), slice(h * HD, (h + 1) * HD))
            for s in range(token_count // SEQ)
            for h in range(queries.shape[1] // HD)
        ]
        scores = [matmul(keys[at], queries[at], NT) for at in heads]
        dprobs = [matmul(values[at], upstream[at], NT) for at in heads]
        powers = [jnp.exp(x * scale) for x in scores]
        probs = [x * (1.0 / jnp.sum(x, axis=0, keepdims=True)) for x in powers]
        lows = [x.astype(LOW) for x in probs]
        for at, low in zip(heads, lows):
            dvalues[at] = matmul(low, upstream[at]).astype(LOW)
        rowdots = [jnp.sum(x * y, axis=0, keepdims=True) for x, y in zip(dprobs, probs)]
        dscores = [
            (y * (x - z)).astype(LOW) for x, y, z in zip(dprobs, probs, rowdots)
        ]
        for at, dscore in zip(heads, dscores):
            dkeys[at] = (matmul(dscore, queries[at]) * scale).astype(LOW)
        for i, low in enumerate(lows):
            low_ref[i] = low
        terms(dkeys, dvalues, key_w, value_w, 1 - sec % 2, away)

    @pl.when(sec == 0)
    def _():
        away[...] = jnp.zeros_like(away)


def terms(dkeys, dvalues, key_w, value_w, parity, out):
    pairs = lax.axis_size("sec") // 2
    block = out.shape[1] // pairs
    for i in range(pairs):
        rows = part(2 * i + parity, block)
        value = matmul(dkeys[...], key_w[rows, :], NT)
        value = value + matmul(dvalues[...], value_w[rows, :], NT)
        out[:, i * block : (i + 1) * block] = value.astype(out.dtype)


def keep(dkeys, dvalues, key_w, value_w, out):
    sec = lax.axis_index("sec")

    @pl.when(sec != 0)
    def _():
        terms(dkeys, dvalues, key_w, value_w, sec % 2, out)

    @pl.when(sec == 0)
    def _():
        out[...] = jnp.zeros_like(out)


def contexts(low_ref, values, hidden, out):
    sec = lax.axis_index("sec")
    head_count = values.shape[1] // HD

    @pl.when(sec == 0)
    def _():
        out[...] = hidden[...]

    @pl.when(sec != 0)
    def _():
        for i in range(low_ref.shape[0]):
            s, h = i // head_count, i % head_count
            at = slice(s * SEQ, (s + 1) * SEQ), slice(h * HD, (h + 1) * HD)
            out[at] = matmul(low_ref[i], values[at], TN).astype(LOW)


def gather_term(kept, arrived, own, *sent):
    tp = lax.axis_index("tp")
    here = lax.axis_index("sec") // 2 * lax.axis_size("tp") + tp
    width = own.shape[1]
    for k in range(len(sent) + 1):
        columns = part(here ^ k, width)
        value = kept[:, columns] + arrived[:, columns].astype(WIDE)
        if k == 0:
            own[...] = value
        else:
            sent[k - 1][...] = value.astype(LOW)


def swap(block, axis, step):
    size = lax.axis_size(axis)
    return lax.ppermute(block, axis, [(i, i ^ step) for i in range(size)])


def shards(
    tokens,
    routes,
    gate_weights,
    moe_gain,
    attn_gain,
    expert_in,
    expert_out,
    query_weight,
    key_weight,
    value_weight,
    cotangent,
):
    token_rows = tokens[0]
    route_rows = routes[0].T
    gate_rows = gate_weights[0].T
    token_count, model_width = token_rows.shape
    experts = lax.axis_size("exp")
    sections = lax.axis_size("sec")
    tp_size = lax.axis_size("tp")
    sec = lax.axis_index("sec")
    half = model_width // tp_size
    capacity = 3 * token_count // experts
    weight_first = expert_in[0, 0]
    weight_second = expert_out[0, 0]
    units = weight_first.shape[1]

    middle = max(2, experts // 2 + 1)
    groups = [list(range(middle - 1, 1, -1)), list(range(experts - 1, middle - 1, -1))]
    row_half, row_whole = shape_of((capacity, half)), shape_of((capacity, model_width))
    earlier = call(
        triangle,
        [shape_of((token_count, token_count))],
        [],
        flops=20 * token_count * token_count * model_width,
    )[0]
    *far_rows, near_rows, own_rows = call(
        functools.partial(prepare, experts),
        [row_half] * (experts - 2) + [row_whole] * 2,
        [token_rows, route_rows, moe_gain, earlier],
        [pltpu.VMEM((token_count, model_width), LOW)],
        flops=2 * 3 * token_count * token_count * model_width,
    )
    def hold(array, after):
        return call(idle, [], [], after=after, held=[array])[0]

    def joined(group):
        blocks = [swap(far_rows[k - 2], "exp", k) for k in group]
        return blocks[0] if len(blocks) == 1 else jnp.concatenate(blocks, axis=0)

    def total(away, kept, plain=False):
        arrived = swap(away, "tp", 1)
        if plain:
            return (kept + arrived.astype(WIDE)).astype(LOW)
        return call(add, [shape_of(away.shape)], [kept, arrived])[0]

    def through(rows, after):
        count = rows[0].shape[0]
        return call(
            functools.partial(expert, len(rows) - 1),
            [shape_of((count, half)), shape_of((count, half), WIDE)],
            [*rows, weight_first, weight_second],
            [pltpu.VMEM((count, units), LOW)],
            flops=4 * count * model_width * units,
            limit=24,
            after=after,
        )

    arriving = [joined(groups[0])]
    near = swap(near_rows, "exp", 1)
    later = [far_rows[k - 2] for k in groups[1]]
    loads = max(1, units // 512) + 1
    own_away, own_kept, weight_first, weight_second = call(
        expert_first,
        [
            row_half,
            shape_of((capacity, half), WIDE),
            shape_of(weight_first.shape),
            shape_of(weight_second.shape),
        ],
        [own_rows, weight_first, weight_second],
        [pltpu.VMEM((capacity, units), LOW), pltpu.SemaphoreType.DMA((loads,))],
        flops=4 * capacity * model_width * units,
        remote=(1, 2),
        limit=44,
    )
    returned = {0: total(own_away, own_kept)}
    arriving[0], *later = call(idle, [], [], after=[own_away], held=[arriving[0], *later])
    for k, rows in zip(groups[1], later):
        far_rows[k - 2] = rows
    arriving.append(joined(groups[1]))
    others = [swap(arriving[0], "tp", 1)]
    high, low, upstream = call(
        functools.partial(mixing, experts),
        [shape_of((experts, token_count, capacity))] * 2 + [shape_of(cotangent.shape[1:])],
        [route_rows, gate_rows, earlier, cotangent[0]],
        [pltpu.SemaphoreType.DMA],
        remote=(3,),
        after=[arriving[0]],
    )
    others.append(swap(arriving[1], "tp", 1))

    def give_back(group, away, kept):
        mixed = total(away, kept)
        for i, k in enumerate(group):
            block = mixed if len(group) == 1 else mixed[i * capacity : (i + 1) * capacity]
            returned[k] = swap(block, "exp", k)
        return mixed

    away, kept = through([arriving[0], others[0]], [returned[0], high])
    near_away, near_kept = through([near], [away])
    near_away = hold(near_away, [others[1]])
    mixed = give_back(groups[0], away, kept)
    returned[1] = swap(total(near_away, near_kept, plain=True), "exp", 1)
    away, kept = through([arriving[1], others[1]], [mixed])
    give_back(groups[1], away, kept)

    hidden_half = call(
        functools.partial(combine, experts),
        [shape_of((token_count, half))],
        [token_rows, high, low, *(returned[k] for k in range(experts))],
        flops=4 * 3 * token_count * token_count * half,
    )[0]

    hidden_other = swap(hidden_half, "tp", 1)

    def cycle(order, crossed):
        pairs = [(i, i ^ 1) for i in range(sections * tp_size)]
        targets = dict(pairs)
        for a, b in zip(order, order[1:] + order[:1]):
            for t in range(tp_size):
                targets[a * tp_size + t] = b * tp_size + (t ^ crossed if a == 0 else t)
        return lax.ppermute(hidden_half, ("sec", "tp"), list(targets.items()))

    moved = [[cycle([0, 2 * i, 2 * i + 1, 1], 0), cycle([0, 2 * i + 1, 2 * i, 1], 1)] for i in range(1, sections // 2)]
    beside = swap(hidden_half, "sec", 1)
    first = call(choose, [shape_of(hidden_half.shape)], [hidden_other, beside, *sum(moved, [])])[0]
    second = swap(first, "sec", 1)

    local_width = query_weight.shape[2]
    queries = call(
        project,
        [shape_of((token_count, local_width))],
        [hidden_half, hidden_other, attn_gain, query_weight[0]],
        flops=2 * token_count * model_width * local_width,
    )[0]
    heads = token_count // SEQ * (local_width // HD)
    away, lows, values, dkeys, dvalues = call(
        attend,
        [
            shape_of((token_count, model_width // 2)),
            shape_of((heads, SEQ, SEQ)),
            *[shape_of((token_count, local_width))] * 3,
        ],
        [first, second, queries, upstream, key_weight[0], value_weight[0]],
        [pltpu.VMEM((token_count, local_width), LOW)],
        flops=8 * token_count * model_width * local_width,
    )
    kept = call(
        keep,
        [shape_of((token_count, model_width // 2), WIDE)],
        [dkeys, dvalues, key_weight[0], value_weight[0]],
        flops=2 * token_count * model_width * local_width,
    )[0]
    context = call(
        contexts,
        [shape_of((token_count, local_width))],
        [lows, values, hidden_half],
        flops=2 * token_count * SEQ * local_width,
    )[0]

    own = model_width // (sections * tp_size)
    count = sections // 2 * tp_size
    both = sections * tp_size
    blocks = call(
        gather_term,
        [shape_of((token_count, own), WIDE)] + [shape_of((token_count, own))] * (count - 1),
        [kept, swap(away, "sec", 1)],
    )
    total = blocks[0]
    for k in range(1, count):
        pairs = []
        for i in range(both):
            section, t = i // tp_size, i % tp_size
            target = (section // 2 * tp_size + t) ^ k
            pairs.append((i, (target // tp_size * 2 + section % 2) * tp_size + target % tp_size))
        total = total + lax.ppermute(blocks[k], ("sec", "tp"), pairs).astype(WIDE)
    return (context[None], total.astype(LOW))


def solution(mesh):
    placed = (
        P("sec", "exp", None),
        P("sec", "exp", None),
        P("sec", "exp", None),
        P("sec", None),
        P("sec", None),
        P("sec", "exp", None, "tp"),
        P("sec", "exp", "tp", None),
        P("sec", None, "tp"),
        P("sec", None, "tp"),
        P("sec", None, "tp"),
        P("sec", "exp", "tp"),
    )
    return jax.shard_map(
        shards,
        mesh=mesh,
        in_specs=placed,
        out_specs=(P("sec", "exp", "tp"), P("exp", ("sec", "tp"))),
        check_vma=False,
    )
```

```python
import functools
import math

import jax
import jax.numpy as jnp
from jax import lax
from jax.experimental import pallas as pl
from jax.experimental.pallas import tpu as pltpu
from jax.sharding import PartitionSpec as P

HD = 128
SEQ = 128
EPS = 1e-05

LOW = jnp.bfloat16
WIDE = jnp.float32
VMEM = pl.BlockSpec(memory_space=pltpu.VMEM)
HBM = pl.BlockSpec(memory_space=pltpu.HBM)
ANY = pl.BlockSpec(memory_space=pl.ANY)
NT = (((1,), (1,)), ((), ()))
TN = (((0,), (0,)), ((), ()))


def matmul(a, b, dims=(((1,), (0,)), ((), ()))):
    return lax.dot_general(a, b, dims, preferred_element_type=WIDE)


def call(body, out_shape, inputs, scratch=(), flops=0, limit=16, remote=(), after=(), held=()):
    def size(x):
        return math.prod(x.shape) * jnp.dtype(x.dtype).itemsize

    count, results = len(inputs), len(out_shape)
    extra = len(after) + len(held)

    def run(*refs):
        outs = refs[count + extra : count + extra + results]
        return body(*refs[:count], *outs, *refs[count + extra + results + len(held) :])

    moved = sum(size(x) for x in inputs) + sum(size(x) for x in out_shape)
    return pl.pallas_call(
        run,
        out_shape=[*out_shape, *(shape_of(x.shape, x.dtype) for x in held)],
        in_specs=[HBM if i in remote else VMEM for i in range(count)] + [ANY] * extra,
        out_specs=[VMEM] * results + [ANY] * len(held),
        scratch_shapes=list(scratch),
        input_output_aliases={count + len(after) + i: results + i for i in range(len(held))},
        compiler_params=pltpu.CompilerParams(vmem_limit_bytes=limit * 2**20),
        cost_estimate=pl.CostEstimate(flops=flops, bytes_accessed=moved, transcendentals=0),
    )(*inputs, *after, *held)


def shape_of(dims, kind=LOW):
    return jax.ShapeDtypeStruct(dims, kind)


def part(index, width):
    return pl.ds(pl.multiple_of(index * width, width), width)


def triangle(out):
    source = lax.broadcasted_iota(jnp.int32, out.shape, 0)
    target = lax.broadcasted_iota(jnp.int32, out.shape, 1)
    out[...] = jnp.where(source < target, 1.0, 0.0).astype(LOW)


def places(routes, earlier, me, rows):
    labels = lax.broadcasted_iota(jnp.int32, (rows, 1), 0) ^ me
    first = routes[0:1, :] == labels
    second = routes[1:2, :] == labels
    either = first | second
    before = matmul(jnp.where(either, 1.0, 0.0).astype(LOW), earlier)
    return jnp.where(either, before, -1.0), first, second


def table(place, k, capacity):
    slots = lax.broadcasted_iota(jnp.int32, (capacity, place.shape[1]), 0).astype(WIDE)
    return jnp.where(place[k : k + 1, :] == slots, 1.0, 0.0).astype(LOW)


def prepare(experts, tokens, routes, gain, earlier, *outs):
    far, near, own, normed_ref = outs[:-3], outs[-3], outs[-2], outs[-1]
    me = lax.axis_index("exp")
    tp = lax.axis_index("tp")
    capacity, width = own.shape
    half = width // 2
    wide = tokens[...].astype(WIDE)
    average = jnp.mean(wide, axis=-1, keepdims=True)
    centred = wide - average
    spread = jnp.mean(centred * centred, axis=-1, keepdims=True)
    normed_ref[...] = (centred * lax.rsqrt(spread + EPS) * gain[...]).astype(LOW)
    place, _, _ = places(routes[...], earlier[...], me, max(16, experts))
    normed_half = normed_ref[:, part(tp, half)]
    for k in range(experts - 1, 1, -1):
        far[k - 2][...] = matmul(table(place, k, capacity), normed_half).astype(LOW)
    normed = normed_ref[...]
    near[...] = matmul(table(place, 1, capacity), normed).astype(LOW)
    own[...] = matmul(table(place, 0, capacity), normed).astype(LOW)


def mixing(experts, routes, gates, earlier, upstream, high, low, upstream_here, arrived):
    load = pltpu.make_async_copy(upstream, upstream_here, arrived)
    load.start()
    me = lax.axis_index("exp")
    token_count = routes.shape[1]
    capacity = high.shape[2]
    place, first, second = places(routes[...], earlier[...], me, max(16, experts))
    gate = jnp.where(first, gates[0:1, :], 0.0) + jnp.where(second, gates[1:2, :], 0.0)
    place = place.T
    gate = gate.T
    slots = lax.broadcasted_iota(jnp.int32, (token_count, capacity), 1).astype(WIDE)
    for k in range(experts):
        weight = jnp.where(place[:, k : k + 1] == slots, gate[:, k : k + 1], 0.0)
        upper = weight.astype(LOW)
        high[k] = upper
        low[k] = (weight - upper.astype(WIDE)).astype(LOW)
    load.wait()


def expert(split, *refs):
    rows, refs = refs[: 1 + split], refs[1 + split :]
    first, second, away, kept, inner = refs
    tp = lax.axis_index("tp")
    width, hidden = first.shape
    half = width // 2
    chunk = min(512, hidden)
    for c in range(hidden // chunk):
        columns = slice(c * chunk, (c + 1) * chunk)
        if split:
            value = matmul(rows[0][...], first[part(tp, half), columns])
            value = value + matmul(rows[1][...], first[part(1 - tp, half), columns])
        else:
            value = matmul(rows[0][...], first[:, columns])
        inner[:, columns] = jnp.maximum(value, 0.0).astype(LOW)
    away[...] = matmul(inner[...], second[:, part(1 - tp, half)]).astype(LOW)
    kept[...] = matmul(inner[...], second[:, part(tp, half)])


def expert_first(rows, first, second, away, kept, first_here, second_here, inner, arrived):
    tp = lax.axis_index("tp")
    width, hidden = first.shape
    half = width // 2
    chunk = min(512, hidden)
    columns = [slice(c * chunk, (c + 1) * chunk) for c in range(hidden // chunk)]
    loads = [
        pltpu.make_async_copy(first.at[:, c], first_here.at[:, c], arrived.at[i])
        for i, c in enumerate(columns)
    ]
    loads.append(pltpu.make_async_copy(second, second_here, arrived.at[len(columns)]))
    for load in loads:
        load.start()
    for c, load in zip(columns, loads):
        load.wait()
        inner[:, c] = jnp.maximum(matmul(rows[...], first_here[:, c]), 0.0).astype(LOW)
    loads[-1].wait()
    away[...] = matmul(inner[...], second_here[:, part(1 - tp, half)]).astype(LOW)
    kept[...] = matmul(inner[...], second_here[:, part(tp, half)])


def idle():
    pass


def add(kept, arrived, out):
    out[...] = (kept[...] + arrived[...].astype(WIDE)).astype(LOW)


def combine(experts, tokens, high, low, *refs):
    returned, out = refs[:-1], refs[-1]
    tp = lax.axis_index("tp")
    half = out.shape[1]
    mixed = tokens[:, part(tp, half)].astype(WIDE)
    for k in range(experts):
        rows = returned[k][...]
        mixed = mixed + (matmul(high[k], rows) + matmul(low[k], rows))
    out[...] = mixed.astype(LOW)


def project(mine, other, gain, weight, out):
    tp = lax.axis_index("tp")
    half = mine.shape[1]
    own = mine[...].astype(WIDE)
    rest = other[...].astype(WIDE)
    average = (
        jnp.sum(own, axis=-1, keepdims=True) + jnp.sum(rest, axis=-1, keepdims=True)
    ) / (2 * half)
    own = own - average
    rest = rest - average
    spread = (
        jnp.sum(own * own, axis=-1, keepdims=True) + jnp.sum(rest * rest, axis=-1, keepdims=True)
    ) / (2 * half)
    factor = lax.rsqrt(spread + EPS)
    own = (own * factor * gain[:, part(tp, half)]).astype(LOW)
    rest = (rest * factor * gain[:, part(1 - tp, half)]).astype(LOW)
    value = matmul(own, weight[part(tp, half), :]) + matmul(rest, weight[part(1 - tp, half), :])
    out[...] = value.astype(LOW)


def choose(own, beside, *refs):
    sec = lax.axis_index("sec")
    moved, out = refs[:-1], refs[-1]
    for i, source in enumerate((own, beside, *moved)):

        @pl.when(sec == i)
        def _():
            out[...] = source[...]


def attend(
    first, second, queries, upstream, key_w, value_w, away, low_ref, values, dkeys, dvalues, keys
):
    tp = lax.axis_index("tp")
    sec = lax.axis_index("sec")
    token_count, half = first.shape
    scale = 1.0 / math.sqrt(HD)

    @pl.when(sec != 0)
    def _():
        crossed = ((sec > 1) & (sec % 2 == 1)).astype(jnp.int32)
        place = tp ^ crossed
        for weight, target in ((key_w, keys), (value_w, values)):
            value = matmul(first[...], weight[part(place, half), :])
            value = value + matmul(second[...], weight[part(1 - place, half), :])
            target[...] = value.astype(LOW)
        heads = [
            (slice(s * SEQ, (s + 1) * SEQ), slice(h * HD, (h + 1) * HD))
            for s in range(token_count // SEQ)
            for h in range(queries.shape[1] // HD)
        ]
        scores = [matmul(keys[at], queries[at], NT) for at in heads]
        dprobs = [matmul(values[at], upstream[at], NT) for at in heads]
        powers = [jnp.exp(x * scale) for x in scores]
        probs = [x * (1.0 / jnp.sum(x, axis=0, keepdims=True)) for x in powers]
        lows = [x.astype(LOW) for x in probs]
        for at, low in zip(heads, lows):
            dvalues[at] = matmul(low, upstream[at]).astype(LOW)
        rowdots = [jnp.sum(x * y, axis=0, keepdims=True) for x, y in zip(dprobs, probs)]
        dscores = [
            (y * (x - z)).astype(LOW) for x, y, z in zip(dprobs, probs, rowdots)
        ]
        for at, dscore in zip(heads, dscores):
            dkeys[at] = (matmul(dscore, queries[at]) * scale).astype(LOW)
        for i, low in enumerate(lows):
            low_ref[i] = low
        terms(dkeys, dvalues, key_w, value_w, 1 - sec % 2, away)

    @pl.when(sec == 0)
    def _():
        away[...] = jnp.zeros_like(away)


def terms(dkeys, dvalues, key_w, value_w, parity, out):
    pairs = lax.axis_size("sec") // 2
    block = out.shape[1] // pairs
    for i in range(pairs):
        rows = part(2 * i + parity, block)
        value = matmul(dkeys[...], key_w[rows, :], NT)
        value = value + matmul(dvalues[...], value_w[rows, :], NT)
        out[:, i * block : (i + 1) * block] = value.astype(out.dtype)


def keep(dkeys, dvalues, key_w, value_w, out):
    sec = lax.axis_index("sec")

    @pl.when(sec != 0)
    def _():
        terms(dkeys, dvalues, key_w, value_w, sec % 2, out)

    @pl.when(sec == 0)
    def _():
        out[...] = jnp.zeros_like(out)


def contexts(low_ref, values, hidden, out):
    sec = lax.axis_index("sec")
    head_count = values.shape[1] // HD

    @pl.when(sec == 0)
    def _():
        out[...] = hidden[...]

    @pl.when(sec != 0)
    def _():
        for i in range(low_ref.shape[0]):
            s, h = i // head_count, i % head_count
            at = slice(s * SEQ, (s + 1) * SEQ), slice(h * HD, (h + 1) * HD)
            out[at] = matmul(low_ref[i], values[at], TN).astype(LOW)


def gather_term(kept, arrived, own, *sent):
    tp = lax.axis_index("tp")
    here = lax.axis_index("sec") // 2 * lax.axis_size("tp") + tp
    width = own.shape[1]
    for k in range(len(sent) + 1):
        columns = part(here ^ k, width)
        value = kept[:, columns] + arrived[:, columns].astype(WIDE)
        if k == 0:
            own[...] = value
        else:
            sent[k - 1][...] = value.astype(LOW)


def swap(block, axis, step):
    size = lax.axis_size(axis)
    return lax.ppermute(block, axis, [(i, i ^ step) for i in range(size)])


def shards(
    tokens,
    routes,
    gate_weights,
    moe_gain,
    attn_gain,
    expert_in,
    expert_out,
    query_weight,
    key_weight,
    value_weight,
    cotangent,
):
    token_rows = tokens[0]
    route_rows = routes[0].T
    gate_rows = gate_weights[0].T
    token_count, model_width = token_rows.shape
    experts = lax.axis_size("exp")
    sections = lax.axis_size("sec")
    tp_size = lax.axis_size("tp")
    sec = lax.axis_index("sec")
    half = model_width // tp_size
    capacity = 3 * token_count // experts
    weight_first = expert_in[0, 0]
    weight_second = expert_out[0, 0]
    units = weight_first.shape[1]

    middle = max(2, experts // 2 + 1)
    groups = [list(range(middle - 1, 1, -1)), list(range(experts - 1, middle - 1, -1))]
    row_half, row_whole = shape_of((capacity, half)), shape_of((capacity, model_width))
    earlier = call(
        triangle,
        [shape_of((token_count, token_count))],
        [],
        flops=20 * token_count * token_count * model_width,
    )[0]
    *far_rows, near_rows, own_rows = call(
        functools.partial(prepare, experts),
        [row_half] * (experts - 2) + [row_whole] * 2,
        [token_rows, route_rows, moe_gain, earlier],
        [pltpu.VMEM((token_count, model_width), LOW)],
        flops=2 * 3 * token_count * token_count * model_width,
    )
    def hold(array, after):
        return call(idle, [], [], after=after, held=[array])[0]

    def joined(group):
        blocks = [swap(far_rows[k - 2], "exp", k) for k in group]
        return blocks[0] if len(blocks) == 1 else jnp.concatenate(blocks, axis=0)

    def total(away, kept, plain=False):
        arrived = swap(away, "tp", 1)
        if plain:
            return (kept + arrived.astype(WIDE)).astype(LOW)
        return call(add, [shape_of(away.shape)], [kept, arrived])[0]

    def through(rows, after):
        count = rows[0].shape[0]
        return call(
            functools.partial(expert, len(rows) - 1),
            [shape_of((count, half)), shape_of((count, half), WIDE)],
            [*rows, weight_first, weight_second],
            [pltpu.VMEM((count, units), LOW)],
            flops=4 * count * model_width * units,
            limit=24,
            after=after,
        )

    arriving = [joined(groups[0])]
    near = swap(near_rows, "exp", 1)
    later = [far_rows[k - 2] for k in groups[1]]
    loads = max(1, units // 512) + 1
    own_away, own_kept, weight_first, weight_second, *later = call(
        expert_first,
        [
            row_half,
            shape_of((capacity, half), WIDE),
            shape_of(weight_first.shape),
            shape_of(weight_second.shape),
        ],
        [own_rows, weight_first, weight_second],
        [pltpu.VMEM((capacity, units), LOW), pltpu.SemaphoreType.DMA((loads,))],
        flops=4 * capacity * model_width * units,
        remote=(1, 2),
        limit=44,
        held=later,
    )
    for k, rows in zip(groups[1], later):
        far_rows[k - 2] = rows
    arriving.append(joined(groups[1]))
    returned = {0: total(own_away, own_kept)}
    arriving[0] = hold(arriving[0], [own_away])
    others = [swap(arriving[0], "tp", 1)]
    high, low, upstream = call(
        functools.partial(mixing, experts),
        [shape_of((experts, token_count, capacity))] * 2 + [shape_of(cotangent.shape[1:])],
        [route_rows, gate_rows, earlier, cotangent[0]],
        [pltpu.SemaphoreType.DMA],
        remote=(3,),
        after=[arriving[0]],
    )
    others.append(swap(arriving[1], "tp", 1))

    def give_back(group, away, kept):
        mixed = total(away, kept)
        for i, k in enumerate(group):
            block = mixed if len(group) == 1 else mixed[i * capacity : (i + 1) * capacity]
            returned[k] = swap(block, "exp", k)
        return mixed

    away, kept = through([arriving[0], others[0]], [returned[0], high])
    near_away, near_kept = through([near], [away])
    mixed = give_back(groups[0], away, kept)
    returned[1] = swap(total(near_away, near_kept, plain=True), "exp", 1)
    away, kept = through([arriving[1], others[1]], [near_away, mixed])
    give_back(groups[1], away, kept)

    hidden_half = call(
        functools.partial(combine, experts),
        [shape_of((token_count, half))],
        [token_rows, high, low, *(returned[k] for k in range(experts))],
        flops=4 * 3 * token_count * token_count * half,
    )[0]

    hidden_other = swap(hidden_half, "tp", 1)

    def cycle(order, crossed):
        pairs = [(i, i ^ 1) for i in range(sections * tp_size)]
        targets = dict(pairs)
        for a, b in zip(order, order[1:] + order[:1]):
            for t in range(tp_size):
                targets[a * tp_size + t] = b * tp_size + (t ^ crossed if a == 0 else t)
        return lax.ppermute(hidden_half, ("sec", "tp"), list(targets.items()))

    moved = [[cycle([0, 2 * i, 2 * i + 1, 1], 0), cycle([0, 2 * i + 1, 2 * i, 1], 1)] for i in range(1, sections // 2)]
    beside = swap(hidden_half, "sec", 1)
    first = call(choose, [shape_of(hidden_half.shape)], [hidden_other, beside, *sum(moved, [])])[0]
    second = swap(first, "sec", 1)

    local_width = query_weight.shape[2]
    queries = call(
        project,
        [shape_of((token_count, local_width))],
        [hidden_half, hidden_other, attn_gain, query_weight[0]],
        flops=2 * token_count * model_width * local_width,
    )[0]
    heads = token_count // SEQ * (local_width // HD)
    away, lows, values, dkeys, dvalues = call(
        attend,
        [
            shape_of((token_count, model_width // 2)),
            shape_of((heads, SEQ, SEQ)),
            *[shape_of((token_count, local_width))] * 3,
        ],
        [first, second, queries, upstream, key_weight[0], value_weight[0]],
        [pltpu.VMEM((token_count, local_width), LOW)],
        flops=8 * token_count * model_width * local_width,
    )
    kept = call(
        keep,
        [shape_of((token_count, model_width // 2), WIDE)],
        [dkeys, dvalues, key_weight[0], value_weight[0]],
        flops=2 * token_count * model_width * local_width,
    )[0]
    context = call(
        contexts,
        [shape_of((token_count, local_width))],
        [lows, values, hidden_half],
        flops=2 * token_count * SEQ * local_width,
    )[0]

    own = model_width // (sections * tp_size)
    count = sections // 2 * tp_size
    both = sections * tp_size
    blocks = call(
        gather_term,
        [shape_of((token_count, own), WIDE)] + [shape_of((token_count, own))] * (count - 1),
        [kept, swap(away, "sec", 1)],
    )
    total = blocks[0]
    for k in range(1, count):
        pairs = []
        for i in range(both):
            section, t = i // tp_size, i % tp_size
            target = (section // 2 * tp_size + t) ^ k
            pairs.append((i, (target // tp_size * 2 + section % 2) * tp_size + target % tp_size))
        total = total + lax.ppermute(blocks[k], ("sec", "tp"), pairs).astype(WIDE)
    return (context[None], total.astype(LOW))


def solution(mesh):
    placed = (
        P("sec", "exp", None),
        P("sec", "exp", None),
        P("sec", "exp", None),
        P("sec", None),
        P("sec", None),
        P("sec", "exp", None, "tp"),
        P("sec", "exp", "tp", None),
        P("sec", None, "tp"),
        P("sec", None, "tp"),
        P("sec", None, "tp"),
        P("sec", "exp", "tp"),
    )
    return jax.shard_map(
        shards,
        mesh=mesh,
        in_specs=placed,
        out_specs=(P("sec", "exp", "tp"), P("exp", ("sec", "tp"))),
        check_vma=False,
    )
```

```python
import functools
import math

import jax
import jax.numpy as jnp
from jax import lax
from jax.experimental import pallas as pl
from jax.experimental.pallas import tpu as pltpu
from jax.sharding import PartitionSpec as P

HD = 128
SEQ = 128
EPS = 1e-05

LOW = jnp.bfloat16
WIDE = jnp.float32
VMEM = pl.BlockSpec(memory_space=pltpu.VMEM)
HBM = pl.BlockSpec(memory_space=pltpu.HBM)
ANY = pl.BlockSpec(memory_space=pl.ANY)
NT = (((1,), (1,)), ((), ()))
TN = (((0,), (0,)), ((), ()))


def matmul(a, b, dims=(((1,), (0,)), ((), ()))):
    return lax.dot_general(a, b, dims, preferred_element_type=WIDE)


def call(body, out_shape, inputs, scratch=(), flops=0, limit=16, remote=(), after=(), held=()):
    def size(x):
        return math.prod(x.shape) * jnp.dtype(x.dtype).itemsize

    count, results = len(inputs), len(out_shape)
    extra = len(after) + len(held)

    def run(*refs):
        outs = refs[count + extra : count + extra + results]
        return body(*refs[:count], *outs, *refs[count + extra + results + len(held) :])

    moved = sum(size(x) for x in inputs) + sum(size(x) for x in out_shape)
    return pl.pallas_call(
        run,
        out_shape=[*out_shape, *(shape_of(x.shape, x.dtype) for x in held)],
        in_specs=[HBM if i in remote else VMEM for i in range(count)] + [ANY] * extra,
        out_specs=[VMEM] * results + [ANY] * len(held),
        scratch_shapes=list(scratch),
        input_output_aliases={count + len(after) + i: results + i for i in range(len(held))},
        compiler_params=pltpu.CompilerParams(vmem_limit_bytes=limit * 2**20),
        cost_estimate=pl.CostEstimate(flops=flops, bytes_accessed=moved, transcendentals=0),
    )(*inputs, *after, *held)


def shape_of(dims, kind=LOW):
    return jax.ShapeDtypeStruct(dims, kind)


def part(index, width):
    return pl.ds(pl.multiple_of(index * width, width), width)


def triangle(out):
    source = lax.broadcasted_iota(jnp.int32, out.shape, 0)
    target = lax.broadcasted_iota(jnp.int32, out.shape, 1)
    out[...] = jnp.where(source < target, 1.0, 0.0).astype(LOW)


def places(routes, earlier, me, rows):
    labels = lax.broadcasted_iota(jnp.int32, (rows, 1), 0) ^ me
    first = routes[0:1, :] == labels
    second = routes[1:2, :] == labels
    either = first | second
    before = matmul(jnp.where(either, 1.0, 0.0).astype(LOW), earlier)
    return jnp.where(either, before, -1.0), first, second


def table(place, k, capacity):
    slots = lax.broadcasted_iota(jnp.int32, (capacity, place.shape[1]), 0).astype(WIDE)
    return jnp.where(place[k : k + 1, :] == slots, 1.0, 0.0).astype(LOW)


def prepare(experts, tokens, routes, gain, earlier, *outs):
    far, near, own, normed_ref = outs[:-3], outs[-3], outs[-2], outs[-1]
    me = lax.axis_index("exp")
    tp = lax.axis_index("tp")
    capacity, width = own.shape
    half = width // 2
    wide = tokens[...].astype(WIDE)
    average = jnp.mean(wide, axis=-1, keepdims=True)
    centred = wide - average
    spread = jnp.mean(centred * centred, axis=-1, keepdims=True)
    normed_ref[...] = (centred * lax.rsqrt(spread + EPS) * gain[...]).astype(LOW)
    place, _, _ = places(routes[...], earlier[...], me, max(16, experts))
    normed_half = normed_ref[:, part(tp, half)]
    for k in range(experts - 1, 1, -1):
        far[k - 2][...] = matmul(table(place, k, capacity), normed_half).astype(LOW)
    normed = normed_ref[...]
    near[...] = matmul(table(place, 1, capacity), normed).astype(LOW)
    own[...] = matmul(table(place, 0, capacity), normed).astype(LOW)


def mixing(experts, routes, gates, earlier, upstream, high, low, upstream_here, arrived):
    load = pltpu.make_async_copy(upstream, upstream_here, arrived)
    load.start()
    me = lax.axis_index("exp")
    token_count = routes.shape[1]
    capacity = high.shape[2]
    place, first, second = places(routes[...], earlier[...], me, max(16, experts))
    gate = jnp.where(first, gates[0:1, :], 0.0) + jnp.where(second, gates[1:2, :], 0.0)
    place = place.T
    gate = gate.T
    slots = lax.broadcasted_iota(jnp.int32, (token_count, capacity), 1).astype(WIDE)
    for k in range(experts):
        weight = jnp.where(place[:, k : k + 1] == slots, gate[:, k : k + 1], 0.0)
        upper = weight.astype(LOW)
        high[k] = upper
        low[k] = (weight - upper.astype(WIDE)).astype(LOW)
    load.wait()


def expert(split, *refs):
    rows, refs = refs[: 1 + split], refs[1 + split :]
    first, second, away, kept, inner = refs
    tp = lax.axis_index("tp")
    width, hidden = first.shape
    half = width // 2
    chunk = min(512, hidden)
    for c in range(hidden // chunk):
        columns = slice(c * chunk, (c + 1) * chunk)
        if split:
            value = matmul(rows[0][...], first[part(tp, half), columns])
            value = value + matmul(rows[1][...], first[part(1 - tp, half), columns])
        else:
            value = matmul(rows[0][...], first[:, columns])
        inner[:, columns] = jnp.maximum(value, 0.0).astype(LOW)
    away[...] = matmul(inner[...], second[:, part(1 - tp, half)]).astype(LOW)
    kept[...] = matmul(inner[...], second[:, part(tp, half)])


def expert_first(rows, first, second, away, kept, first_here, second_here, inner, arrived):
    tp = lax.axis_index("tp")
    width, hidden = first.shape
    half = width // 2
    chunk = min(512, hidden)
    columns = [slice(c * chunk, (c + 1) * chunk) for c in range(hidden // chunk)]
    loads = [
        pltpu.make_async_copy(first.at[:, c], first_here.at[:, c], arrived.at[i])
        for i, c in enumerate(columns)
    ]
    loads.append(pltpu.make_async_copy(second, second_here, arrived.at[len(columns)]))
    for load in loads:
        load.start()
    for c, load in zip(columns, loads):
        load.wait()
        inner[:, c] = jnp.maximum(matmul(rows[...], first_here[:, c]), 0.0).astype(LOW)
    loads[-1].wait()
    away[...] = matmul(inner[...], second_here[:, part(1 - tp, half)]).astype(LOW)
    kept[...] = matmul(inner[...], second_here[:, part(tp, half)])


def idle():
    pass


def add(kept, arrived, out):
    out[...] = (kept[...] + arrived[...].astype(WIDE)).astype(LOW)


def combine(experts, tokens, high, low, *refs):
    returned, out = refs[:-1], refs[-1]
    tp = lax.axis_index("tp")
    half = out.shape[1]
    mixed = tokens[:, part(tp, half)].astype(WIDE)
    for k in range(experts):
        rows = returned[k][...]
        mixed = mixed + (matmul(high[k], rows) + matmul(low[k], rows))
    out[...] = mixed.astype(LOW)


def project(mine, other, gain, weight, out):
    tp = lax.axis_index("tp")
    half = mine.shape[1]
    own = mine[...].astype(WIDE)
    rest = other[...].astype(WIDE)
    average = (
        jnp.sum(own, axis=-1, keepdims=True) + jnp.sum(rest, axis=-1, keepdims=True)
    ) / (2 * half)
    own = own - average
    rest = rest - average
    spread = (
        jnp.sum(own * own, axis=-1, keepdims=True) + jnp.sum(rest * rest, axis=-1, keepdims=True)
    ) / (2 * half)
    factor = lax.rsqrt(spread + EPS)
    own = (own * factor * gain[:, part(tp, half)]).astype(LOW)
    rest = (rest * factor * gain[:, part(1 - tp, half)]).astype(LOW)
    value = matmul(own, weight[part(tp, half), :]) + matmul(rest, weight[part(1 - tp, half), :])
    out[...] = value.astype(LOW)


def choose(order, *refs):
    sec = lax.axis_index("sec")
    out = refs[-1]
    for i, source in zip(order, refs[:-1], strict=True):

        @pl.when(sec == i)
        def _():
            out[...] = source[...]


def attend(
    first, second, queries, upstream, key_w, value_w, away, low_ref, values, dkeys, dvalues, keys
):
    tp = lax.axis_index("tp")
    sec = lax.axis_index("sec")
    token_count, half = first.shape
    scale = 1.0 / math.sqrt(HD)

    @pl.when(sec != 0)
    def _():
        crossed = ((sec > 1) & (sec % 2 == 1)).astype(jnp.int32)
        place = tp ^ crossed
        for weight, target in ((key_w, keys), (value_w, values)):
            value = matmul(first[...], weight[part(place, half), :])
            value = value + matmul(second[...], weight[part(1 - place, half), :])
            target[...] = value.astype(LOW)
        heads = [
            (slice(s * SEQ, (s + 1) * SEQ), slice(h * HD, (h + 1) * HD))
            for s in range(token_count // SEQ)
            for h in range(queries.shape[1] // HD)
        ]
        scores = [matmul(keys[at], queries[at], NT) for at in heads]
        dprobs = [matmul(values[at], upstream[at], NT) for at in heads]
        powers = [jnp.exp(x * scale) for x in scores]
        probs = [x * (1.0 / jnp.sum(x, axis=0, keepdims=True)) for x in powers]
        lows = [x.astype(LOW) for x in probs]
        for at, low in zip(heads, lows):
            dvalues[at] = matmul(low, upstream[at]).astype(LOW)
        rowdots = [jnp.sum(x * y, axis=0, keepdims=True) for x, y in zip(dprobs, probs)]
        dscores = [
            (y * (x - z)).astype(LOW) for x, y, z in zip(dprobs, probs, rowdots)
        ]
        for at, dscore in zip(heads, dscores):
            dkeys[at] = (matmul(dscore, queries[at]) * scale).astype(LOW)
        for i, low in enumerate(lows):
            low_ref[i] = low
        terms(dkeys, dvalues, key_w, value_w, 1 - sec % 2, away)

    @pl.when(sec == 0)
    def _():
        away[...] = jnp.zeros_like(away)


def terms(dkeys, dvalues, key_w, value_w, parity, out):
    pairs = lax.axis_size("sec") // 2
    block = out.shape[1] // pairs
    for i in range(pairs):
        rows = part(2 * i + parity, block)
        value = matmul(dkeys[...], key_w[rows, :], NT)
        value = value + matmul(dvalues[...], value_w[rows, :], NT)
        out[:, i * block : (i + 1) * block] = value.astype(out.dtype)


def keep(dkeys, dvalues, key_w, value_w, out):
    sec = lax.axis_index("sec")

    @pl.when(sec != 0)
    def _():
        terms(dkeys, dvalues, key_w, value_w, sec % 2, out)

    @pl.when(sec == 0)
    def _():
        out[...] = jnp.zeros_like(out)


def contexts(low_ref, values, hidden, out):
    sec = lax.axis_index("sec")
    head_count = values.shape[1] // HD

    @pl.when(sec == 0)
    def _():
        out[...] = hidden[...]

    @pl.when(sec != 0)
    def _():
        for i in range(low_ref.shape[0]):
            s, h = i // head_count, i % head_count
            at = slice(s * SEQ, (s + 1) * SEQ), slice(h * HD, (h + 1) * HD)
            out[at] = matmul(low_ref[i], values[at], TN).astype(LOW)


def gather_term(kept, arrived, own, *sent):
    tp = lax.axis_index("tp")
    here = lax.axis_index("sec") // 2 * lax.axis_size("tp") + tp
    width = own.shape[1]
    for k in range(len(sent) + 1):
        columns = part(here ^ k, width)
        value = kept[:, columns] + arrived[:, columns].astype(WIDE)
        if k == 0:
            own[...] = value
        else:
            sent[k - 1][...] = value.astype(LOW)


def swap(block, axis, step):
    size = lax.axis_size(axis)
    return lax.ppermute(block, axis, [(i, i ^ step) for i in range(size)])


def shards(
    tokens,
    routes,
    gate_weights,
    moe_gain,
    attn_gain,
    expert_in,
    expert_out,
    query_weight,
    key_weight,
    value_weight,
    cotangent,
):
    token_rows = tokens[0]
    route_rows = routes[0].T
    gate_rows = gate_weights[0].T
    token_count, model_width = token_rows.shape
    experts = lax.axis_size("exp")
    sections = lax.axis_size("sec")
    tp_size = lax.axis_size("tp")
    sec = lax.axis_index("sec")
    half = model_width // tp_size
    capacity = 3 * token_count // experts
    weight_first = expert_in[0, 0]
    weight_second = expert_out[0, 0]
    units = weight_first.shape[1]

    middle = max(2, experts // 2 + 1)
    groups = [list(range(middle - 1, 1, -1)), list(range(experts - 1, middle - 1, -1))]
    row_half, row_whole = shape_of((capacity, half)), shape_of((capacity, model_width))
    earlier = call(
        triangle,
        [shape_of((token_count, token_count))],
        [],
        flops=20 * token_count * token_count * model_width,
    )[0]
    *far_rows, near_rows, own_rows = call(
        functools.partial(prepare, experts),
        [row_half] * (experts - 2) + [row_whole] * 2,
        [token_rows, route_rows, moe_gain, earlier],
        [pltpu.VMEM((token_count, model_width), LOW)],
        flops=2 * 3 * token_count * token_count * model_width,
    )
    def hold(array, after):
        return call(idle, [], [], after=after, held=[array])[0]

    def joined(group):
        blocks = [swap(far_rows[k - 2], "exp", k) for k in group]
        return blocks[0] if len(blocks) == 1 else jnp.concatenate(blocks, axis=0)

    def total(away, kept, plain=False):
        arrived = swap(away, "tp", 1)
        if plain:
            return (kept + arrived.astype(WIDE)).astype(LOW)
        return call(add, [shape_of(away.shape)], [kept, arrived])[0]

    def through(rows, after):
        count = rows[0].shape[0]
        return call(
            functools.partial(expert, len(rows) - 1),
            [shape_of((count, half)), shape_of((count, half), WIDE)],
            [*rows, weight_first, weight_second],
            [pltpu.VMEM((count, units), LOW)],
            flops=4 * count * model_width * units,
            limit=24,
            after=after,
        )

    arriving = [joined(groups[0])]
    near = swap(near_rows, "exp", 1)
    later = [far_rows[k - 2] for k in groups[1]]
    loads = max(1, units // 512) + 1
    own_away, own_kept, weight_first, weight_second, *later = call(
        expert_first,
        [
            row_half,
            shape_of((capacity, half), WIDE),
            shape_of(weight_first.shape),
            shape_of(weight_second.shape),
        ],
        [own_rows, weight_first, weight_second],
        [pltpu.VMEM((capacity, units), LOW), pltpu.SemaphoreType.DMA((loads,))],
        flops=4 * capacity * model_width * units,
        remote=(1, 2),
        limit=44,
        held=later,
    )
    for k, rows in zip(groups[1], later):
        far_rows[k - 2] = rows
    arriving.append(joined(groups[1]))
    returned = {0: total(own_away, own_kept)}
    arriving[0] = hold(arriving[0], [own_away])
    others = [swap(arriving[0], "tp", 1)]
    high, low, upstream = call(
        functools.partial(mixing, experts),
        [shape_of((experts, token_count, capacity))] * 2 + [shape_of(cotangent.shape[1:])],
        [route_rows, gate_rows, earlier, cotangent[0]],
        [pltpu.SemaphoreType.DMA],
        remote=(3,),
        after=[arriving[0]],
    )
    others.append(swap(arriving[1], "tp", 1))

    def give_back(group, away, kept):
        mixed = total(away, kept)
        for i, k in enumerate(group):
            block = mixed if len(group) == 1 else mixed[i * capacity : (i + 1) * capacity]
            returned[k] = swap(block, "exp", k)
        return mixed

    away, kept = through([arriving[0], others[0]], [returned[0], high])
    near_away, near_kept = through([near], [away])
    mixed = give_back(groups[0], away, kept)
    returned[1] = swap(total(near_away, near_kept, plain=True), "exp", 1)
    away, kept = through([arriving[1], others[1]], [near_away, mixed])
    give_back(groups[1], away, kept)

    hidden_half = call(
        functools.partial(combine, experts),
        [shape_of((token_count, half))],
        [token_rows, high, low, *(returned[k] for k in range(experts))],
        flops=4 * 3 * token_count * token_count * half,
    )[0]

    hidden_other = swap(hidden_half, "tp", 1)

    def cycle(order, crossed):
        pairs = [(i, i ^ 1) for i in range(sections * tp_size)]
        targets = dict(pairs)
        for a, b in zip(order, order[1:] + order[:1]):
            for t in range(tp_size):
                targets[a * tp_size + t] = b * tp_size + (t ^ crossed if a == 0 else t)
        return lax.ppermute(hidden_half, ("sec", "tp"), list(targets.items()))

    beside = swap(hidden_half, "sec", 1)
    choices = {}
    for i in range(1, sections // 2):
        choices[2 * i] = cycle([0, 2 * i, 2 * i + 1, 1], 0)
        choices.setdefault(0, hidden_other)
        choices[2 * i + 1] = cycle([0, 2 * i + 1, 2 * i, 1], 1)
    choices |= {0: hidden_other, 1: beside}
    first = call(
        functools.partial(choose, list(choices)), [shape_of(hidden_half.shape)], list(choices.values())
    )[0]
    second = swap(first, "sec", 1)

    local_width = query_weight.shape[2]
    queries = call(
        project,
        [shape_of((token_count, local_width))],
        [hidden_half, hidden_other, attn_gain, query_weight[0]],
        flops=2 * token_count * model_width * local_width,
    )[0]
    heads = token_count // SEQ * (local_width // HD)
    away, lows, values, dkeys, dvalues = call(
        attend,
        [
            shape_of((token_count, model_width // 2)),
            shape_of((heads, SEQ, SEQ)),
            *[shape_of((token_count, local_width))] * 3,
        ],
        [first, second, queries, upstream, key_weight[0], value_weight[0]],
        [pltpu.VMEM((token_count, local_width), LOW)],
        flops=8 * token_count * model_width * local_width,
    )
    kept = call(
        keep,
        [shape_of((token_count, model_width // 2), WIDE)],
        [dkeys, dvalues, key_weight[0], value_weight[0]],
        flops=2 * token_count * model_width * local_width,
    )[0]
    context = call(
        contexts,
        [shape_of((token_count, local_width))],
        [lows, values, hidden_half],
        flops=2 * token_count * SEQ * local_width,
    )[0]

    own = model_width // (sections * tp_size)
    count = sections // 2 * tp_size
    both = sections * tp_size
    blocks = call(
        gather_term,
        [shape_of((token_count, own), WIDE)] + [shape_of((token_count, own))] * (count - 1),
        [kept, swap(away, "sec", 1)],
    )
    total = blocks[0]
    for k in range(count - 1, 0, -1):
        pairs = []
        for i in range(both):
            section, t = i // tp_size, i % tp_size
            target = (section // 2 * tp_size + t) ^ k
            pairs.append((i, (target // tp_size * 2 + section % 2) * tp_size + target % tp_size))
        total = total + lax.ppermute(blocks[k], ("sec", "tp"), pairs).astype(WIDE)
    return (context[None], total.astype(LOW))


def solution(mesh):
    placed = (
        P("sec", "exp", None),
        P("sec", "exp", None),
        P("sec", "exp", None),
        P("sec", None),
        P("sec", None),
        P("sec", "exp", None, "tp"),
        P("sec", "exp", "tp", None),
        P("sec", None, "tp"),
        P("sec", None, "tp"),
        P("sec", None, "tp"),
        P("sec", "exp", "tp"),
    )
    return jax.shard_map(
        shards,
        mesh=mesh,
        in_specs=placed,
        out_specs=(P("sec", "exp", "tp"), P("exp", ("sec", "tp"))),
        check_vma=False,
    )
```

```python
import functools
import math

import jax
import jax.numpy as jnp
from jax import lax
from jax.experimental import pallas as pl
from jax.experimental.pallas import tpu as pltpu
from jax.sharding import PartitionSpec as P

HD = 128
SEQ = 128
EPS = 1e-05

LOW = jnp.bfloat16
WIDE = jnp.float32
VMEM = pl.BlockSpec(memory_space=pltpu.VMEM)
HBM = pl.BlockSpec(memory_space=pltpu.HBM)
ANY = pl.BlockSpec(memory_space=pl.ANY)
NT = (((1,), (1,)), ((), ()))
TN = (((0,), (0,)), ((), ()))


def matmul(a, b, dims=(((1,), (0,)), ((), ()))):
    return lax.dot_general(a, b, dims, preferred_element_type=WIDE)


def call(body, out_shape, inputs, scratch=(), flops=0, limit=16, remote=(), after=(), held=()):
    def size(x):
        return math.prod(x.shape) * jnp.dtype(x.dtype).itemsize

    count, results = len(inputs), len(out_shape)
    extra = len(after) + len(held)

    def run(*refs):
        outs = refs[count + extra : count + extra + results]
        return body(*refs[:count], *outs, *refs[count + extra + results + len(held) :])

    moved = sum(size(x) for x in inputs) + sum(size(x) for x in out_shape)
    return pl.pallas_call(
        run,
        out_shape=[*out_shape, *(shape_of(x.shape, x.dtype) for x in held)],
        in_specs=[HBM if i in remote else VMEM for i in range(count)] + [ANY] * extra,
        out_specs=[VMEM] * results + [ANY] * len(held),
        scratch_shapes=list(scratch),
        input_output_aliases={count + len(after) + i: results + i for i in range(len(held))},
        compiler_params=pltpu.CompilerParams(vmem_limit_bytes=limit * 2**20),
        cost_estimate=pl.CostEstimate(flops=flops, bytes_accessed=moved, transcendentals=0),
    )(*inputs, *after, *held)


def shape_of(dims, kind=LOW):
    return jax.ShapeDtypeStruct(dims, kind)


def part(index, width):
    return pl.ds(pl.multiple_of(index * width, width), width)


def triangle(out):
    source = lax.broadcasted_iota(jnp.int32, out.shape, 0)
    target = lax.broadcasted_iota(jnp.int32, out.shape, 1)
    out[...] = jnp.where(source < target, 1.0, 0.0).astype(LOW)


def places(routes, earlier, me, rows):
    labels = lax.broadcasted_iota(jnp.int32, (rows, 1), 0) ^ me
    first = routes[0:1, :] == labels
    second = routes[1:2, :] == labels
    either = first | second
    before = matmul(jnp.where(either, 1.0, 0.0).astype(LOW), earlier)
    return jnp.where(either, before, -1.0), first, second


def table(place, k, capacity):
    slots = lax.broadcasted_iota(jnp.int32, (capacity, place.shape[1]), 0).astype(WIDE)
    return jnp.where(place[k : k + 1, :] == slots, 1.0, 0.0).astype(LOW)


def prepare(experts, tokens, routes, gain, earlier, *outs):
    far, near, own, normed_ref = outs[:-3], outs[-3], outs[-2], outs[-1]
    me = lax.axis_index("exp")
    tp = lax.axis_index("tp")
    capacity, width = own.shape
    half = width // 2
    wide = tokens[...].astype(WIDE)
    average = jnp.mean(wide, axis=-1, keepdims=True)
    centred = wide - average
    spread = jnp.mean(centred * centred, axis=-1, keepdims=True)
    normed_ref[...] = (centred * lax.rsqrt(spread + EPS) * gain[...]).astype(LOW)
    place, _, _ = places(routes[...], earlier[...], me, max(16, experts))
    normed_half = normed_ref[:, part(tp, half)]
    for k in range(experts - 1, 1, -1):
        far[k - 2][...] = matmul(table(place, k, capacity), normed_half).astype(LOW)
    normed = normed_ref[...]
    near[...] = matmul(table(place, 1, capacity), normed).astype(LOW)
    own[...] = matmul(table(place, 0, capacity), normed).astype(LOW)


def mixing(experts, routes, gates, earlier, upstream, high, low, upstream_here, arrived):
    load = pltpu.make_async_copy(upstream, upstream_here, arrived)
    load.start()
    me = lax.axis_index("exp")
    token_count = routes.shape[1]
    capacity = high.shape[2]
    place, first, second = places(routes[...], earlier[...], me, max(16, experts))
    gate = jnp.where(first, gates[0:1, :], 0.0) + jnp.where(second, gates[1:2, :], 0.0)
    place = place.T
    gate = gate.T
    slots = lax.broadcasted_iota(jnp.int32, (token_count, capacity), 1).astype(WIDE)
    for k in range(experts):
        weight = jnp.where(place[:, k : k + 1] == slots, gate[:, k : k + 1], 0.0)
        upper = weight.astype(LOW)
        high[k] = upper
        low[k] = (weight - upper.astype(WIDE)).astype(LOW)
    load.wait()


def expert(split, *refs):
    rows, refs = refs[: 1 + split], refs[1 + split :]
    first, second, away, kept, inner = refs
    tp = lax.axis_index("tp")
    width, hidden = first.shape
    half = width // 2
    chunk = min(512, hidden)
    for c in range(hidden // chunk):
        columns = slice(c * chunk, (c + 1) * chunk)
        if split:
            value = matmul(rows[0][...], first[part(tp, half), columns])
            value = value + matmul(rows[1][...], first[part(1 - tp, half), columns])
        else:
            value = matmul(rows[0][...], first[:, columns])
        inner[:, columns] = jnp.maximum(value, 0.0).astype(LOW)
    away[...] = matmul(inner[...], second[:, part(1 - tp, half)]).astype(LOW)
    kept[...] = matmul(inner[...], second[:, part(tp, half)])


def expert_first(rows, first, second, away, kept, first_here, second_here, inner, arrived):
    tp = lax.axis_index("tp")
    width, hidden = first.shape
    half = width // 2
    chunk = min(512, hidden)
    columns = [slice(c * chunk, (c + 1) * chunk) for c in range(hidden // chunk)]
    loads = [
        pltpu.make_async_copy(first.at[:, c], first_here.at[:, c], arrived.at[i])
        for i, c in enumerate(columns)
    ]
    loads.append(pltpu.make_async_copy(second, second_here, arrived.at[len(columns)]))
    for load in loads:
        load.start()
    for c, load in zip(columns, loads):
        load.wait()
        inner[:, c] = jnp.maximum(matmul(rows[...], first_here[:, c]), 0.0).astype(LOW)
    loads[-1].wait()
    away[...] = matmul(inner[...], second_here[:, part(1 - tp, half)]).astype(LOW)
    kept[...] = matmul(inner[...], second_here[:, part(tp, half)])


def idle():
    pass


def add(kept, arrived, out):
    out[...] = (kept[...] + arrived[...].astype(WIDE)).astype(LOW)


def combine(experts, tokens, high, low, *refs):
    returned, out = refs[:-1], refs[-1]
    tp = lax.axis_index("tp")
    half = out.shape[1]
    mixed = tokens[:, part(tp, half)].astype(WIDE)
    for k in range(experts):
        rows = returned[k][...]
        mixed = mixed + (matmul(high[k], rows) + matmul(low[k], rows))
    out[...] = mixed.astype(LOW)


def project(mine, other, gain, weight, out):
    tp = lax.axis_index("tp")
    half = mine.shape[1]
    own = mine[...].astype(WIDE)
    rest = other[...].astype(WIDE)
    average = (
        jnp.sum(own, axis=-1, keepdims=True) + jnp.sum(rest, axis=-1, keepdims=True)
    ) / (2 * half)
    own = own - average
    rest = rest - average
    spread = (
        jnp.sum(own * own, axis=-1, keepdims=True) + jnp.sum(rest * rest, axis=-1, keepdims=True)
    ) / (2 * half)
    factor = lax.rsqrt(spread + EPS)
    own = (own * factor * gain[:, part(tp, half)]).astype(LOW)
    rest = (rest * factor * gain[:, part(1 - tp, half)]).astype(LOW)
    value = matmul(own, weight[part(tp, half), :]) + matmul(rest, weight[part(1 - tp, half), :])
    out[...] = value.astype(LOW)


def choose(order, *refs):
    sec = lax.axis_index("sec")
    out = refs[-1]
    for i, source in zip(order, refs[:-1], strict=True):

        @pl.when(sec == i)
        def _():
            out[...] = source[...]


def attend(
    first, second, queries, upstream, key_w, value_w, away, low_ref, values, dkeys, dvalues, keys
):
    tp = lax.axis_index("tp")
    sec = lax.axis_index("sec")
    token_count, half = first.shape
    scale = 1.0 / math.sqrt(HD)

    @pl.when(sec != 0)
    def _():
        crossed = ((sec > 1) & (sec % 2 == 1)).astype(jnp.int32)
        place = tp ^ crossed
        for weight, target in ((key_w, keys), (value_w, values)):
            value = matmul(first[...], weight[part(place, half), :])
            value = value + matmul(second[...], weight[part(1 - place, half), :])
            target[...] = value.astype(LOW)
        heads = [
            (slice(s * SEQ, (s + 1) * SEQ), slice(h * HD, (h + 1) * HD))
            for s in range(token_count // SEQ)
            for h in range(queries.shape[1] // HD)
        ]
        scores = [matmul(keys[at], queries[at], NT) for at in heads]
        dprobs = [matmul(values[at], upstream[at], NT) for at in heads]
        powers = [jnp.exp(x * scale) for x in scores]
        probs = [x * (1.0 / jnp.sum(x, axis=0, keepdims=True)) for x in powers]
        lows = [x.astype(LOW) for x in probs]
        for at, low in zip(heads, lows):
            dvalues[at] = matmul(low, upstream[at]).astype(LOW)
        rowdots = [jnp.sum(x * y, axis=0, keepdims=True) for x, y in zip(dprobs, probs)]
        dscores = [
            (y * (x - z)).astype(LOW) for x, y, z in zip(dprobs, probs, rowdots)
        ]
        for at, dscore in zip(heads, dscores):
            dkeys[at] = (matmul(dscore, queries[at]) * scale).astype(LOW)
        for i, low in enumerate(lows):
            low_ref[i] = low
        terms(dkeys, dvalues, key_w, value_w, 1 - sec % 2, away)

    @pl.when(sec == 0)
    def _():
        away[...] = jnp.zeros_like(away)


def terms(dkeys, dvalues, key_w, value_w, parity, out):
    pairs = lax.axis_size("sec") // 2
    block = out.shape[1] // pairs
    for i in range(pairs):
        rows = part(2 * i + parity, block)
        value = matmul(dkeys[...], key_w[rows, :], NT)
        value = value + matmul(dvalues[...], value_w[rows, :], NT)
        out[:, i * block : (i + 1) * block] = value.astype(out.dtype)


def keep(dkeys, dvalues, key_w, value_w, out):
    sec = lax.axis_index("sec")

    @pl.when(sec != 0)
    def _():
        terms(dkeys, dvalues, key_w, value_w, sec % 2, out)

    @pl.when(sec == 0)
    def _():
        out[...] = jnp.zeros_like(out)


def contexts(low_ref, values, hidden, out):
    sec = lax.axis_index("sec")
    head_count = values.shape[1] // HD

    @pl.when(sec == 0)
    def _():
        out[...] = hidden[...]

    @pl.when(sec != 0)
    def _():
        for i in range(low_ref.shape[0]):
            s, h = i // head_count, i % head_count
            at = slice(s * SEQ, (s + 1) * SEQ), slice(h * HD, (h + 1) * HD)
            out[at] = matmul(low_ref[i], values[at], TN).astype(LOW)


def gather_term(kept, arrived, own, *sent):
    tp = lax.axis_index("tp")
    here = lax.axis_index("sec") // 2 * lax.axis_size("tp") + tp
    width = own.shape[1]
    for k in range(len(sent) + 1):
        columns = part(here ^ k, width)
        value = kept[:, columns] + arrived[:, columns].astype(WIDE)
        if k == 0:
            own[...] = value
        else:
            sent[k - 1][...] = value.astype(LOW)


def swap(block, axis, step):
    size = lax.axis_size(axis)
    return lax.ppermute(block, axis, [(i, i ^ step) for i in range(size)])


def shards(
    tokens,
    routes,
    gate_weights,
    moe_gain,
    attn_gain,
    expert_in,
    expert_out,
    query_weight,
    key_weight,
    value_weight,
    cotangent,
):
    token_rows = tokens[0]
    route_rows = routes[0].T
    gate_rows = gate_weights[0].T
    token_count, model_width = token_rows.shape
    experts = lax.axis_size("exp")
    sections = lax.axis_size("sec")
    tp_size = lax.axis_size("tp")
    sec = lax.axis_index("sec")
    half = model_width // tp_size
    capacity = 3 * token_count // experts
    weight_first = expert_in[0, 0]
    weight_second = expert_out[0, 0]
    units = weight_first.shape[1]

    middle = max(2, experts // 2 + 1)
    groups = [list(range(middle - 1, 1, -1)), list(range(experts - 1, middle - 1, -1))]
    row_half, row_whole = shape_of((capacity, half)), shape_of((capacity, model_width))
    earlier = call(
        triangle,
        [shape_of((token_count, token_count))],
        [],
        flops=20 * token_count * token_count * model_width,
    )[0]
    *far_rows, near_rows, own_rows = call(
        functools.partial(prepare, experts),
        [row_half] * (experts - 2) + [row_whole] * 2,
        [token_rows, route_rows, moe_gain, earlier],
        [pltpu.VMEM((token_count, model_width), LOW)],
        flops=2 * 3 * token_count * token_count * model_width,
    )
    def hold(array, after):
        return call(idle, [], [], after=after, held=[array])[0]

    def joined(group):
        blocks = [swap(far_rows[k - 2], "exp", k) for k in group]
        return blocks[0] if len(blocks) == 1 else jnp.concatenate(blocks, axis=0)

    def total(away, kept, plain=False):
        arrived = swap(away, "tp", 1)
        if plain:
            return (kept + arrived.astype(WIDE)).astype(LOW)
        return call(add, [shape_of(away.shape)], [kept, arrived])[0]

    def through(rows, after):
        count = rows[0].shape[0]
        return call(
            functools.partial(expert, len(rows) - 1),
            [shape_of((count, half)), shape_of((count, half), WIDE)],
            [*rows, weight_first, weight_second],
            [pltpu.VMEM((count, units), LOW)],
            flops=4 * count * model_width * units,
            limit=24,
            after=after,
        )

    arriving = [joined(groups[0])]
    near = swap(near_rows, "exp", 1)
    later = [far_rows[k - 2] for k in groups[1]]
    loads = max(1, units // 512) + 1
    own_away, own_kept, weight_first, weight_second, *later = call(
        expert_first,
        [
            row_half,
            shape_of((capacity, half), WIDE),
            shape_of(weight_first.shape),
            shape_of(weight_second.shape),
        ],
        [own_rows, weight_first, weight_second],
        [pltpu.VMEM((capacity, units), LOW), pltpu.SemaphoreType.DMA((loads,))],
        flops=4 * capacity * model_width * units,
        remote=(1, 2),
        limit=44,
        held=later,
    )
    for k, rows in zip(groups[1], later):
        far_rows[k - 2] = rows
    arriving.append(joined(groups[1]))
    returned = {0: total(own_away, own_kept)}
    arriving[0] = hold(arriving[0], [own_away])
    others = [swap(arriving[0], "tp", 1)]
    high, low, upstream = call(
        functools.partial(mixing, experts),
        [shape_of((experts, token_count, capacity))] * 2 + [shape_of(cotangent.shape[1:])],
        [route_rows, gate_rows, earlier, cotangent[0]],
        [pltpu.SemaphoreType.DMA],
        remote=(3,),
        after=[arriving[0]],
    )
    others.append(swap(arriving[1], "tp", 1))

    def give_back(group, away, kept):
        mixed = total(away, kept)
        for i, k in enumerate(group):
            block = mixed if len(group) == 1 else mixed[i * capacity : (i + 1) * capacity]
            returned[k] = swap(block, "exp", k)
        return mixed

    away, kept = through([arriving[0], others[0]], [returned[0], high])
    near_away, near_kept = through([near], [away])
    mixed = give_back(groups[0], away, kept)
    returned[1] = swap(total(near_away, near_kept, plain=True), "exp", 1)
    away, kept = through([arriving[1], others[1]], [near_away, mixed])
    give_back(groups[1], away, kept)

    hidden_half = call(
        functools.partial(combine, experts),
        [shape_of((token_count, half))],
        [token_rows, high, low, *(returned[k] for k in range(experts))],
        flops=4 * 3 * token_count * token_count * half,
    )[0]

    hidden_other = swap(hidden_half, "tp", 1)

    def cycle(order, crossed):
        pairs = [(i, i ^ 1) for i in range(sections * tp_size)]
        targets = dict(pairs)
        for a, b in zip(order, order[1:] + order[:1]):
            for t in range(tp_size):
                targets[a * tp_size + t] = b * tp_size + (t ^ crossed if a == 0 else t)
        return lax.ppermute(hidden_half, ("sec", "tp"), list(targets.items()))

    beside = swap(hidden_half, "sec", 1)
    choices = {}
    for i in range(1, sections // 2):
        choices[2 * i] = cycle([0, 2 * i, 2 * i + 1, 1], 0)
        choices.setdefault(0, hidden_other)
        choices[2 * i + 1] = cycle([0, 2 * i + 1, 2 * i, 1], 1)
    choices |= {0: hidden_other, 1: beside}
    first = call(
        functools.partial(choose, list(choices)), [shape_of(hidden_half.shape)], list(choices.values())
    )[0]
    second = swap(first, "sec", 1)

    local_width = query_weight.shape[2]
    queries = call(
        project,
        [shape_of((token_count, local_width))],
        [hidden_half, hidden_other, attn_gain, query_weight[0]],
        flops=2 * token_count * model_width * local_width,
        after=list(choices.values())[:1],
    )[0]
    heads = token_count // SEQ * (local_width // HD)
    away, lows, values, dkeys, dvalues = call(
        attend,
        [
            shape_of((token_count, model_width // 2)),
            shape_of((heads, SEQ, SEQ)),
            *[shape_of((token_count, local_width))] * 3,
        ],
        [first, second, queries, upstream, key_weight[0], value_weight[0]],
        [pltpu.VMEM((token_count, local_width), LOW)],
        flops=8 * token_count * model_width * local_width,
    )
    kept = call(
        keep,
        [shape_of((token_count, model_width // 2), WIDE)],
        [dkeys, dvalues, key_weight[0], value_weight[0]],
        flops=2 * token_count * model_width * local_width,
    )[0]
    context = call(
        contexts,
        [shape_of((token_count, local_width))],
        [lows, values, hidden_half],
        flops=2 * token_count * SEQ * local_width,
    )[0]

    own = model_width // (sections * tp_size)
    count = sections // 2 * tp_size
    both = sections * tp_size
    blocks = call(
        gather_term,
        [shape_of((token_count, own), WIDE)] + [shape_of((token_count, own))] * (count - 1),
        [kept, swap(away, "sec", 1)],
    )
    total = blocks[0]
    for k in range(count - 1, 0, -1):
        pairs = []
        for i in range(both):
            section, t = i // tp_size, i % tp_size
            target = (section // 2 * tp_size + t) ^ k
            pairs.append((i, (target // tp_size * 2 + section % 2) * tp_size + target % tp_size))
        total = total + lax.ppermute(blocks[k], ("sec", "tp"), pairs).astype(WIDE)
    return (context[None], total.astype(LOW))


def solution(mesh):
    placed = (
        P("sec", "exp", None),
        P("sec", "exp", None),
        P("sec", "exp", None),
        P("sec", None),
        P("sec", None),
        P("sec", "exp", None, "tp"),
        P("sec", "exp", "tp", None),
        P("sec", None, "tp"),
        P("sec", None, "tp"),
        P("sec", None, "tp"),
        P("sec", "exp", "tp"),
    )
    return jax.shard_map(
        shards,
        mesh=mesh,
        in_specs=placed,
        out_specs=(P("sec", "exp", "tp"), P("exp", ("sec", "tp"))),
        check_vma=False,
    )
```

```python
import functools
import math

import jax
import jax.numpy as jnp
from jax import lax
from jax.experimental import pallas as pl
from jax.experimental.pallas import tpu as pltpu
from jax.sharding import PartitionSpec as P

HD = 128
SEQ = 128
EPS = 1e-05

LOW = jnp.bfloat16
WIDE = jnp.float32
VMEM = pl.BlockSpec(memory_space=pltpu.VMEM)
HBM = pl.BlockSpec(memory_space=pltpu.HBM)
ANY = pl.BlockSpec(memory_space=pl.ANY)
NT = (((1,), (1,)), ((), ()))
TN = (((0,), (0,)), ((), ()))


def matmul(a, b, dims=(((1,), (0,)), ((), ()))):
    return lax.dot_general(a, b, dims, preferred_element_type=WIDE)


def call(body, out_shape, inputs, scratch=(), flops=0, limit=16, remote=(), after=(), held=()):
    def size(x):
        return math.prod(x.shape) * jnp.dtype(x.dtype).itemsize

    count, results = len(inputs), len(out_shape)
    extra = len(after) + len(held)

    def run(*refs):
        outs = refs[count + extra : count + extra + results]
        return body(*refs[:count], *outs, *refs[count + extra + results + len(held) :])

    moved = sum(size(x) for x in inputs) + sum(size(x) for x in out_shape)
    return pl.pallas_call(
        run,
        out_shape=[*out_shape, *(shape_of(x.shape, x.dtype) for x in held)],
        in_specs=[HBM if i in remote else VMEM for i in range(count)] + [ANY] * extra,
        out_specs=[VMEM] * results + [ANY] * len(held),
        scratch_shapes=list(scratch),
        input_output_aliases={count + len(after) + i: results + i for i in range(len(held))},
        compiler_params=pltpu.CompilerParams(vmem_limit_bytes=limit * 2**20),
        cost_estimate=pl.CostEstimate(flops=flops, bytes_accessed=moved, transcendentals=0),
    )(*inputs, *after, *held)


def shape_of(dims, kind=LOW):
    return jax.ShapeDtypeStruct(dims, kind)


def part(index, width):
    return pl.ds(pl.multiple_of(index * width, width), width)


def triangle(out):
    source = lax.broadcasted_iota(jnp.int32, out.shape, 0)
    target = lax.broadcasted_iota(jnp.int32, out.shape, 1)
    out[...] = jnp.where(source < target, 1.0, 0.0).astype(LOW)


def places(routes, earlier, me, rows):
    labels = lax.broadcasted_iota(jnp.int32, (rows, 1), 0) ^ me
    first = routes[0:1, :] == labels
    second = routes[1:2, :] == labels
    either = first | second
    before = matmul(jnp.where(either, 1.0, 0.0).astype(LOW), earlier)
    return jnp.where(either, before, -1.0), first, second


def table(place, k, capacity):
    slots = lax.broadcasted_iota(jnp.int32, (capacity, place.shape[1]), 0).astype(WIDE)
    return jnp.where(place[k : k + 1, :] == slots, 1.0, 0.0).astype(LOW)


def prepare(experts, tokens, routes, gain, earlier, *outs):
    far, near, own, normed_ref = outs[:-3], outs[-3], outs[-2], outs[-1]
    me = lax.axis_index("exp")
    tp = lax.axis_index("tp")
    capacity, width = own.shape
    half = width // 2
    wide = tokens[...].astype(WIDE)
    average = jnp.mean(wide, axis=-1, keepdims=True)
    centred = wide - average
    spread = jnp.mean(centred * centred, axis=-1, keepdims=True)
    normed_ref[...] = (centred * lax.rsqrt(spread + EPS) * gain[...]).astype(LOW)
    place, _, _ = places(routes[...], earlier[...], me, max(16, experts))
    normed_half = normed_ref[:, part(tp, half)]
    for k in range(experts - 1, 1, -1):
        far[k - 2][...] = matmul(table(place, k, capacity), normed_half).astype(LOW)
    normed = normed_ref[...]
    near[...] = matmul(table(place, 1, capacity), normed).astype(LOW)
    own[...] = matmul(table(place, 0, capacity), normed).astype(LOW)


def mixing(experts, routes, gates, earlier, upstream, high, low, upstream_here, arrived):
    load = pltpu.make_async_copy(upstream, upstream_here, arrived)
    load.start()
    me = lax.axis_index("exp")
    token_count = routes.shape[1]
    capacity = high.shape[2]
    place, first, second = places(routes[...], earlier[...], me, max(16, experts))
    gate = jnp.where(first, gates[0:1, :], 0.0) + jnp.where(second, gates[1:2, :], 0.0)
    place = place.T
    gate = gate.T
    slots = lax.broadcasted_iota(jnp.int32, (token_count, capacity), 1).astype(WIDE)
    for k in range(experts):
        weight = jnp.where(place[:, k : k + 1] == slots, gate[:, k : k + 1], 0.0)
        upper = weight.astype(LOW)
        high[k] = upper
        low[k] = (weight - upper.astype(WIDE)).astype(LOW)
    load.wait()


def expert(split, *refs):
    rows, refs = refs[: 1 + split], refs[1 + split :]
    first, second, away, kept, inner = refs
    tp = lax.axis_index("tp")
    width, hidden = first.shape
    half = width // 2
    chunk = min(512, hidden)
    for c in range(hidden // chunk):
        columns = slice(c * chunk, (c + 1) * chunk)
        if split:
            value = matmul(rows[0][...], first[part(tp, half), columns])
            value = value + matmul(rows[1][...], first[part(1 - tp, half), columns])
        else:
            value = matmul(rows[0][...], first[:, columns])
        inner[:, columns] = jnp.maximum(value, 0.0).astype(LOW)
    away[...] = matmul(inner[...], second[:, part(1 - tp, half)]).astype(LOW)
    kept[...] = matmul(inner[...], second[:, part(tp, half)])


def expert_first(rows, first, second, away, kept, first_here, second_here, inner, arrived):
    tp = lax.axis_index("tp")
    width, hidden = first.shape
    half = width // 2
    chunk = min(512, hidden)
    columns = [slice(c * chunk, (c + 1) * chunk) for c in range(hidden // chunk)]
    loads = [
        pltpu.make_async_copy(first.at[:, c], first_here.at[:, c], arrived.at[i])
        for i, c in enumerate(columns)
    ]
    loads.append(pltpu.make_async_copy(second, second_here, arrived.at[len(columns)]))
    for load in loads:
        load.start()
    for c, load in zip(columns, loads):
        load.wait()
        inner[:, c] = jnp.maximum(matmul(rows[...], first_here[:, c]), 0.0).astype(LOW)
    loads[-1].wait()
    away[...] = matmul(inner[...], second_here[:, part(1 - tp, half)]).astype(LOW)
    kept[...] = matmul(inner[...], second_here[:, part(tp, half)])


def idle():
    pass


def add(kept, arrived, out):
    out[...] = (kept[...] + arrived[...].astype(WIDE)).astype(LOW)


def combine(order, base, high, low, *refs):
    returned, out = refs[:-1], refs[-1]
    half = out.shape[1]
    if base.shape[1] == half:
        mixed = base[...]
    else:
        mixed = base[:, part(lax.axis_index("tp"), half)].astype(WIDE)
    for k, block in zip(order, returned, strict=True):
        rows = block[...]
        mixed = mixed + (matmul(high[k], rows) + matmul(low[k], rows))
    out[...] = mixed.astype(out.dtype)


def project(mine, other, gain, weight, out):
    tp = lax.axis_index("tp")
    half = mine.shape[1]
    own = mine[...].astype(WIDE)
    rest = other[...].astype(WIDE)
    average = (
        jnp.sum(own, axis=-1, keepdims=True) + jnp.sum(rest, axis=-1, keepdims=True)
    ) / (2 * half)
    own = own - average
    rest = rest - average
    spread = (
        jnp.sum(own * own, axis=-1, keepdims=True) + jnp.sum(rest * rest, axis=-1, keepdims=True)
    ) / (2 * half)
    factor = lax.rsqrt(spread + EPS)
    own = (own * factor * gain[:, part(tp, half)]).astype(LOW)
    rest = (rest * factor * gain[:, part(1 - tp, half)]).astype(LOW)
    value = matmul(own, weight[part(tp, half), :]) + matmul(rest, weight[part(1 - tp, half), :])
    out[...] = value.astype(LOW)


def choose(order, *refs):
    sec = lax.axis_index("sec")
    out = refs[-1]
    for i, source in zip(order, refs[:-1], strict=True):

        @pl.when(sec == i)
        def _():
            out[...] = source[...]


def attend(
    first, second, queries, upstream, key_w, value_w, away, low_ref, values, dkeys, dvalues, keys
):
    tp = lax.axis_index("tp")
    sec = lax.axis_index("sec")
    token_count, half = first.shape
    scale = 1.0 / math.sqrt(HD)

    @pl.when(sec != 0)
    def _():
        crossed = ((sec > 1) & (sec % 2 == 1)).astype(jnp.int32)
        place = tp ^ crossed
        for weight, target in ((key_w, keys), (value_w, values)):
            value = matmul(first[...], weight[part(place, half), :])
            value = value + matmul(second[...], weight[part(1 - place, half), :])
            target[...] = value.astype(LOW)
        heads = [
            (slice(s * SEQ, (s + 1) * SEQ), slice(h * HD, (h + 1) * HD))
            for s in range(token_count // SEQ)
            for h in range(queries.shape[1] // HD)
        ]
        scores = [matmul(keys[at], queries[at], NT) for at in heads]
        dprobs = [matmul(values[at], upstream[at], NT) for at in heads]
        powers = [jnp.exp(x * scale) for x in scores]
        probs = [x * (1.0 / jnp.sum(x, axis=0, keepdims=True)) for x in powers]
        lows = [x.astype(LOW) for x in probs]
        for at, low in zip(heads, lows):
            dvalues[at] = matmul(low, upstream[at]).astype(LOW)
        rowdots = [jnp.sum(x * y, axis=0, keepdims=True) for x, y in zip(dprobs, probs)]
        dscores = [
            (y * (x - z)).astype(LOW) for x, y, z in zip(dprobs, probs, rowdots)
        ]
        for at, dscore in zip(heads, dscores):
            dkeys[at] = (matmul(dscore, queries[at]) * scale).astype(LOW)
        for i, low in enumerate(lows):
            low_ref[i] = low
        terms(dkeys, dvalues, key_w, value_w, 1 - sec % 2, away)

    @pl.when(sec == 0)
    def _():
        away[...] = jnp.zeros_like(away)


def terms(dkeys, dvalues, key_w, value_w, parity, out):
    pairs = lax.axis_size("sec") // 2
    block = out.shape[1] // pairs
    for i in range(pairs):
        rows = part(2 * i + parity, block)
        value = matmul(dkeys[...], key_w[rows, :], NT)
        value = value + matmul(dvalues[...], value_w[rows, :], NT)
        out[:, i * block : (i + 1) * block] = value.astype(out.dtype)


def keep(dkeys, dvalues, key_w, value_w, out):
    sec = lax.axis_index("sec")

    @pl.when(sec != 0)
    def _():
        terms(dkeys, dvalues, key_w, value_w, sec % 2, out)

    @pl.when(sec == 0)
    def _():
        out[...] = jnp.zeros_like(out)


def contexts(low_ref, values, hidden, out):
    sec = lax.axis_index("sec")
    head_count = values.shape[1] // HD

    @pl.when(sec == 0)
    def _():
        out[...] = hidden[...]

    @pl.when(sec != 0)
    def _():
        for i in range(low_ref.shape[0]):
            s, h = i // head_count, i % head_count
            at = slice(s * SEQ, (s + 1) * SEQ), slice(h * HD, (h + 1) * HD)
            out[at] = matmul(low_ref[i], values[at], TN).astype(LOW)


def gather_term(kept, arrived, own, *sent):
    tp = lax.axis_index("tp")
    here = lax.axis_index("sec") // 2 * lax.axis_size("tp") + tp
    width = own.shape[1]
    for k in range(len(sent) + 1):
        columns = part(here ^ k, width)
        value = kept[:, columns] + arrived[:, columns].astype(WIDE)
        if k == 0:
            own[...] = value
        else:
            sent[k - 1][...] = value.astype(LOW)


def swap(block, axis, step):
    size = lax.axis_size(axis)
    return lax.ppermute(block, axis, [(i, i ^ step) for i in range(size)])


def shards(
    tokens,
    routes,
    gate_weights,
    moe_gain,
    attn_gain,
    expert_in,
    expert_out,
    query_weight,
    key_weight,
    value_weight,
    cotangent,
):
    token_rows = tokens[0]
    route_rows = routes[0].T
    gate_rows = gate_weights[0].T
    token_count, model_width = token_rows.shape
    experts = lax.axis_size("exp")
    sections = lax.axis_size("sec")
    tp_size = lax.axis_size("tp")
    sec = lax.axis_index("sec")
    half = model_width // tp_size
    capacity = 3 * token_count // experts
    weight_first = expert_in[0, 0]
    weight_second = expert_out[0, 0]
    units = weight_first.shape[1]

    middle = max(2, experts // 2 + 1)
    groups = [list(range(middle - 1, 1, -1)), list(range(experts - 1, middle - 1, -1))]
    row_half, row_whole = shape_of((capacity, half)), shape_of((capacity, model_width))
    earlier = call(
        triangle,
        [shape_of((token_count, token_count))],
        [],
        flops=20 * token_count * token_count * model_width,
    )[0]
    *far_rows, near_rows, own_rows = call(
        functools.partial(prepare, experts),
        [row_half] * (experts - 2) + [row_whole] * 2,
        [token_rows, route_rows, moe_gain, earlier],
        [pltpu.VMEM((token_count, model_width), LOW)],
        flops=2 * 3 * token_count * token_count * model_width,
    )
    def hold(array, after):
        return call(idle, [], [], after=after, held=[array])[0]

    def joined(group):
        blocks = [swap(far_rows[k - 2], "exp", k) for k in group]
        return blocks[0] if len(blocks) == 1 else jnp.concatenate(blocks, axis=0)

    def total(away, kept, plain=False):
        arrived = swap(away, "tp", 1)
        if plain:
            return (kept + arrived.astype(WIDE)).astype(LOW)
        return call(add, [shape_of(away.shape)], [kept, arrived])[0]

    def through(rows, after):
        count = rows[0].shape[0]
        return call(
            functools.partial(expert, len(rows) - 1),
            [shape_of((count, half)), shape_of((count, half), WIDE)],
            [*rows, weight_first, weight_second],
            [pltpu.VMEM((count, units), LOW)],
            flops=4 * count * model_width * units,
            limit=24,
            after=after,
        )

    arriving = [joined(groups[0])]
    near = swap(near_rows, "exp", 1)
    later = [far_rows[k - 2] for k in groups[1]]
    loads = max(1, units // 512) + 1
    own_away, own_kept, weight_first, weight_second, *later = call(
        expert_first,
        [
            row_half,
            shape_of((capacity, half), WIDE),
            shape_of(weight_first.shape),
            shape_of(weight_second.shape),
        ],
        [own_rows, weight_first, weight_second],
        [pltpu.VMEM((capacity, units), LOW), pltpu.SemaphoreType.DMA((loads,))],
        flops=4 * capacity * model_width * units,
        remote=(1, 2),
        limit=44,
        held=later,
    )
    for k, rows in zip(groups[1], later):
        far_rows[k - 2] = rows
    arriving.append(joined(groups[1]))
    returned = {0: total(own_away, own_kept)}
    arriving[0] = hold(arriving[0], [own_away])
    others = [swap(arriving[0], "tp", 1)]
    high, low, upstream = call(
        functools.partial(mixing, experts),
        [shape_of((experts, token_count, capacity))] * 2 + [shape_of(cotangent.shape[1:])],
        [route_rows, gate_rows, earlier, cotangent[0]],
        [pltpu.SemaphoreType.DMA],
        remote=(3,),
        after=[arriving[0]],
    )
    others.append(swap(arriving[1], "tp", 1))

    def give_back(group, away, kept):
        mixed = total(away, kept)
        for i, k in enumerate(group):
            block = mixed if len(group) == 1 else mixed[i * capacity : (i + 1) * capacity]
            returned[k] = swap(block, "exp", k)
        return mixed

    away, kept = through([arriving[0], others[0]], [returned[0], high])
    near_away, near_kept = through([near], [away])
    mixed = give_back(groups[0], away, kept)
    returned[1] = swap(total(near_away, near_kept, plain=True), "exp", 1)
    away, kept = through([arriving[1], others[1]], [near_away, mixed])
    give_back(groups[1], away, kept)

    there, rest = [0, *groups[0], 1], groups[1]
    so_far = call(
        functools.partial(combine, there),
        [shape_of((token_count, half), WIDE)],
        [token_rows, high, low, *(returned[k] for k in there)],
        flops=4 * len(there) * token_count * capacity * half,
    )[0]
    hidden_half = call(
        functools.partial(combine, rest),
        [shape_of((token_count, half))],
        [so_far, high, low, *(returned[k] for k in rest)],
        flops=4 * len(rest) * token_count * capacity * half,
    )[0]

    hidden_other = swap(hidden_half, "tp", 1)

    def cycle(order, crossed):
        pairs = [(i, i ^ 1) for i in range(sections * tp_size)]
        targets = dict(pairs)
        for a, b in zip(order, order[1:] + order[:1]):
            for t in range(tp_size):
                targets[a * tp_size + t] = b * tp_size + (t ^ crossed if a == 0 else t)
        return lax.ppermute(hidden_half, ("sec", "tp"), list(targets.items()))

    beside = swap(hidden_half, "sec", 1)
    choices = {}
    for i in range(1, sections // 2):
        choices[2 * i] = cycle([0, 2 * i, 2 * i + 1, 1], 0)
        choices.setdefault(0, hidden_other)
        choices[2 * i + 1] = cycle([0, 2 * i + 1, 2 * i, 1], 1)
    choices |= {0: hidden_other, 1: beside}
    first = call(
        functools.partial(choose, list(choices)), [shape_of(hidden_half.shape)], list(choices.values())
    )[0]
    second = swap(first, "sec", 1)

    local_width = query_weight.shape[2]
    queries = call(
        project,
        [shape_of((token_count, local_width))],
        [hidden_half, hidden_other, attn_gain, query_weight[0]],
        flops=2 * token_count * model_width * local_width,
        after=list(choices.values())[:1],
    )[0]
    heads = token_count // SEQ * (local_width // HD)
    away, lows, values, dkeys, dvalues = call(
        attend,
        [
            shape_of((token_count, model_width // 2)),
            shape_of((heads, SEQ, SEQ)),
            *[shape_of((token_count, local_width))] * 3,
        ],
        [first, second, queries, upstream, key_weight[0], value_weight[0]],
        [pltpu.VMEM((token_count, local_width), LOW)],
        flops=8 * token_count * model_width * local_width,
    )
    kept = call(
        keep,
        [shape_of((token_count, model_width // 2), WIDE)],
        [dkeys, dvalues, key_weight[0], value_weight[0]],
        flops=2 * token_count * model_width * local_width,
    )[0]
    context = call(
        contexts,
        [shape_of((token_count, local_width))],
        [lows, values, hidden_half],
        flops=2 * token_count * SEQ * local_width,
    )[0]

    own = model_width // (sections * tp_size)
    count = sections // 2 * tp_size
    both = sections * tp_size
    blocks = call(
        gather_term,
        [shape_of((token_count, own), WIDE)] + [shape_of((token_count, own))] * (count - 1),
        [kept, swap(away, "sec", 1)],
    )
    total = blocks[0]
    for k in range(1, count):
        pairs = []
        for i in range(both):
            section, t = i // tp_size, i % tp_size
            target = (section // 2 * tp_size + t) ^ k
            pairs.append((i, (target // tp_size * 2 + section % 2) * tp_size + target % tp_size))
        total = total + lax.ppermute(blocks[k], ("sec", "tp"), pairs).astype(WIDE)
    return (context[None], total.astype(LOW))


def solution(mesh):
    placed = (
        P("sec", "exp", None),
        P("sec", "exp", None),
        P("sec", "exp", None),
        P("sec", None),
        P("sec", None),
        P("sec", "exp", None, "tp"),
        P("sec", "exp", "tp", None),
        P("sec", None, "tp"),
        P("sec", None, "tp"),
        P("sec", None, "tp"),
        P("sec", "exp", "tp"),
    )
    return jax.shard_map(
        shards,
        mesh=mesh,
        in_specs=placed,
        out_specs=(P("sec", "exp", "tp"), P("exp", ("sec", "tp"))),
        check_vma=False,
    )
```
